32 devices in a mesh: group: 2 (over x), term: 16 (over z, y, core).
Axes of the slice: x: 2, y: 2, z: 4, core: 2. Of those that a mesh axis runs over, the one named last changes fastest.
Arguments:
- wavefn: float32 [64, 128, 128], P(('group', 'term')), parts along dimension 0, may hold values from -6 to 6
- left_ops: float32 [256, 128, 128], P(('group', 'term')), parts along dimension 0, may hold values from -0.5 to 1.1
- right_ops: float32 [256, 128, 128], P(('group', 'term')), parts along dimension 0, may hold values from -0.5 to 1.1
- precond: float32 [64, 128, 128], P(('group', 'term')), parts along dimension 0, may hold values from 0.02 to 0.2
- fetch_map: int32 [16, 16], replicated, may hold values from 0 to 1
- store_map: int32 [16, 16], replicated, may hold values from 0 to 1
- pair_list: int32 [16, 128, 3], P('term'), may hold values from 0 to 15, as said below
- live_count: int32 [16], P('term'), may hold values from 32 to 128, as said below
Outputs:
- next_vector: float32 [64, 128, 128], P(('group', 'term')), parts along dimension 0
- residual: float32 [64, 128, 128], P(('group', 'term')), parts along dimension 0
The draws below stay inside these ranges and needn't reach their ends.
There are 2 independent parts, one for each index of `group`. The reference program is written for one: setup_inputs(seed, part) draws one part's arguments, and reference() takes and returns one part's arrays. A program takes and returns all parts, laid end to end along the dimension named above; an argument that names none is the same for every part. Nothing has to cross between parts.
Inputs may be any that keep to these rules, and one draw needn't show every extreme that they name: `pair_list`: column 0 is a window slot below 16, column 1 a local term below 8, column 2 a result slot below 16. `live_count`: some device has all 128 pairs live, some only 32.
All inputs are finite; a program needn't handle non-finite values.
Results may differ from the reference program's by a relative error of at most 0.0003.
Values sent between devices are 32-bit elements; how exact they have to be, the bound alone decides.
No kernel may reach another device: no remote copies, remote signals or barrier semaphores. Data moves between devices by JAX's collectives and lax.ppermute only.
A program may use at most 128 MiB of HBM per device.

```python
import jax
import jax.numpy as jnp
from jax import lax

BLK = 128
NB_DEV = 2
TERM_DEV = 8
PAIRS = 128
ITERS = 2
NBLOCKS = 32
OPS = 128
N_TERM = 16


def operator_from_noise(noise):
    scaled = jnp.clip(noise * BLK ** (-0.5), -0.5, 0.5)
    return (scaled + 0.6 * jnp.eye(BLK, dtype=jnp.float32)[None, :, :]).astype(jnp.float32)


def draw_left_ops(key, part):
    key = jax.random.fold_in(key, 21)
    noise = jax.random.normal(key, (OPS, BLK, BLK), jnp.float32)
    return operator_from_noise(noise)


def draw_right_ops(key, part):
    key = jax.random.fold_in(key, 22)
    noise = jax.random.normal(key, (OPS, BLK, BLK), jnp.float32)
    return operator_from_noise(noise)


def draw_precond(key, part):
    key = jax.random.fold_in(key, 23)
    first, second, third = jax.random.split(key, 3)
    shape = (NBLOCKS, BLK, BLK)
    upper = jax.random.uniform(first, shape, jnp.float32) < 0.5
    lower_value = jnp.exp(jax.random.uniform(second, shape, jnp.float32, jnp.log(0.02), jnp.log(0.03)))
    upper_value = jnp.exp(jax.random.uniform(third, shape, jnp.float32, jnp.log(0.13), jnp.log(0.2)))
    values = jnp.where(upper, upper_value, lower_value)
    return jnp.clip(values, 0.02, 0.2).astype(jnp.float32)


def draw_pair_list(key, part):
    key = jax.random.fold_in(key, 11)
    first, second, third = jax.random.split(key, 3)
    window = jax.random.randint(first, (N_TERM, PAIRS), 0, N_TERM)
    window = window.at[0, 0].set(N_TERM - 1).at[0, 1].set(0)
    terms = jax.random.randint(second, (N_TERM, PAIRS), 0, TERM_DEV)
    slots = jax.random.randint(third, (N_TERM, PAIRS), 0, N_TERM)
    slots = slots.at[0, 2].set(N_TERM - 1)
    return jnp.stack([window, terms, slots], axis=-1).astype(jnp.int32)


def draw_live_count(key, part):
    key = jax.random.fold_in(key, 12)
    first, second = jax.random.split(key)
    counts = jax.random.randint(first, (N_TERM,), PAIRS // 4, PAIRS + 1)
    order = jax.random.permutation(second, N_TERM)
    counts = counts.at[order[0]].set(PAIRS).at[order[1]].set(PAIRS // 4)
    return counts.astype(jnp.int32)


def with_ends(result, stream_key, low, high):
    longest = result.shape.index(max(result.shape))
    spots = []
    for shift in (0, 1):
        where = [jax.random.randint(jax.random.fold_in(stream_key, axis), (), 0, length) for axis, length in enumerate(result.shape)]
        where[longest] = (where[longest] + shift) % result.shape[longest]
        spots.append(tuple(where))
    return result.at[spots[0]].set(low).at[spots[1]].set(high)


def block_scale(rng, extent, pieces, low, top_value):
    level, own = 1.0, jax.random.fold_in(rng, 6)
    for position, shards_of in pieces:
        steps = jnp.exp(jax.random.uniform(jax.random.fold_in(own, position), (shards_of,), jnp.float32, low / len(pieces), top_value / len(pieces)))
        level = level * jnp.repeat(steps, extent[position] // shards_of).reshape([-1 if axis == position else 1 for axis in range(len(extent))])
    return level


def bell_draw(rng, shape, scale, bound, shards=(), held_as=jnp.bfloat16):
    gain = block_scale(rng, shape, shards, -0.22, 0.18) if shards else 1.0
    array = jax.random.normal(rng, shape, jnp.float32) * scale * gain
    return jnp.minimum(jnp.maximum(array, -bound), bound).astype(held_as)


def setup_inputs(seed: int = 0, part: int = 0) -> dict:
    key_list = jax.random.split(jax.random.key(seed), 9)
    own_keys = jax.random.split(jax.random.fold_in(key_list[8], part), 9)
    return {
        "wavefn": bell_draw(own_keys[0], (NBLOCKS, BLK, BLK), 1.0, 6.0, ((0, 16),), jnp.float32),
        "left_ops": draw_left_ops(jax.random.fold_in(jax.random.fold_in(key_list[8], part), 71), part),
        "right_ops": draw_right_ops(jax.random.fold_in(jax.random.fold_in(key_list[8], part), 71), part),
        "precond": draw_precond(jax.random.fold_in(jax.random.fold_in(key_list[8], part), 71), part),
        "fetch_map": with_ends(jax.random.randint(key_list[4], (N_TERM, N_TERM), 0, NB_DEV), jax.random.fold_in(key_list[4], 1), 0, NB_DEV - 1).astype(jnp.int32),
        "store_map": with_ends(jax.random.randint(key_list[5], (N_TERM, N_TERM), 0, NB_DEV), jax.random.fold_in(key_list[5], 1), 0, NB_DEV - 1).astype(jnp.int32),
        "pair_list": draw_pair_list(jax.random.fold_in(key_list[8], 71), part),
        "live_count": draw_live_count(jax.random.fold_in(key_list[8], 71), part),
    }


def matvec(vector, left_ops, right_ops, fetch_map, store_map, pair_list, live_count):
    devices = fetch_map.shape[0]
    owners = jnp.arange(devices, dtype=jnp.int32)
    highest = lax.Precision.HIGHEST

    def device_term(carry, index):
        window = vector[owners * NB_DEV + fetch_map[:, index]]
        pairs_here = pair_list[index]
        picked = window[pairs_here[:, 0]]
        lefts = left_ops[index * TERM_DEV + pairs_here[:, 1]]
        rights = right_ops[index * TERM_DEV + pairs_here[:, 1]]
        inner = jnp.einsum('pik,pkl->pil', lefts, picked, precision=highest)
        terms = jnp.einsum('pil,plm->pim', inner, rights, precision=highest)
        active = (jnp.arange(PAIRS, dtype=jnp.int32) < live_count[index]).astype(jnp.float32)
        select = (pairs_here[:, 2][:, None] == owners[None, :]).astype(jnp.float32) * active[:, None]
        slots = jnp.einsum('ps,pij->sij', select, terms, precision=highest)
        targets = owners * NB_DEV + store_map[index]
        return (carry.at[targets].add(slots), None)
    start = jnp.zeros(vector.shape, jnp.float32)
    total, _ = lax.scan(device_term, start, jnp.arange(devices, dtype=jnp.int32))
    return total

def reference(wavefn, left_ops, right_ops, precond, fetch_map, store_map, pair_list, live_count):
    vector = wavefn
    residual = wavefn
    for iteration in range(ITERS):
        sigma = matvec(vector, left_ops, right_ops, fetch_map, store_map, pair_list, live_count)
        theta = jnp.sum(vector * sigma) / jnp.sum(vector * vector)
        residual = sigma - theta * vector
        corrected = vector - precond * residual
        mean_square = jnp.sum(corrected * corrected) / corrected.size
        vector = corrected / jnp.sqrt(mean_square + 1e-06)
    return (vector, residual)
```

```python
import functools

import jax
import jax.numpy as jnp
from jax import lax
from jax.experimental import pallas as pl
from jax.experimental.pallas import tpu as pltpu
from jax.sharding import PartitionSpec as P

ITERS = 2
CORE, ROW = 1, 2
SMEM = pl.BlockSpec(memory_space=pltpu.SMEM)
VMEM = pl.BlockSpec(memory_space=pltpu.VMEM)
PARAMS = pltpu.CompilerParams(vmem_limit_bytes=56 * 2**20)


def halves(x):
    high = x.astype(jnp.bfloat16)
    return high, (x - high.astype(jnp.float32)).astype(jnp.bfloat16)


def tile_sum(x):
    return jnp.sum(x.reshape(-1, 8, x.shape[-1]), axis=0)


def prep_kernel(n, spare, me_ref, pairs_ref, live_ref, left_ref, right_ref,
                l4_ref, rr_ref, first_ref, second_ref, dst_ref, one_ref, two_ref, count_ref, seen_ref):
    me = me_ref[0]
    terms = left_ref.shape[0]
    width = left_ref.shape[1]
    zero = terms * n

    def clear(cell, carry):
        first_ref[cell] = zero
        second_ref[cell] = zero
        seen_ref[cell] = 0
        return carry

    lax.fori_loop(0, terms * n, clear, 0, unroll=8)

    def pair(p, carry):
        extra, ops = carry
        a = lax.bitwise_xor(pairs_ref[3 * p], me)
        j = pairs_ref[3 * p + 1]
        o = lax.bitwise_xor(pairs_ref[3 * p + 2], me)
        cell = j * n + o
        source = a * terms + j
        seen = seen_ref[cell]
        seen_ref[cell] = seen + 1
        before = second_ref[cell]
        place = jnp.where(seen == 2, spare + extra, before)
        first_ref[cell] = jnp.where(seen == 0, source, first_ref[cell])
        second_ref[cell] = jnp.where(seen == 0, before, jnp.where(seen == 1, source, place))
        dst_ref[ops] = place
        one_ref[ops] = before
        two_ref[ops] = source
        return extra + (seen == 2).astype(jnp.int32), ops + (seen >= 2).astype(jnp.int32)

    _, ops = lax.fori_loop(0, live_ref[0], pair, (jnp.int32(0), jnp.int32(0)))
    count_ref[0] = ops

    for j in range(terms):
        high, low = halves(left_ref[j])
        for k, part in enumerate((high, low, high, low)):
            l4_ref[j, :, k * width:(k + 1) * width] = part
        high, low = halves(right_ref[j])
        for k in range(2):
            row = (k * terms + j) * width
            rr_ref[row:row + width, :width] = high
            rr_ref[row:row + width, width:] = low


def prep(n, me, pairs, live, left_ops, right_ops):
    terms, width = left_ops.shape[:2]
    npairs = pairs.shape[0] // 3
    table = jax.ShapeDtypeStruct((terms * n,), jnp.int32)
    listed = jax.ShapeDtypeStruct((npairs,), jnp.int32)
    return pl.pallas_call(
        functools.partial(prep_kernel, n, terms * n + 1),
        out_shape=(
            jax.ShapeDtypeStruct((terms, width, 4 * width), jnp.bfloat16),
            jax.ShapeDtypeStruct((2 * terms * width, 2 * width), jnp.bfloat16),
            table, table, listed, listed, listed,
            jax.ShapeDtypeStruct((1,), jnp.int32),
        ),
        in_specs=[SMEM] * 3 + [VMEM] * 2,
        out_specs=[VMEM] * 2 + [SMEM] * 6,
        scratch_shapes=[pltpu.SMEM((terms * n,), jnp.int32)],
        compiler_params=PARAMS,
        name="prep",
    )(me, pairs, live, left_ops, right_ops)


def apply_kernel(n, rows, me_ref, fetch_ref, store_ref, first_ref, second_ref, dst_ref, one_ref, two_ref,
                 count_ref, l4_ref, rr_ref, *refs):
    pieces, (out_ref, square_ref, field, block, total) = refs[:n], refs[n:]
    me = me_ref[0]
    terms, width = l4_ref.shape[:2]
    for r in range(n):
        high, low = halves(pieces[r][fetch_ref[lax.bitwise_xor(me, r) * n + me]])
        at = (r % 2) * width
        for k, part in enumerate((high, high, low, low)):
            field[r // 2, k * width:(k + 1) * width, at:at + width] = part
    square = jnp.zeros((8, width), jnp.float32)
    for r in range(n):
        square = square + tile_sum(pieces[r][...] * pieces[r][...])
    square_ref[...] = square
    product = jnp.zeros((8, width), jnp.float32)
    block[terms * n] = jnp.zeros((rows, width), jnp.float32)
    for start in range(0, width, rows):
        left = l4_ref[:, start:start + rows, :].reshape(terms * rows, 4 * width)

        def products(c, carry):
            both = jnp.dot(left, field[c], preferred_element_type=jnp.float32)
            for k in range(2):
                at = pl.multiple_of((2 * c + k) * terms, terms)
                block[pl.ds(at, terms)] = both[:, k * width:(k + 1) * width].reshape(terms, rows, width)
            return carry

        lax.fori_loop(0, n // 2, products, 0)

        def add(i, carry):
            block[dst_ref[i]] = block[one_ref[i]] + block[two_ref[i]]
            return carry

        lax.fori_loop(0, count_ref[0], add, 0)
        for j in range(terms):

            def cell(o, carry):
                at = j * n + o
                high, low = halves(block[first_ref[at]] + block[second_ref[at]])
                total[o, :, j * width:(j + 1) * width] = high
                total[o, :, (terms + j) * width:(terms + j + 1) * width] = low
                return carry

            lax.fori_loop(0, n, cell, 0, unroll=4)
        group = 8
        for o in range(0, n, group):
            both = jnp.dot(total[o:o + group].reshape(group * rows, 2 * terms * width), rr_ref[...],
                           preferred_element_type=jnp.float32)
            slots = both[:, :width] + both[:, width:]
            for k in range(group):
                slot = slots[k * rows:(k + 1) * rows]
                owner = lax.bitwise_xor(me, o + k)
                out_ref[owner, start:start + rows, :] = slot
                held = pieces[o + k][store_ref[me * n + owner], start:start + rows, :]
                product = product + tile_sum(held * slot)
    for r in range(n):
        out_ref[r, width:, :] = product


def apply(n, me, fetch, store, tables, pieces):
    l4 = tables[0]
    terms, width = l4.shape[:2]
    npairs = tables[4].shape[0]
    rows = width if n <= 16 else width // 4
    return pl.pallas_call(
        functools.partial(apply_kernel, n, rows),
        out_shape=(
            jax.ShapeDtypeStruct((n, width + 8, width), jnp.float32),
            jax.ShapeDtypeStruct((8, width), jnp.float32),
        ),
        in_specs=[SMEM] * 9 + [VMEM] * (2 + n),
        out_specs=[VMEM] * 2,
        scratch_shapes=[
            pltpu.VMEM((n // 2, 4 * width, 2 * width), jnp.bfloat16),
            pltpu.VMEM((terms * n + 1 + npairs // 3, rows, width), jnp.float32),
            pltpu.VMEM((n, rows, 2 * terms * width), jnp.bfloat16),
        ],
        compiler_params=PARAMS,
        name="apply",
    )(me, fetch, store, *tables[2:], *tables[:2], *pieces)


def landed(n, me_ref, store_ref, arrived_ref):
    me = me_ref[0]
    width = arrived_ref.shape[2]
    sums = [jnp.zeros((width, width), jnp.float32) for _ in range(2)]
    tile = jnp.zeros((8, width), jnp.float32)
    for r in range(n):
        mine = store_ref[r * n + me]
        for b in range(2):
            sums[b] = sums[b] + (mine == b).astype(jnp.float32) * arrived_ref[r, :width, :]
        tile = tile + arrived_ref[r, width:, :]
    return sums, jnp.sum(tile)


def step_kernel(n, me_ref, store_ref, arrived_ref, square_ref, vector_ref, precond_ref, out_ref):
    sigma, product = landed(n, me_ref, store_ref, arrived_ref)
    theta = product / jnp.sum(square_ref[...])
    for b in range(2):
        v = vector_ref[b]
        out_ref[b] = v - precond_ref[b] * (sigma[b] - theta * v)


def last_kernel(n, cells, me_ref, store_ref, arrived_ref, square_ref, vector_ref, precond_ref,
                residual_ref, out_ref, tile_ref):
    sigma, product = landed(n, me_ref, store_ref, arrived_ref)
    square = jnp.sum(square_ref[...])
    theta = product / square
    scale = 1.0 / jnp.sqrt(square / cells + 1e-06)
    tile = jnp.zeros(tile_ref.shape, jnp.float32)
    for b in range(2):
        v = vector_ref[b]
        residual = (sigma[b] - theta * v) * scale
        residual_ref[b] = residual
        corrected = v * scale - precond_ref[b] * residual
        out_ref[b] = corrected
        tile = tile + tile_sum(corrected * corrected)
    tile_ref[...] = tile


def gathered(n, x):
    def send(y, k):
        return lax.ppermute(y, "term", [(i, i ^ k) for i in range(n)])

    pieces = {0: x, ROW: send(x, ROW)}
    for k in range(4, n, 4):
        pieces[k] = send(x, k)
    for k in range(4, n, 4):
        pieces[k + ROW] = send(pieces[ROW], k) if k == 4 else send(pieces[k], ROW)
    for k in range(0, n, 2):
        pieces[k + CORE] = send(pieces[k], CORE)
    return [pieces[k] for k in range(n)]


def shards(wavefn, left_ops, right_ops, precond, fetch_map, store_map, pair_list, live_count):
    n = lax.axis_size("term")
    me = lax.axis_index("term").astype(jnp.int32).reshape(1)
    width = wavefn.shape[1]
    cells = wavefn.size * n
    fetch, store = fetch_map.reshape(-1), store_map.reshape(-1)
    tables = prep(n, me, pair_list.reshape(-1), live_count, left_ops, right_ops)
    block = jax.ShapeDtypeStruct(wavefn.shape, jnp.float32)
    tile = jax.ShapeDtypeStruct((8, width), jnp.float32)
    vector = wavefn
    for iteration in range(ITERS):
        slots, square = apply(n, me, fetch, store, tables, gathered(n, vector))
        arrived = lax.all_to_all(slots, "term", split_axis=0, concat_axis=0, tiled=True)
        last = iteration == ITERS - 1
        result = pl.pallas_call(
            functools.partial(last_kernel, n, cells) if last else functools.partial(step_kernel, n),
            out_shape=(block, block, tile) if last else block,
            in_specs=[SMEM] * 2 + [VMEM] * 4,
            out_specs=[VMEM] * 3 if last else VMEM,
            compiler_params=PARAMS,
            name="last" if last else "step",
        )(me, store, arrived, square, vector, precond)
        if not last:
            vector = result
    residual, corrected, partial = result
    tiles = lax.all_to_all(jnp.broadcast_to(partial[None], (n, 8, width)), "term",
                           split_axis=0, concat_axis=0, tiled=True)
    return corrected / jnp.sqrt(jnp.sum(tiles) / cells + 1e-06), residual


def solution(mesh):
    field = P(("group", "term"), None, None)
    return jax.shard_map(
        shards,
        mesh=mesh,
        in_specs=(field, field, field, field, P(), P(), P("term", None, None), P("term")),
        out_specs=(field, field),
        check_vma=False,
    )
```

```python
import functools

import jax
import jax.numpy as jnp
from jax import lax
from jax.experimental import pallas as pl
from jax.experimental.pallas import tpu as pltpu
from jax.sharding import PartitionSpec as P

ITERS = 2
CORE, ROW = 1, 2
SMEM = pl.BlockSpec(memory_space=pltpu.SMEM)
VMEM = pl.BlockSpec(memory_space=pltpu.VMEM)


def params(mebibytes):
    return pltpu.CompilerParams(vmem_limit_bytes=mebibytes * 2**20)


def halves(x):
    high = x.astype(jnp.bfloat16)
    return high, (x - high.astype(jnp.float32)).astype(jnp.bfloat16)


def tile_sum(x):
    return jnp.sum(x.reshape(-1, 8, x.shape[-1]), axis=0)


def prep_kernel(n, spare, me_ref, pairs_ref, live_ref, left_ref, right_ref,
                l4_ref, rr_ref, first_ref, second_ref, dst_ref, one_ref, two_ref, count_ref, seen_ref):
    me = me_ref[0]
    terms = left_ref.shape[0]
    width = left_ref.shape[1]
    zero = terms * n

    def clear(cell, carry):
        first_ref[cell] = zero
        second_ref[cell] = zero
        seen_ref[cell] = 0
        return carry

    lax.fori_loop(0, terms * n, clear, 0, unroll=8)

    def pair(p, carry):
        extra, ops = carry
        a = lax.bitwise_xor(pairs_ref[p, 0], me)
        j = pairs_ref[p, 1]
        o = lax.bitwise_xor(pairs_ref[p, 2], me)
        cell = j * n + o
        source = a * terms + j
        seen = seen_ref[cell]
        seen_ref[cell] = seen + 1
        before = second_ref[cell]
        place = jnp.where(seen == 2, spare + extra, before)
        first_ref[cell] = jnp.where(seen == 0, source, first_ref[cell])
        second_ref[cell] = jnp.where(seen == 0, before, jnp.where(seen == 1, source, place))
        dst_ref[ops] = place
        one_ref[ops] = before
        two_ref[ops] = source
        return extra + (seen == 2).astype(jnp.int32), ops + (seen >= 2).astype(jnp.int32)

    _, ops = lax.fori_loop(0, live_ref[0], pair, (jnp.int32(0), jnp.int32(0)))
    count_ref[0] = ops

    for j in range(terms):
        high, low = halves(left_ref[j])
        for k, part in enumerate((high, low, high, low)):
            l4_ref[j, :, k * width:(k + 1) * width] = part
        high, low = halves(right_ref[j])
        for k in range(2):
            row = (k * terms + j) * width
            rr_ref[row:row + width, :width] = high
            rr_ref[row:row + width, width:] = low


def prep(n, me, pairs, live, left_ops, right_ops):
    terms, width = left_ops.shape[:2]
    npairs = pairs.shape[0]
    table = jax.ShapeDtypeStruct((terms * n,), jnp.int32)
    listed = jax.ShapeDtypeStruct((npairs,), jnp.int32)
    return pl.pallas_call(
        functools.partial(prep_kernel, n, terms * n + 1),
        out_shape=(
            jax.ShapeDtypeStruct((terms, width, 4 * width), jnp.bfloat16),
            jax.ShapeDtypeStruct((2 * terms * width, 2 * width), jnp.bfloat16),
            table, table, listed, listed, listed,
            jax.ShapeDtypeStruct((1,), jnp.int32),
        ),
        in_specs=[SMEM] * 3 + [VMEM] * 2,
        out_specs=[VMEM] * 2 + [SMEM] * 6,
        scratch_shapes=[pltpu.SMEM((terms * n,), jnp.int32)],
        compiler_params=params(16),
        name="prep",
    )(me, pairs, live, left_ops, right_ops)


def apply_kernel(n, rows, me_ref, fetch_ref, store_ref, first_ref, second_ref, dst_ref, one_ref, two_ref,
                 count_ref, l4_ref, rr_ref, *refs):
    pieces, (out_ref, square_ref, block, total) = refs[:n], refs[n:]
    me = me_ref[0]
    terms, width = l4_ref.shape[:2]
    square = jnp.zeros((8, width), jnp.float32)
    product = jnp.zeros((8, width), jnp.float32)
    block[terms * n] = jnp.zeros((rows, width), jnp.float32)
    for start in range(0, width, rows):
        left = l4_ref[:, start:start + rows, :].reshape(terms * rows, 4 * width)

        for c in range(n // 2):
            columns = []
            for r in (2 * c, 2 * c + 1):
                high, low = halves(pieces[r][fetch_ref[lax.bitwise_xor(me, r), me]])
                columns.append(jnp.concatenate([high, high, low, low], axis=0))
                if start == 0:
                    square = square + tile_sum(pieces[r][...] * pieces[r][...])
            both = jnp.dot(left, jnp.concatenate(columns, axis=1), preferred_element_type=jnp.float32)
            for k in range(2):
                at = (2 * c + k) * terms
                block[at:at + terms] = both[:, k * width:(k + 1) * width].reshape(terms, rows, width)

        def add(i, carry):
            block[dst_ref[i]] = block[one_ref[i]] + block[two_ref[i]]
            return carry

        lax.fori_loop(0, count_ref[0], add, 0)
        group = 4
        for o in range(0, n, group):
            for k in range(group):
                for j in range(terms):
                    at = j * n + o + k
                    high, low = halves(block[first_ref[at]] + block[second_ref[at]])
                    total[o + k, :, j * width:(j + 1) * width] = high
                    total[o + k, :, (terms + j) * width:(terms + j + 1) * width] = low
            both = jnp.dot(total[o:o + group].reshape(group * rows, 2 * terms * width), rr_ref[...],
                           preferred_element_type=jnp.float32)
            slots = both[:, :width] + both[:, width:]
            for k in range(group):
                slot = slots[k * rows:(k + 1) * rows]
                owner = lax.bitwise_xor(me, o + k)
                out_ref[owner, start:start + rows, :] = slot
                held = pieces[o + k][store_ref[me, owner], start:start + rows, :]
                product = product + tile_sum(held * slot)
    square_ref[...] = square
    for r in range(n):
        out_ref[r, width:, :] = product


def apply(n, me, fetch, store, tables, pieces):
    l4 = tables[0]
    terms, width = l4.shape[:2]
    npairs = tables[4].shape[0]
    rows = width if n <= 16 else width // 4
    return pl.pallas_call(
        functools.partial(apply_kernel, n, rows),
        out_shape=(
            jax.ShapeDtypeStruct((n, width + 8, width), jnp.float32),
            jax.ShapeDtypeStruct((8, width), jnp.float32),
        ),
        in_specs=[SMEM] * 9 + [VMEM] * (2 + n),
        out_specs=[VMEM] * 2,
        scratch_shapes=[
            pltpu.VMEM((terms * n + 1 + npairs // 3, rows, width), jnp.float32),
            pltpu.VMEM((n, rows, 2 * terms * width), jnp.bfloat16),
        ],
        compiler_params=params(32 if n <= 16 else 56),
        name="apply",
    )(me, fetch, store, *tables[2:], *tables[:2], *pieces)


def landed(n, me_ref, store_ref, arrived_ref):
    me = me_ref[0]
    width = arrived_ref.shape[2]
    sums = [jnp.zeros((width, width), jnp.float32) for _ in range(2)]
    tile = jnp.zeros((8, width), jnp.float32)
    for r in range(n):
        mine = store_ref[r, me]
        for b in range(2):
            sums[b] = sums[b] + (mine == b).astype(jnp.float32) * arrived_ref[r, :width, :]
        tile = tile + arrived_ref[r, width:, :]
    return sums, jnp.sum(tile)


def step_kernel(n, me_ref, store_ref, arrived_ref, square_ref, vector_ref, precond_ref, out_ref):
    sigma, product = landed(n, me_ref, store_ref, arrived_ref)
    theta = product / jnp.sum(square_ref[...])
    for b in range(2):
        v = vector_ref[b]
        out_ref[b] = v - precond_ref[b] * (sigma[b] - theta * v)


def last_kernel(n, cells, me_ref, store_ref, arrived_ref, square_ref, vector_ref, precond_ref,
                residual_ref, out_ref, tile_ref):
    sigma, product = landed(n, me_ref, store_ref, arrived_ref)
    square = jnp.sum(square_ref[...])
    theta = product / square
    scale = 1.0 / jnp.sqrt(square / cells + 1e-06)
    tile = jnp.zeros(tile_ref.shape, jnp.float32)
    for b in range(2):
        v = vector_ref[b]
        residual = (sigma[b] - theta * v) * scale
        residual_ref[b] = residual
        corrected = v * scale - precond_ref[b] * residual
        out_ref[b] = corrected
        tile = tile + tile_sum(corrected * corrected)
    tile_ref[...] = tile


def gathered(n, x, beside=None):
    def send(y, k):
        return lax.ppermute(y, "term", [(i, i ^ k) for i in range(n)])

    pieces = {0: x, ROW: send(x, ROW)}
    for k in range(4, n, 4):
        pieces[k] = send(x, k)
    if beside is not None:
        pieces[4], _ = lax.optimization_barrier((pieces[4], beside))
    for k in range(4, n, 4):
        pieces[k + ROW] = send(pieces[ROW], k) if k == 4 else send(pieces[k], ROW)
    for k in range(0, n, 2):
        pieces[k + CORE] = send(pieces[k], CORE)
    return [pieces[k] for k in range(n)]


def shards(wavefn, left_ops, right_ops, precond, fetch_map, store_map, pair_list, live_count):
    n = lax.axis_size("term")
    me = lax.axis_index("term").astype(jnp.int32).reshape(1)
    width = wavefn.shape[1]
    cells = wavefn.size * n
    tables = prep(n, me, pair_list[0], live_count, left_ops, right_ops)
    block = jax.ShapeDtypeStruct(wavefn.shape, jnp.float32)
    tile = jax.ShapeDtypeStruct((8, width), jnp.float32)
    vector = wavefn
    for iteration in range(ITERS):
        slots, square = apply(n, me, fetch_map, store_map, tables, gathered(n, vector, tables if iteration == 0 else None))
        arrived = lax.all_to_all(slots, "term", split_axis=0, concat_axis=0, tiled=True)
        last = iteration == ITERS - 1
        result = pl.pallas_call(
            functools.partial(last_kernel, n, cells) if last else functools.partial(step_kernel, n),
            out_shape=(block, block, tile) if last else block,
            in_specs=[SMEM] * 2 + [VMEM] * 4,
            out_specs=[VMEM] * 3 if last else VMEM,
            compiler_params=params(16),
            name="last" if last else "step",
        )(me, store_map, arrived, square, vector, precond)
        if not last:
            vector = result
    residual, corrected, partial = result
    tiles = lax.all_to_all(jnp.broadcast_to(partial[None], (n, 8, width)), "term",
                           split_axis=0, concat_axis=0, tiled=True)
    return corrected / jnp.sqrt(jnp.sum(tiles) / cells + 1e-06), residual


def solution(mesh):
    field = P(("group", "term"), None, None)
    return jax.shard_map(
        shards,
        mesh=mesh,
        in_specs=(field, field, field, field, P(), P(), P("term", None, None), P("term")),
        out_specs=(field, field),
        check_vma=False,
    )
```

```python
import functools

import jax
import jax.numpy as jnp
from jax import lax
from jax.experimental import pallas as pl
from jax.experimental.pallas import tpu as pltpu
from jax.sharding import PartitionSpec as P

ITERS = 2
CORE, ROW, COLUMN = 1, 2, 4
SMEM = pl.BlockSpec(memory_space=pltpu.SMEM)
VMEM = pl.BlockSpec(memory_space=pltpu.VMEM)


def params(mebibytes):
    return pltpu.CompilerParams(vmem_limit_bytes=mebibytes * 2**20)


def halves(x):
    high = x.astype(jnp.bfloat16)
    return high, (x - high.astype(jnp.float32)).astype(jnp.bfloat16)


def tile_sum(x):
    return jnp.sum(x.reshape(-1, 8, x.shape[-1]), axis=0)


def prep_kernel(n, spare, me_ref, pairs_ref, live_ref, left_ref, right_ref,
                l4_ref, rr_ref, first_ref, second_ref, dst_ref, one_ref, two_ref, count_ref, seen_ref):
    me = me_ref[0]
    terms = left_ref.shape[0]
    width = left_ref.shape[1]
    zero = terms * n

    def clear(cell, carry):
        first_ref[cell] = zero
        second_ref[cell] = zero
        seen_ref[cell] = 0
        return carry

    lax.fori_loop(0, terms * n, clear, 0, unroll=8)

    def pair(p, carry):
        extra, ops = carry
        a = lax.bitwise_xor(pairs_ref[p, 0], me)
        j = pairs_ref[p, 1]
        o = lax.bitwise_xor(pairs_ref[p, 2], me)
        cell = j * n + o
        source = a * terms + j
        seen = seen_ref[cell]
        seen_ref[cell] = seen + 1
        before = second_ref[cell]
        place = jnp.where(seen == 2, spare + extra, before)
        first_ref[cell] = jnp.where(seen == 0, source, first_ref[cell])
        second_ref[cell] = jnp.where(seen == 0, before, jnp.where(seen == 1, source, place))
        dst_ref[ops] = place
        one_ref[ops] = before
        two_ref[ops] = source
        return extra + (seen == 2).astype(jnp.int32), ops + (seen >= 2).astype(jnp.int32)

    _, ops = lax.fori_loop(0, live_ref[0], pair, (jnp.int32(0), jnp.int32(0)))
    count_ref[0] = ops

    for j in range(terms):
        high, low = halves(left_ref[j])
        for k, part in enumerate((high, low, high, low)):
            l4_ref[j, :, k * width:(k + 1) * width] = part
        high, low = halves(right_ref[j])
        for k in range(2):
            row = (k * terms + j) * width
            rr_ref[row:row + width, :width] = high
            rr_ref[row:row + width, width:] = low


def prep(n, me, pairs, live, left_ops, right_ops):
    terms, width = left_ops.shape[:2]
    npairs = pairs.shape[0]
    table = jax.ShapeDtypeStruct((terms * n,), jnp.int32)
    listed = jax.ShapeDtypeStruct((npairs,), jnp.int32)
    return pl.pallas_call(
        functools.partial(prep_kernel, n, terms * n + 1),
        out_shape=(
            jax.ShapeDtypeStruct((terms, width, 4 * width), jnp.bfloat16),
            jax.ShapeDtypeStruct((2 * terms * width, 2 * width), jnp.bfloat16),
            table, table, listed, listed, listed,
            jax.ShapeDtypeStruct((1,), jnp.int32),
        ),
        in_specs=[SMEM] * 3 + [VMEM] * 2,
        out_specs=[VMEM] * 2 + [SMEM] * 6,
        scratch_shapes=[pltpu.SMEM((terms * n,), jnp.int32)],
        compiler_params=params(16),
        name="prep",
    )(me, pairs, live, left_ops, right_ops)


def apply_kernel(n, rows, me_ref, fetch_ref, store_ref, first_ref, second_ref, dst_ref, one_ref, two_ref,
                 count_ref, l4_ref, rr_ref, *refs):
    pieces, (near_ref, far_ref, square_ref, block, total) = refs[:n], refs[n:]
    me = me_ref[0]
    terms, width = l4_ref.shape[:2]
    square = jnp.zeros((8, width), jnp.float32)
    product = jnp.zeros((8, width), jnp.float32)
    block[terms * n] = jnp.zeros((rows, width), jnp.float32)
    for start in range(0, width, rows):
        left = l4_ref[:, start:start + rows, :].reshape(terms * rows, 4 * width)

        for c in range(n // 2):
            columns = []
            for r in (2 * c, 2 * c + 1):
                high, low = halves(pieces[r][fetch_ref[lax.bitwise_xor(me, r), me]])
                columns.append(jnp.concatenate([high, high, low, low], axis=0))
                if start == 0:
                    square = square + tile_sum(pieces[r][...] * pieces[r][...])
            both = jnp.dot(left, jnp.concatenate(columns, axis=1), preferred_element_type=jnp.float32)
            for k in range(2):
                at = (2 * c + k) * terms
                block[at:at + terms] = both[:, k * width:(k + 1) * width].reshape(terms, rows, width)

        def add(i, carry):
            block[dst_ref[i]] = block[one_ref[i]] + block[two_ref[i]]
            return carry

        lax.fori_loop(0, count_ref[0], add, 0)
        group = 4
        for o in range(0, n, group):
            for k in range(group):
                for j in range(terms):
                    at = j * n + o + k
                    high, low = halves(block[first_ref[at]] + block[second_ref[at]])
                    total[o + k, :, j * width:(j + 1) * width] = high
                    total[o + k, :, (terms + j) * width:(terms + j + 1) * width] = low
            both = jnp.dot(total[o:o + group].reshape(group * rows, 2 * terms * width), rr_ref[...],
                           preferred_element_type=jnp.float32)
            slots = both[:, :width] + both[:, width:]
            for k in range(group):
                slot = slots[k * rows:(k + 1) * rows]
                owner = lax.bitwise_xor(me, o + k)
                chip = (o + k) // 2
                if (o + k) % 2:
                    far_ref[chip * width + start:chip * width + start + rows, :] = slot
                else:
                    near_ref[chip, start:start + rows, :] = slot
                held = pieces[o + k][store_ref[me, owner], start:start + rows, :]
                product = product + tile_sum(held * slot)
    square_ref[...] = square
    far_ref[n // 2 * width:, :] = product


def apply(n, me, fetch, store, tables, pieces):
    l4 = tables[0]
    terms, width = l4.shape[:2]
    npairs = tables[4].shape[0]
    rows = width if n <= 16 else width // 4
    return pl.pallas_call(
        functools.partial(apply_kernel, n, rows),
        out_shape=(
            jax.ShapeDtypeStruct((n // 2, width, width), jnp.float32),
            jax.ShapeDtypeStruct((n // 2 * width + 8, width), jnp.float32),
            jax.ShapeDtypeStruct((8, width), jnp.float32),
        ),
        in_specs=[SMEM] * 9 + [VMEM] * (2 + n),
        out_specs=[VMEM] * 3,
        scratch_shapes=[
            pltpu.VMEM((terms * n + 1 + npairs // 3, rows, width), jnp.float32),
            pltpu.VMEM((n, rows, 2 * terms * width), jnp.bfloat16),
        ],
        compiler_params=params(32 if n <= 16 else 56),
        name="apply",
    )(me, fetch, store, *tables[2:], *tables[:2], *pieces)


def swapped(x, k):
    n = lax.axis_size("term")
    return lax.ppermute(x, "term", [(i, i ^ k) for i in range(n)])


def local(kernel, name, out_shape, scalars, arrays):
    many = isinstance(out_shape, tuple)
    return pl.pallas_call(
        kernel,
        out_shape=out_shape,
        in_specs=[SMEM] * len(scalars) + [VMEM] * len(arrays),
        out_specs=[VMEM] * len(out_shape) if many else VMEM,
        compiler_params=params(16),
        name=name,
    )(*scalars, *arrays)


def merge_kernel(over_rows, me_ref, store_ref, near_ref, far_ref, other_ref, keep_ref, column_ref, rows_ref, tile_ref):
    me = me_ref[0]
    chips, width = near_ref.shape[:2]
    kept = 0
    for g in range(chips):
        owner = lax.bitwise_xor(me, 2 * g)
        mine = store_ref[me, owner]
        others = store_ref[lax.bitwise_xor(me, CORE), owner]
        for b in range(2):
            block = (near_ref[g] * (mine == b).astype(jnp.float32)
                     + other_ref[g * width:(g + 1) * width] * (others == b).astype(jnp.float32))
            if g == 3:
                column_ref[b] = block
            elif g in over_rows:
                at = (2 * over_rows.index(g) + b) * width
                rows_ref[at:at + width] = block
            else:
                keep_ref[kept, b] = block
        kept += g != 3 and g not in over_rows
    tile = far_ref[chips * width:] + other_ref[chips * width:]
    rows_ref[2 * len(over_rows) * width:] = tile
    tile_ref[...] = tile


def fold_kernel(over_rows, keep_ref, column_ref, rows_ref, tile_ref, step_ref, *send_refs):
    width = keep_ref.shape[2]
    tile = tile_ref[...] + rows_ref[2 * len(over_rows) * width:]
    step_ref[...] = keep_ref[1] + column_ref[...]
    for i, send_ref in enumerate(send_refs):
        for b in range(2):
            block = keep_ref[2 + i, b]
            if 2 * i + 3 in over_rows:
                at = (2 * over_rows.index(2 * i + 3) + b) * width
                block = block + rows_ref[at:at + width]
            send_ref[b * width:(b + 1) * width] = block
        send_ref[2 * width:] = tile


def landed(keep_ref, step_ref, refs):
    width = keep_ref.shape[2]
    sent, came = refs[0], refs[1:]
    tile = sent[2 * width:]
    for ref in came:
        tile = tile + ref[2 * width:]
    sums = []
    for b in range(2):
        total = keep_ref[0, b] + step_ref[b]
        for ref in came:
            total = total + ref[b * width:(b + 1) * width]
        sums.append(total)
    return sums, jnp.sum(tile)


def step_kernel(keep_ref, step_ref, square_ref, vector_ref, precond_ref, *refs):
    out_ref = refs[-1]
    sigma, product = landed(keep_ref, step_ref, refs[:-1])
    theta = product / jnp.sum(square_ref[...])
    for b in range(2):
        v = vector_ref[b]
        out_ref[b] = v - precond_ref[b] * (sigma[b] - theta * v)


def last_kernel(cells, keep_ref, step_ref, square_ref, vector_ref, precond_ref, *refs):
    residual_ref, out_ref, tile_ref = refs[-3:]
    sigma, product = landed(keep_ref, step_ref, refs[:-3])
    square = jnp.sum(square_ref[...])
    theta = product / square
    scale = 1.0 / jnp.sqrt(square / cells + 1e-06)
    tile = jnp.zeros(tile_ref.shape, jnp.float32)
    for b in range(2):
        v = vector_ref[b]
        residual = (sigma[b] - theta * v) * scale
        residual_ref[b] = residual
        corrected = v * scale - precond_ref[b] * residual
        out_ref[b] = corrected
        tile = tile + tile_sum(corrected * corrected)
    tile_ref[...] = tile


def scattered(n, me, store, near, far):
    width = near.shape[1]
    chips = n // 2
    other = swapped(far, CORE)
    over_rows = [g for g in range(5, chips, 2)][::-1]
    kept = chips - 1 - len(over_rows)
    shape = lambda *dims: jax.ShapeDtypeStruct(dims, jnp.float32)
    keep, column, rows, tile = local(
        functools.partial(merge_kernel, over_rows), "merge",
        (shape(kept, 2, width, width), shape(2, width, width),
         shape(2 * len(over_rows) * width + 8, width), shape(8, width)),
        (me, store), (near, far, other))
    rows = swapped(rows, ROW)
    column = swapped(column, COLUMN)
    step, *sends = local(
        functools.partial(fold_kernel, over_rows), "fold",
        (shape(2, width, width),) + (shape(2 * width + 8, width),) * (chips // 2 - 1),
        (), (keep, column, rows, tile))
    came = [swapped(x, 2 * ROW * (i + 1)) for i, x in reversed(list(enumerate(sends)))]
    return keep, swapped(step, ROW), [sends[0], *came]


def gathered(n, x, beside=None):
    pieces = {0: x}
    for k in reversed(range(8, n, 4)):
        pieces[k] = swapped(x, k)
    if beside is not None:
        x, _ = lax.optimization_barrier((x, beside))
    pieces[ROW] = swapped(x, ROW)
    pieces[COLUMN] = swapped(x, COLUMN)
    for k in reversed(range(8, n, 4)):
        pieces[k + ROW] = swapped(pieces[k], ROW)
    pieces[COLUMN + ROW] = swapped(pieces[ROW], COLUMN)
    for k in range(0, n, 2):
        pieces[k + CORE] = swapped(pieces[k], CORE)
    return [pieces[k] for k in range(n)]


def shards(wavefn, left_ops, right_ops, precond, fetch_map, store_map, pair_list, live_count):
    n = lax.axis_size("term")
    me = lax.axis_index("term").astype(jnp.int32).reshape(1)
    width = wavefn.shape[1]
    cells = wavefn.size * n
    tables = prep(n, me, pair_list[0], live_count, left_ops, right_ops)
    block = jax.ShapeDtypeStruct(wavefn.shape, jnp.float32)
    tile = jax.ShapeDtypeStruct((8, width), jnp.float32)
    vector = wavefn
    for iteration in range(ITERS):
        pieces = gathered(n, vector, tables if iteration == 0 else None)
        near, far, square = apply(n, me, fetch_map, store_map, tables, pieces)
        keep, step, parts = scattered(n, me, store_map, near, far)
        arrays = (keep, step, square, vector, precond, *parts)
        if iteration < ITERS - 1:
            vector = local(step_kernel, "step", block, (), arrays)
    residual, corrected, partial = local(
        functools.partial(last_kernel, cells), "last", (block, block, tile), (), arrays)
    tiles = lax.all_to_all(jnp.broadcast_to(partial[None], (n, 8, width)), "term",
                           split_axis=0, concat_axis=0, tiled=True)
    return corrected / jnp.sqrt(jnp.sum(tiles) / cells + 1e-06), residual


def solution(mesh):
    field = P(("group", "term"), None, None)
    return jax.shard_map(
        shards,
        mesh=mesh,
        in_specs=(field, field, field, field, P(), P(), P("term", None, None), P("term")),
        out_specs=(field, field),
        check_vma=False,
    )
```

```python
import functools

import jax
import jax.numpy as jnp
from jax import lax
from jax.experimental import pallas as pl
from jax.experimental.pallas import tpu as pltpu
from jax.sharding import PartitionSpec as P

ITERS = 2
CORE, ROW, COLUMN = 1, 2, 4
SMEM = pl.BlockSpec(memory_space=pltpu.SMEM)
VMEM = pl.BlockSpec(memory_space=pltpu.VMEM)


def params(mebibytes):
    return pltpu.CompilerParams(vmem_limit_bytes=mebibytes * 2**20)


def halves(x):
    high = x.astype(jnp.bfloat16)
    return high, (x - high.astype(jnp.float32)).astype(jnp.bfloat16)


def tile_sum(x):
    return jnp.sum(x.reshape(-1, 8, x.shape[-1]), axis=0)


def prep_kernel(n, spare, me_ref, fetch_ref, store_ref, pairs_ref, live_ref, vector_in, left_in, right_in, l4_ref, rr_ref,
                pick_ref, mine_ref, other_ref, first_ref, second_ref, dst_ref, one_ref, two_ref, count_ref, vector_ref,
                seen_ref, left_ref, right_ref, sems):
    copies = [pltpu.make_async_copy(source, target, sems.at[i]) for i, (source, target) in enumerate(
        ((left_in, left_ref), (right_in, right_ref), (vector_in, vector_ref)))]
    for copy in copies:
        copy.start()
    me = me_ref[0]
    terms = left_ref.shape[0]
    width = left_ref.shape[1]
    zero = terms * n
    for r in range(n):
        device = lax.bitwise_xor(me, r)
        pick_ref[r] = fetch_ref[device, me]
        mine_ref[r] = store_ref[me, device]
        other_ref[r] = store_ref[lax.bitwise_xor(me, CORE), device]

    def clear(cell, carry):
        first_ref[cell] = zero
        second_ref[cell] = zero
        seen_ref[cell] = 0
        return carry

    lax.fori_loop(0, terms * n, clear, 0, unroll=8)

    def pair(p, carry):
        extra, ops = carry
        a = lax.bitwise_xor(pairs_ref[p, 0], me)
        j = pairs_ref[p, 1]
        o = lax.bitwise_xor(pairs_ref[p, 2], me)
        cell = j * n + o
        source = a * terms + j
        seen = seen_ref[cell]
        seen_ref[cell] = seen + 1
        before = second_ref[cell]
        place = jnp.where(seen == 2, spare + extra, before)
        first_ref[cell] = jnp.where(seen == 0, source, first_ref[cell])
        second_ref[cell] = jnp.where(seen == 0, before, jnp.where(seen == 1, source, place))
        dst_ref[ops] = place
        one_ref[ops] = before
        two_ref[ops] = source
        return extra + (seen == 2).astype(jnp.int32), ops + (seen >= 2).astype(jnp.int32)

    _, ops = lax.fori_loop(0, live_ref[0], pair, (jnp.int32(0), jnp.int32(0)))
    count_ref[0] = ops
    for copy in copies:
        copy.wait()

    for j in range(terms):
        high, low = halves(left_ref[j])
        for k, part in enumerate((high, low, high, low)):
            l4_ref[j, :, k * width:(k + 1) * width] = part
        high, low = halves(right_ref[j])
        for k in range(2):
            row = (k * terms + j) * width
            rr_ref[row:row + width, :width] = high
            rr_ref[row:row + width, width:] = low


def prep(n, me, fetch, store, pairs, live, vector, left_ops, right_ops):
    terms, width = left_ops.shape[:2]
    npairs = pairs.shape[0]
    table = jax.ShapeDtypeStruct((terms * n,), jnp.int32)
    listed = jax.ShapeDtypeStruct((npairs,), jnp.int32)
    relative = jax.ShapeDtypeStruct((n,), jnp.int32)
    return pl.pallas_call(
        functools.partial(prep_kernel, n, terms * n + 1),
        out_shape=(
            jax.ShapeDtypeStruct((terms, width, 4 * width), jnp.bfloat16),
            jax.ShapeDtypeStruct((2 * terms * width, 2 * width), jnp.bfloat16),
            relative, relative, relative, table, table, listed, listed, listed,
            jax.ShapeDtypeStruct((1,), jnp.int32),
            jax.ShapeDtypeStruct(vector.shape, jnp.float32),
        ),
        in_specs=[SMEM] * 5 + [pl.BlockSpec(memory_space=pl.ANY)] * 3,
        out_specs=[VMEM] * 2 + [SMEM] * 9 + [VMEM],
        scratch_shapes=[
            pltpu.SMEM((terms * n,), jnp.int32),
            pltpu.VMEM(left_ops.shape, jnp.float32),
            pltpu.VMEM(left_ops.shape, jnp.float32),
            pltpu.SemaphoreType.DMA((3,)),
        ],
        compiler_params=params(16),
        name="prep",
    )(me, fetch, store, pairs, live, vector, left_ops, right_ops)


def right_products(picked, rows, start, mine_ref, first_ref, second_ref, rr_ref, pieces, block, total, near_ref, far_ref):
    width = block.shape[2]
    terms = rr_ref.shape[0] // (2 * width)
    n = len(pieces)
    product = jnp.zeros((8, width), jnp.float32)
    order = [(g, core) for g in picked for core in range(2)]
    for low_end in range(0, len(order), 4):
        group = order[low_end:low_end + 4]
        for k, (g, core) in enumerate(group):
            for j in range(terms):
                at = j * n + 2 * g + core
                high, low = halves(block[first_ref[at]] + block[second_ref[at]])
                total[low_end + k, :, j * width:(j + 1) * width] = high
                total[low_end + k, :, (terms + j) * width:(terms + j + 1) * width] = low
        both = jnp.dot(total[low_end:low_end + len(group)].reshape(len(group) * rows, 2 * terms * width), rr_ref[...],
                       preferred_element_type=jnp.float32)
        slots = both[:, :width] + both[:, width:]
        for k, (g, core) in enumerate(group):
            slot = slots[k * rows:(k + 1) * rows]
            at = picked.index(g) * rows
            if core and isinstance(far_ref, tuple):
                far_ref[picked.index(g)][...] = slot
            else:
                (far_ref if core else near_ref)[at:at + rows, :] = slot
            held = pieces[2 * g + core][mine_ref[2 * g + core], start:start + rows, :]
            product = product + tile_sum(held * slot)
    return product


def left_kernel(n, picked, rows, start, pick_ref, mine_ref, first_ref, second_ref, dst_ref, one_ref, two_ref,
                count_ref, l4_ref, rr_ref, *refs):
    pieces, (near_ref, far_ref, tile_ref, square_ref, block, total) = refs[:n], refs[n:]
    terms, width = l4_ref.shape[:2]
    square = jnp.zeros((8, width), jnp.float32)
    block[terms * n] = jnp.zeros((rows, width), jnp.float32)
    left = l4_ref[:, start:start + rows, :].reshape(terms * rows, 4 * width)
    for c in range(n // 2):
        columns = []
        for r in (2 * c, 2 * c + 1):
            high, low = halves(pieces[r][pick_ref[r]])
            columns.append(jnp.concatenate([high, high, low, low], axis=0))
            held = pieces[r][:, start:start + rows, :]
            square = square + tile_sum(held * held)
        both = jnp.dot(left, jnp.concatenate(columns, axis=1), preferred_element_type=jnp.float32)
        for k in range(2):
            at = (2 * c + k) * terms
            block[at:at + terms] = both[:, k * width:(k + 1) * width].reshape(terms, rows, width)
    square_ref[...] = square

    def add(i, carry):
        block[dst_ref[i]] = block[one_ref[i]] + block[two_ref[i]]
        return carry

    lax.fori_loop(0, count_ref[0], add, 0)
    tile_ref[...] = right_products(picked, rows, start, mine_ref, first_ref, second_ref, rr_ref, pieces, block,
                                   total, near_ref, far_ref)


def right_kernel(n, picked, rows, start, mine_ref, first_ref, second_ref, rr_ref, block, tile_ref, *refs):
    pieces, (near_ref, sum_ref), far_refs, total = refs[:n], refs[n:n + 2], refs[n + 2:-1], refs[-1]
    product = right_products(picked, rows, start, mine_ref, first_ref, second_ref, rr_ref, pieces, block,
                             total, near_ref, far_refs)
    sum_ref[...] = tile_ref[...] + product


def left(n, picked, rows, start, tables, pieces):
    terms, width = tables[0].shape[:2]
    spare = tables[7].shape[0] // 3
    shape = lambda *dims: jax.ShapeDtypeStruct(dims, jnp.float32)
    return pl.pallas_call(
        functools.partial(left_kernel, n, picked, rows, start),
        out_shape=(shape(len(picked) * rows, width), shape(len(picked) * rows, width), shape(8, width), shape(8, width),
                   shape(terms * n + 1 + spare, rows, width)),
        in_specs=[SMEM] * 8 + [VMEM] * (2 + n),
        out_specs=[VMEM] * 5,
        scratch_shapes=[pltpu.VMEM((2 * len(picked), rows, 2 * terms * width), jnp.bfloat16)],
        compiler_params=params(12 if n <= 16 else 48),
        name="left",
    )(*tables[2:4], *tables[5:], *tables[:2], *pieces)


def right(n, picked, rows, start, tables, blocks, tile, pieces):
    terms, width = tables[0].shape[:2]
    shape = lambda *dims: jax.ShapeDtypeStruct(dims, jnp.float32)
    return pl.pallas_call(
        functools.partial(right_kernel, n, picked, rows, start),
        out_shape=(shape(len(picked) * rows, width), shape(8, width)) + (shape(rows, width),) * len(picked),
        in_specs=[SMEM] * 3 + [VMEM] * (3 + n),
        out_specs=[VMEM] * (2 + len(picked)),
        scratch_shapes=[pltpu.VMEM((2 * len(picked), rows, 2 * terms * width), jnp.bfloat16)],
        compiler_params=params(12 if n <= 16 else 48),
        cost_estimate=pl.CostEstimate(flops=2 * 2 * len(picked) * rows * 2 * terms * width * 2 * width,
                                      bytes_accessed=2**20, transcendentals=0),
        name="right",
    )(tables[3], *tables[5:7], tables[1], blocks, tile, *pieces)


def joined(parts, count):
    if len(parts) == 1:
        return parts[0]
    width = parts[0].shape[1]
    return jnp.concatenate([x.reshape(count, -1, width) for x in parts], axis=1).reshape(-1, width)


def swapped(x, k):
    n = lax.axis_size("term")
    return lax.ppermute(x, "term", [(i, i ^ k) for i in range(n)])


def local(kernel, name, out_shape, scalars, arrays):
    many = isinstance(out_shape, tuple)
    return pl.pallas_call(
        kernel,
        out_shape=out_shape,
        in_specs=[SMEM] * len(scalars) + [VMEM] * len(arrays),
        out_specs=[VMEM] * len(out_shape) if many else VMEM,
        compiler_params=params(16),
        name=name,
    )(*scalars, *arrays)


def placed(mine_ref, other_ref, g, b, near, other):
    mine, others = mine_ref[2 * g], other_ref[2 * g]
    return near * (mine == b).astype(jnp.float32) + other * (others == b).astype(jnp.float32)


def merge_kernel(picked, mine_ref, others_ref, near_ref, other_ref, column_ref, rows_ref):
    width = near_ref.shape[1]
    column_ref[2] = jnp.zeros((width, width), jnp.float32)
    for i, g in enumerate(picked):
        for b in range(2):
            block = placed(mine_ref, others_ref, g, b, near_ref[i * width:(i + 1) * width],
                           other_ref[i * width:(i + 1) * width])
            if i == 0:
                column_ref[b] = block
            else:
                at = (2 * (i - 1) + b) * width
                rows_ref[at:at + width] = block


def fold_kernel(picked, early, mine_ref, others_ref, near_ref, column_ref, rows_ref, tile_ref, other_ref, *refs):
    far_refs, (own_ref, step_ref), send_refs = refs[:len(picked)], refs[len(picked):len(picked) + 2], refs[len(picked) + 2:]
    width = near_ref.shape[1]
    for i, g in enumerate(picked):
        for b in range(2):
            block = placed(mine_ref, others_ref, g, b, near_ref[i * width:(i + 1) * width],
                           far_refs[i][...])
            if g == 0:
                own_ref[b] = block
            elif g == 1:
                step_ref[b] = block + column_ref[b]
            else:
                if g + 1 in early[1:]:
                    at = (2 * early[1:].index(g + 1) + b) * width
                    block = block + rows_ref[at:at + width]
                send_refs[g // 2 - 1][b * width:(b + 1) * width] = block
    for send_ref in send_refs:
        send_ref[2 * width:] = tile_ref[...] + other_ref[...]


def landed(own_ref, step_ref, refs):
    width = own_ref.shape[2]
    sent, came = refs[0], refs[1:]
    tile = sent[2 * width:]
    for ref in came:
        tile = tile + ref[2 * width:]
    sums = []
    for b in range(2):
        total = own_ref[b] + step_ref[b]
        for ref in came:
            total = total + ref[b * width:(b + 1) * width]
        sums.append(total)
    return sums, jnp.sum(tile)


def step_kernel(own_ref, step_ref, square_ref, vector_ref, precond_ref, *refs):
    out_ref = refs[-1]
    sigma, product = landed(own_ref, step_ref, refs[:-1])
    theta = product / jnp.sum(square_ref[...])
    for b in range(2):
        v = vector_ref[b]
        out_ref[b] = v - precond_ref[b] * (sigma[b] - theta * v)


def last_kernel(cells, own_ref, step_ref, square_ref, vector_ref, precond_ref, *refs):
    residual_ref, out_ref, tile_ref = refs[-3:]
    sigma, product = landed(own_ref, step_ref, refs[:-3])
    square = jnp.sum(square_ref[...])
    theta = product / square
    scale = 1.0 / jnp.sqrt(square / cells + 1e-06)
    tile = jnp.zeros(tile_ref.shape, jnp.float32)
    for b in range(2):
        v = vector_ref[b]
        residual = (sigma[b] - theta * v) * scale
        residual_ref[b] = residual
        corrected = v * scale - precond_ref[b] * residual
        out_ref[b] = corrected
        tile = tile + tile_sum(corrected * corrected)
    tile_ref[...] = tile


def norm_kernel(cells, corrected_ref, tiles_ref, out_ref):
    scale = 1.0 / jnp.sqrt(jnp.sum(jnp.sum(tiles_ref[...], axis=0)) / cells + 1e-06)
    out_ref[...] = corrected_ref[...] * scale


def scattered(n, tables, pieces):
    width = pieces[0].shape[1]
    chips = n // 2
    rows = width if n <= 16 else width // 4
    starts = range(0, width, rows)
    over_rows = list(range(chips - 1, 3, -2))
    early = [3] + over_rows
    late = [g for g in range(chips) if g not in early]
    shape = lambda *dims: jax.ShapeDtypeStruct(dims, jnp.float32)

    firsts = [left(n, early, rows, start, tables, pieces) for start in starts]
    near, far = (joined([x[i] for x in firsts], len(early)) for i in range(2))
    square = sum(x[3] for x in firsts[1:]) + firsts[0][3] if len(firsts) > 1 else firsts[0][3]
    column, over = local(
        functools.partial(merge_kernel, early), "merge",
        (shape(3, width, width), shape(2 * len(over_rows) * width, width)), tables[3:5], (near, swapped(far, CORE)))
    tiles, column, over = lax.optimization_barrier(([x[2] for x in firsts], column, over))
    over_came = swapped(over, ROW)
    column_came = swapped(column, COLUMN)

    seconds = [right(n, late, rows, start, tables, x[4], tile, pieces)
               for start, x, tile in zip(starts, firsts, tiles)]
    near = joined([x[0] for x in seconds], len(late))
    far = [swapped(joined([x[2 + i] for x in seconds], 1), CORE) for i in range(len(late))]
    tile = sum(x[1] for x in seconds[1:]) + seconds[0][1] if len(seconds) > 1 else seconds[0][1]
    tile = tile + swapped(tile, CORE)
    own, step, *sends = local(
        functools.partial(fold_kernel, late, early), "fold",
        (shape(2, width, width),) * 2 + (shape(2 * width + 8, width),) * (chips // 2 - 1), tables[3:5],
        (near, column_came, over_came, tile, swapped(tile, ROW), *far))
    came = [swapped(x, 2 * ROW * (i + 1)) for i, x in reversed(list(enumerate(sends)))]
    return square, (own, swapped(step, ROW)), [sends[0], *came]


def gathered(n, x, held=None):
    pieces = {0: x}
    for k in reversed(range(8, n, 4)):
        pieces[k] = swapped(x, k)
    pieces[ROW] = swapped(x, ROW)
    pieces[COLUMN] = swapped(x, COLUMN)
    if held is not None:
        pieces[n - 4], pieces[0] = lax.optimization_barrier((pieces[n - 4], held))
    for k in reversed(range(8, n, 4)):
        pieces[k + ROW] = swapped(pieces[k], ROW)
    pieces[COLUMN + ROW] = swapped(pieces[ROW], COLUMN)
    for k in range(0, n, 2):
        pieces[k + CORE] = swapped(pieces[k], CORE)
    return [pieces[k] for k in range(n)]


def shards(wavefn, left_ops, right_ops, precond, fetch_map, store_map, pair_list, live_count):
    n = lax.axis_size("term")
    me = lax.axis_index("term").astype(jnp.int32).reshape(1)
    width = wavefn.shape[1]
    cells = wavefn.size * n
    *tables, held = prep(n, me, fetch_map, store_map, pair_list[0], live_count, wavefn, left_ops, right_ops)
    block = jax.ShapeDtypeStruct(wavefn.shape, jnp.float32)
    tile = jax.ShapeDtypeStruct((8, width), jnp.float32)
    vector = wavefn
    for iteration in range(ITERS):
        pieces = gathered(n, vector, held if iteration == 0 else None)
        vector = pieces[0]
        square, sums, parts = scattered(n, tables, pieces)
        arrays = (*sums, square, vector, precond, *parts)
        if iteration < ITERS - 1:
            vector = local(step_kernel, "step", block, (), arrays)
    residual, corrected, partial = local(
        functools.partial(last_kernel, cells), "last", (block, block, tile), (), arrays)
    tiles = lax.all_to_all(jnp.broadcast_to(partial[None], (n, 8, width)), "term",
                           split_axis=0, concat_axis=0, tiled=True)
    return local(functools.partial(norm_kernel, cells), "norm", block, (), (corrected, tiles)), residual


def solution(mesh):
    field = P(("group", "term"), None, None)
    return jax.shard_map(
        shards,
        mesh=mesh,
        in_specs=(field, field, field, field, P(), P(), P("term", None, None), P("term")),
        out_specs=(field, field),
        check_vma=False,
    )
```

```python
import functools

import jax
import jax.numpy as jnp
from jax import lax
from jax.experimental import pallas as pl
from jax.experimental.pallas import tpu as pltpu
from jax.sharding import PartitionSpec as P

ITERS = 2
CORE, ROW, COLUMN = 1, 2, 4
SENDERS = 6
SMEM = pl.BlockSpec(memory_space=pltpu.SMEM)
VMEM = pl.BlockSpec(memory_space=pltpu.VMEM)


def params(mebibytes):
    return pltpu.CompilerParams(vmem_limit_bytes=mebibytes * 2**20)


def halves(x):
    high = x.astype(jnp.bfloat16)
    return high, (x - high.astype(jnp.float32)).astype(jnp.bfloat16)


def tile_sum(x):
    return jnp.sum(x.reshape(-1, 8, x.shape[-1]), axis=0)


def prep_kernel(n, spare, me_ref, fetch_in, store_in, pairs_in, live_in, vector_in, left_in, right_in, l4_ref, rr_ref,
                pick_ref, mine_ref, place_ref, first_ref, second_ref, dst_ref, one_ref, two_ref, count_ref, vector_ref,
                seen_ref, fetch_ref, store_ref, pairs_ref, live_ref, left_ref, right_ref, sems):
    copies = [pltpu.make_async_copy(source, target, sems.at[i]) for i, (source, target) in enumerate((
        (fetch_in, fetch_ref), (store_in, store_ref), (pairs_in, pairs_ref), (live_in, live_ref),
        (left_in, left_ref), (right_in, right_ref), (vector_in, vector_ref)))]
    for copy in copies:
        copy.start()
    me = me_ref[0]
    terms = left_ref.shape[0]
    width = left_ref.shape[1]
    zero = terms * n
    npairs = pairs_ref.shape[0] // 3

    def clear(cell, carry):
        first_ref[cell] = zero
        second_ref[cell] = zero
        seen_ref[cell] = 0
        return carry

    lax.fori_loop(0, terms * n, clear, 0, unroll=8)
    for copy in copies[:4]:
        copy.wait()

    def relative(r, carry):
        device = lax.bitwise_xor(me, r)
        pick_ref[r] = fetch_ref[device, me]
        mine_ref[r] = store_ref[me, device]
        return carry

    lax.fori_loop(0, n, relative, 0)

    def chip(g, carry):
        for q in range(SENDERS):
            place_ref[q * (n // 2) + g] = store_ref[lax.bitwise_xor(me, q), lax.bitwise_xor(me, 2 * g)]
        return carry

    lax.fori_loop(0, n // 2, chip, 0)

    def pair(p, carry):
        extra, ops = carry
        a = lax.bitwise_xor(pairs_ref[p], me)
        j = pairs_ref[npairs + p]
        o = lax.bitwise_xor(pairs_ref[2 * npairs + p], me)
        cell = j * n + o
        source = a * terms + j
        seen = seen_ref[cell]
        seen_ref[cell] = seen + 1
        before = second_ref[cell]
        place = jnp.where(seen == 2, spare + extra, before)
        first_ref[cell] = jnp.where(seen == 0, source, first_ref[cell])
        second_ref[cell] = jnp.where(seen == 0, before, jnp.where(seen == 1, source, place))
        dst_ref[ops] = place
        one_ref[ops] = before
        two_ref[ops] = source
        return extra + (seen == 2).astype(jnp.int32), ops + (seen >= 2).astype(jnp.int32)

    _, ops = lax.fori_loop(0, live_ref[0], pair, (jnp.int32(0), jnp.int32(0)))
    count_ref[0] = ops
    for copy in copies[4:]:
        copy.wait()

    for j in range(terms):
        high, low = halves(left_ref[j])
        for k, part in enumerate((high, low, high, low)):
            l4_ref[j, :, k * width:(k + 1) * width] = part
        high, low = halves(right_ref[j])
        for k in range(2):
            row = (k * terms + j) * width
            rr_ref[row:row + width, :width] = high
            rr_ref[row:row + width, width:] = low


def at_home(x):
    return pltpu.with_memory_space_constraint(x, pltpu.HBM)


def prep(n, me, fetch, store, pairs, live, vector, left_ops, right_ops):
    terms, width = left_ops.shape[:2]
    npairs = pairs.shape[0] // 3
    table = jax.ShapeDtypeStruct((terms * n,), jnp.int32)
    listed = jax.ShapeDtypeStruct((npairs,), jnp.int32)
    relative = jax.ShapeDtypeStruct((n,), jnp.int32)
    return pl.pallas_call(
        functools.partial(prep_kernel, n, terms * n + 1),
        out_shape=(
            jax.ShapeDtypeStruct((terms, width, 4 * width), jnp.bfloat16),
            jax.ShapeDtypeStruct((2 * terms * width, 2 * width), jnp.bfloat16),
            relative, relative, jax.ShapeDtypeStruct((SENDERS * n // 2,), jnp.int32), table, table, listed, listed, listed,
            jax.ShapeDtypeStruct((1,), jnp.int32),
            jax.ShapeDtypeStruct(vector.shape, jnp.float32),
        ),
        in_specs=[SMEM] + [pl.BlockSpec(memory_space=pltpu.HBM)] * 7,
        out_specs=[VMEM] * 2 + [SMEM] * 9 + [VMEM],
        scratch_shapes=[
            pltpu.SMEM((terms * n,), jnp.int32),
            pltpu.SMEM(fetch.shape, jnp.int32),
            pltpu.SMEM(store.shape, jnp.int32),
            pltpu.SMEM(pairs.shape, jnp.int32),
            pltpu.SMEM((1,), jnp.int32),
            pltpu.VMEM(left_ops.shape, jnp.float32),
            pltpu.VMEM(left_ops.shape, jnp.float32),
            pltpu.SemaphoreType.DMA((7,)),
        ],
        compiler_params=params(16),
        name="prep",
    )(me, at_home(fetch), at_home(store), at_home(pairs), live, at_home(vector), at_home(left_ops), at_home(right_ops))


def apply_kernel(n, over_rows, rows, start, pick_ref, mine_ref, first_ref, second_ref, dst_ref, one_ref, two_ref, count_ref,
                 l4_ref, rr_ref, *refs):
    pieces, (near_ref, far_ref, row_ref, row_far_ref, column_ref, column_far_ref, square_ref, block, total) = refs[:n], refs[n:]
    terms, width = l4_ref.shape[:2]
    square = jnp.zeros((8, width), jnp.float32)
    product = jnp.zeros((8, width), jnp.float32)
    block[terms * n] = jnp.zeros((rows, width), jnp.float32)
    left = l4_ref[:, start:start + rows, :].reshape(terms * rows, 4 * width)
    for c in range(n // 2):
        columns = []
        for r in (2 * c, 2 * c + 1):
            high, low = halves(pieces[r][pick_ref[r]])
            columns.append(jnp.concatenate([high, high, low, low], axis=0))
            held = pieces[r][:, start:start + rows, :]
            square = square + tile_sum(held * held)
        both = jnp.dot(left, jnp.concatenate(columns, axis=1), preferred_element_type=jnp.float32)
        for k in range(2):
            at = (2 * c + k) * terms
            block[at:at + terms] = both[:, k * width:(k + 1) * width].reshape(terms, rows, width)
    square_ref[...] = square

    def add(i, carry):
        block[dst_ref[i]] = block[one_ref[i]] + block[two_ref[i]]
        return carry

    lax.fori_loop(0, count_ref[0], add, 0)
    late = 0
    for low_end in range(0, n, 4):
        for r in range(low_end, low_end + 4):
            for j in range(terms):
                at = j * n + r
                high, low = halves(block[first_ref[at]] + block[second_ref[at]])
                total[r, :, j * width:(j + 1) * width] = high
                total[r, :, (terms + j) * width:(terms + j + 1) * width] = low
        both = jnp.dot(total[low_end:low_end + 4].reshape(4 * rows, 2 * terms * width), rr_ref[...],
                       preferred_element_type=jnp.float32)
        slots = both[:, :width] + both[:, width:]
        for r in range(low_end, low_end + 4):
            slot = slots[(r - low_end) * rows:(r - low_end + 1) * rows]
            product = product + tile_sum(pieces[r][mine_ref[r], start:start + rows, :] * slot)
            g, core = divmod(r, 2)
            if g == 3:
                (column_far_ref if core else column_ref)[...] = slot
            elif g in over_rows:
                at = over_rows.index(g) * rows
                (row_far_ref if core else row_ref)[at:at + rows, :] = slot
            else:
                (far_ref if core else near_ref)[late * rows:(late + 1) * rows, :] = slot
                late += core
    for ref in (far_ref, row_ref, row_far_ref):
        ref[ref.shape[0] - 8:, :] = product


def apply(n, over_rows, rows, start, tables, pieces):
    terms, width = tables[0].shape[:2]
    spare = tables[7].shape[0] // 3
    late = n // 2 - 1 - len(over_rows)
    shape = lambda *dims: jax.ShapeDtypeStruct(dims, jnp.float32)
    return pl.pallas_call(
        functools.partial(apply_kernel, n, over_rows, rows, start),
        out_shape=(shape(late * rows, width), shape(late * rows + 8, width)) + (shape(len(over_rows) * rows + 8, width),) * 2
        + (shape(rows, width),) * 2 + (shape(8, width),),
        in_specs=[SMEM] * 8 + [VMEM] * (2 + n),
        out_specs=[VMEM] * 7,
        scratch_shapes=[
            pltpu.VMEM((terms * n + 1 + spare, rows, width), jnp.float32),
            pltpu.VMEM((n, rows, 2 * terms * width), jnp.bfloat16),
        ],
        compiler_params=params(32 if n <= 16 else 56),
        name="apply",
    )(*tables[2:4], *tables[5:], *tables[:2], *pieces)


def joined(parts, count):
    if len(parts) == 1:
        return parts[0]
    height, width = parts[0].shape
    end = height // (8 * count) * 8 * count
    whole = jnp.concatenate([x[:end].reshape(count, -1, width) for x in parts], axis=1).reshape(-1, width)
    return whole if end == height else jnp.concatenate([whole, sum(x[end:] for x in parts)])


def swapped(x, k):
    n = lax.axis_size("term")
    return lax.ppermute(x, "term", [(i, i ^ k) for i in range(n)])


def local(kernel, name, out_shape, scalars, arrays):
    many = isinstance(out_shape, tuple)
    return pl.pallas_call(
        kernel,
        out_shape=out_shape,
        in_specs=[SMEM] * len(scalars) + [VMEM] * len(arrays),
        out_specs=[VMEM] * len(out_shape) if many else VMEM,
        compiler_params=params(16),
        name=name,
    )(*scalars, *arrays)


def fold_kernel(late, over_rows, place_ref, near_ref, far_in, far_ref, row_ref, row_far_ref, column_ref, column_far_ref,
                own_ref, step_ref, *send_refs):
    width = near_ref.shape[1]
    chips = place_ref.shape[0] // SENDERS
    end = len(late) * width
    over = len(over_rows) * width
    tile = far_in[end:] + far_ref[end:] + row_ref[over:] + row_far_ref[over:]
    for i, g in enumerate(late):
        come = [(0, near_ref, i), (1, far_ref, i)]
        if g == 1:
            come += [(4, column_ref, 0), (5, column_far_ref, 0)]
        if g + 1 in over_rows:
            come += [(2, row_ref, over_rows.index(g + 1)), (3, row_far_ref, over_rows.index(g + 1))]
        for b in range(2):
            block = sum(ref[at * width:(at + 1) * width] * (place_ref[q * chips + g] == b).astype(jnp.float32)
                        for q, ref, at in come)
            if g == 0:
                own_ref[b] = block
            elif g == 1:
                step_ref[b] = block
            else:
                send_refs[g // 2 - 1][b * width:(b + 1) * width] = block
    for send_ref in send_refs:
        send_ref[2 * width:] = tile


def landed(own_ref, step_ref, refs):
    width = own_ref.shape[2]
    sent, came = refs[0], refs[1:]
    tile = sent[2 * width:]
    for ref in came:
        tile = tile + ref[2 * width:]
    sums = []
    for b in range(2):
        total = own_ref[b] + step_ref[b]
        for ref in came:
            total = total + ref[b * width:(b + 1) * width]
        sums.append(total)
    return sums, jnp.sum(tile)


def step_kernel(own_ref, step_ref, square_ref, vector_ref, precond_ref, *refs):
    out_ref = refs[-1]
    sigma, product = landed(own_ref, step_ref, refs[:-1])
    theta = product / jnp.sum(square_ref[...])
    for b in range(2):
        v = vector_ref[b]
        out_ref[b] = v - precond_ref[b] * (sigma[b] - theta * v)


def last_kernel(cells, own_ref, step_ref, square_ref, vector_ref, precond_ref, *refs):
    residual_ref, out_ref, tile_ref = refs[-3:]
    sigma, product = landed(own_ref, step_ref, refs[:-3])
    square = jnp.sum(square_ref[...])
    theta = product / square
    scale = 1.0 / jnp.sqrt(square / cells + 1e-06)
    tile = jnp.zeros(tile_ref.shape, jnp.float32)
    for b in range(2):
        v = vector_ref[b]
        residual = (sigma[b] - theta * v) * scale
        residual_ref[b] = residual
        corrected = v * scale - precond_ref[b] * residual
        out_ref[b] = corrected
        tile = tile + tile_sum(corrected * corrected)
    tile_ref[...] = tile


def norm_kernel(cells, corrected_ref, tiles_ref, out_ref):
    scale = 1.0 / jnp.sqrt(jnp.sum(jnp.sum(tiles_ref[...], axis=0)) / cells + 1e-06)
    out_ref[...] = corrected_ref[...] * scale


def scattered(n, tables, pieces):
    width = pieces[0].shape[1]
    chips = n // 2
    rows = width if n <= 16 else width // 4
    over_rows = list(range(chips - 1, 3, -2))
    late = [g for g in range(chips) if g != 3 and g not in over_rows]
    shape = lambda *dims: jax.ShapeDtypeStruct(dims, jnp.float32)
    runs = [apply(n, over_rows, rows, start, tables, pieces) for start in range(0, width, rows)]
    counts = (len(late), len(late), len(over_rows), len(over_rows), 1, 1)
    near, far, row, row_far, column, column_far = (joined([x[i] for x in runs], k) for i, k in enumerate(counts))
    square = functools.reduce(jnp.add, [x[6] for x in runs])
    own, step, *sends = local(
        functools.partial(fold_kernel, late, over_rows), "fold",
        (shape(2, width, width),) * 2 + (shape(2 * width + 8, width),) * (chips // 2 - 1), tables[4:5],
        (near, far, swapped(far, CORE), swapped(row, ROW), swapped(row_far, ROW + CORE), swapped(column, COLUMN),
         swapped(column_far, COLUMN + CORE)))
    came = [swapped(x, 2 * ROW * (i + 1)) for i, x in reversed(list(enumerate(sends)))]
    return square, (own, swapped(step, ROW)), [sends[0], *came]


def gathered(n, x, held=None):
    pieces = {0: x}
    for k in reversed(range(8, n, 4)):
        pieces[k] = swapped(x, k)
    pieces[ROW] = swapped(x, ROW)
    pieces[COLUMN] = swapped(x, COLUMN)
    if held is not None:
        pieces[n - 4], pieces[0] = lax.optimization_barrier((pieces[n - 4], held))
    for k in reversed(range(8, n, 4)):
        pieces[k + ROW] = swapped(pieces[k], ROW)
    pieces[COLUMN + ROW] = swapped(pieces[ROW], COLUMN)
    for k in range(0, n, 2):
        pieces[k + CORE] = swapped(pieces[k], CORE)
    return [pieces[k] for k in range(n)]


def shards(wavefn, left_ops, right_ops, precond, fetch_map, store_map, pair_list, live_count):
    n = lax.axis_size("term")
    me = lax.axis_index("term").astype(jnp.int32).reshape(1)
    width = wavefn.shape[1]
    cells = wavefn.size * n
    *tables, held = prep(n, me, fetch_map, store_map, pair_list[0].T.reshape(-1), live_count, wavefn, left_ops, right_ops)
    block = jax.ShapeDtypeStruct(wavefn.shape, jnp.float32)
    tile = jax.ShapeDtypeStruct((8, width), jnp.float32)
    vector = wavefn
    for iteration in range(ITERS):
        pieces = gathered(n, vector, held if iteration == 0 else None)
        vector = pieces[0]
        square, sums, parts = scattered(n, tables, pieces)
        arrays = (*sums, square, vector, precond, *parts)
        if iteration < ITERS - 1:
            vector = local(step_kernel, "step", block, (), arrays)
    residual, corrected, partial = local(
        functools.partial(last_kernel, cells), "last", (block, block, tile), (), arrays)
    tiles = lax.all_to_all(jnp.broadcast_to(partial[None], (n, 8, width)), "term",
                           split_axis=0, concat_axis=0, tiled=True)
    return local(functools.partial(norm_kernel, cells), "norm", block, (), (corrected, tiles)), residual


def solution(mesh):
    field = P(("group", "term"), None, None)
    return jax.shard_map(
        shards,
        mesh=mesh,
        in_specs=(field, field, field, field, P(), P(), P("term", None, None), P("term")),
        out_specs=(field, field),
        check_vma=False,
    )
```

```python
import functools

import jax
import jax.numpy as jnp
from jax import lax
from jax.experimental import pallas as pl
from jax.experimental.pallas import tpu as pltpu
from jax.sharding import PartitionSpec as P

ITERS = 2
CORE, ROW, COLUMN = 1, 2, 4
SENDERS = 6
SMEM = pl.BlockSpec(memory_space=pltpu.SMEM)
VMEM = pl.BlockSpec(memory_space=pltpu.VMEM)


def params(mebibytes):
    return pltpu.CompilerParams(vmem_limit_bytes=mebibytes * 2**20)


def halves(x):
    high = x.astype(jnp.bfloat16)
    return high, (x - high.astype(jnp.float32)).astype(jnp.bfloat16)


def tile_sum(x):
    return jnp.sum(x.reshape(-1, 8, x.shape[-1]), axis=0)


def prep_kernel(n, spare, me_ref, fetch_in, store_in, pairs_in, live_in, vector_in, left_in, right_in, l4_ref, rr_ref,
                pick_ref, mine_ref, place_ref, first_ref, second_ref, dst_ref, one_ref, two_ref, count_ref, vector_ref,
                seen_ref, fetch_ref, store_ref, pairs_ref, live_ref, left_ref, right_ref, sems):
    copies = [pltpu.make_async_copy(source, target, sems.at[i]) for i, (source, target) in enumerate((
        (fetch_in, fetch_ref), (store_in, store_ref), (pairs_in, pairs_ref), (live_in, live_ref),
        (left_in, left_ref), (right_in, right_ref), (vector_in, vector_ref)))]
    for copy in copies:
        copy.start()
    me = me_ref[0]
    terms = left_ref.shape[0]
    width = left_ref.shape[1]
    zero = terms * n
    npairs = pairs_ref.shape[0] // 3

    def clear(cell, carry):
        first_ref[cell] = zero
        second_ref[cell] = zero
        seen_ref[cell] = 0
        return carry

    lax.fori_loop(0, terms * n, clear, 0, unroll=8)
    for copy in copies[:4]:
        copy.wait()

    def relative(r, carry):
        device = lax.bitwise_xor(me, r)
        pick_ref[r] = fetch_ref[device, me]
        mine_ref[r] = store_ref[me, device]
        return carry

    lax.fori_loop(0, n, relative, 0)

    def chip(g, carry):
        for q in range(SENDERS):
            place_ref[q * (n // 2) + g] = store_ref[lax.bitwise_xor(me, q), lax.bitwise_xor(me, 2 * g)]
        return carry

    lax.fori_loop(0, n // 2, chip, 0)

    def pair(p, carry):
        extra, ops = carry
        a = lax.bitwise_xor(pairs_ref[p], me)
        j = pairs_ref[npairs + p]
        o = lax.bitwise_xor(pairs_ref[2 * npairs + p], me)
        cell = j * n + o
        source = a * terms + j
        seen = seen_ref[cell]
        seen_ref[cell] = seen + 1
        before = second_ref[cell]
        place = jnp.where(seen == 2, spare + extra, before)
        first_ref[cell] = jnp.where(seen == 0, source, first_ref[cell])
        second_ref[cell] = jnp.where(seen == 0, before, jnp.where(seen == 1, source, place))
        dst_ref[ops] = place
        one_ref[ops] = before
        two_ref[ops] = source
        return extra + (seen == 2).astype(jnp.int32), ops + (seen >= 2).astype(jnp.int32)

    _, ops = lax.fori_loop(0, live_ref[0], pair, (jnp.int32(0), jnp.int32(0)))
    count_ref[0] = ops
    for copy in copies[4:]:
        copy.wait()

    for j in range(terms):
        high, low = halves(left_ref[j])
        for k, part in enumerate((high, low, high, low)):
            l4_ref[j, :, k * width:(k + 1) * width] = part
        high, low = halves(right_ref[j])
        for k in range(2):
            row = (k * terms + j) * width
            rr_ref[row:row + width, :width] = high
            rr_ref[row:row + width, width:] = low


def at_home(x):
    return pltpu.with_memory_space_constraint(x, pltpu.HBM)


def prep(n, me, fetch, store, pairs, live, vector, left_ops, right_ops):
    terms, width = left_ops.shape[:2]
    npairs = pairs.shape[0] // 3
    table = jax.ShapeDtypeStruct((terms * n,), jnp.int32)
    listed = jax.ShapeDtypeStruct((npairs,), jnp.int32)
    relative = jax.ShapeDtypeStruct((n,), jnp.int32)
    return pl.pallas_call(
        functools.partial(prep_kernel, n, terms * n + 1),
        out_shape=(
            jax.ShapeDtypeStruct((terms, width, 4 * width), jnp.bfloat16),
            jax.ShapeDtypeStruct((2 * terms * width, 2 * width), jnp.bfloat16),
            relative, relative, jax.ShapeDtypeStruct((SENDERS * n // 2,), jnp.int32), table, table, listed, listed, listed,
            jax.ShapeDtypeStruct((1,), jnp.int32),
            jax.ShapeDtypeStruct(vector.shape, jnp.float32),
        ),
        in_specs=[SMEM] + [pl.BlockSpec(memory_space=pltpu.HBM)] * 7,
        out_specs=[VMEM] * 2 + [SMEM] * 9 + [VMEM],
        scratch_shapes=[
            pltpu.SMEM((terms * n,), jnp.int32),
            pltpu.SMEM(fetch.shape, jnp.int32),
            pltpu.SMEM(store.shape, jnp.int32),
            pltpu.SMEM(pairs.shape, jnp.int32),
            pltpu.SMEM((1,), jnp.int32),
            pltpu.VMEM(left_ops.shape, jnp.float32),
            pltpu.VMEM(left_ops.shape, jnp.float32),
            pltpu.SemaphoreType.DMA((7,)),
        ],
        compiler_params=params(16),
        name="prep",
    )(me, at_home(fetch), at_home(store), at_home(pairs), live, at_home(vector), at_home(left_ops), at_home(right_ops))


def nearest_last(n):
    return [*range(8), *(r for k in reversed(range(8, n, 4)) for r in range(k, k + 4))]


def apply_kernel(n, over_rows, rows, start, pick_ref, mine_ref, first_ref, second_ref, dst_ref, one_ref, two_ref, count_ref,
                 l4_ref, rr_ref, *refs):
    pieces = [refs[nearest_last(n).index(k)] for k in range(n)]
    near_ref, far_ref, row_ref, row_far_ref, column_ref, column_far_ref, square_ref, block, total = refs[n:]
    terms, width = l4_ref.shape[:2]
    square = jnp.zeros((8, width), jnp.float32)
    product = jnp.zeros((8, width), jnp.float32)
    block[terms * n] = jnp.zeros((rows, width), jnp.float32)
    left = l4_ref[:, start:start + rows, :].reshape(terms * rows, 4 * width)
    for c in range(n // 2):
        columns = []
        for r in (2 * c, 2 * c + 1):
            high, low = halves(pieces[r][pick_ref[r]])
            columns.append(jnp.concatenate([high, high, low, low], axis=0))
            held = pieces[r][:, start:start + rows, :]
            square = square + tile_sum(held * held)
        both = jnp.dot(left, jnp.concatenate(columns, axis=1), preferred_element_type=jnp.float32)
        for k in range(2):
            at = (2 * c + k) * terms
            block[at:at + terms] = both[:, k * width:(k + 1) * width].reshape(terms, rows, width)
    square_ref[...] = square

    def add(i, carry):
        block[dst_ref[i]] = block[one_ref[i]] + block[two_ref[i]]
        return carry

    lax.fori_loop(0, count_ref[0], add, 0)
    late = 0
    for low_end in range(0, n, 4):
        for r in range(low_end, low_end + 4):
            for j in range(terms):
                at = j * n + r
                high, low = halves(block[first_ref[at]] + block[second_ref[at]])
                total[r, :, j * width:(j + 1) * width] = high
                total[r, :, (terms + j) * width:(terms + j + 1) * width] = low
        both = jnp.dot(total[low_end:low_end + 4].reshape(4 * rows, 2 * terms * width), rr_ref[...],
                       preferred_element_type=jnp.float32)
        slots = both[:, :width] + both[:, width:]
        for r in range(low_end, low_end + 4):
            slot = slots[(r - low_end) * rows:(r - low_end + 1) * rows]
            product = product + tile_sum(pieces[r][mine_ref[r], start:start + rows, :] * slot)
            g, core = divmod(r, 2)
            if g == 3:
                (column_far_ref if core else column_ref)[...] = slot
            elif g in over_rows:
                at = over_rows.index(g) * rows
                (row_far_ref if core else row_ref)[at:at + rows, :] = slot
            else:
                (far_ref if core else near_ref)[late * rows:(late + 1) * rows, :] = slot
                late += core
    for ref in (far_ref, row_ref, row_far_ref):
        ref[ref.shape[0] - 8:, :] = product


def apply(n, over_rows, rows, start, tables, pieces):
    terms, width = tables[0].shape[:2]
    spare = tables[7].shape[0] // 3
    late = n // 2 - 1 - len(over_rows)
    shape = lambda *dims: jax.ShapeDtypeStruct(dims, jnp.float32)
    return pl.pallas_call(
        functools.partial(apply_kernel, n, over_rows, rows, start),
        out_shape=(shape(late * rows, width), shape(late * rows + 8, width)) + (shape(len(over_rows) * rows + 8, width),) * 2
        + (shape(rows, width),) * 2 + (shape(8, width),),
        in_specs=[SMEM] * 8 + [VMEM] * (2 + n),
        out_specs=[VMEM] * 7,
        scratch_shapes=[
            pltpu.VMEM((terms * n + 1 + spare, rows, width), jnp.float32),
            pltpu.VMEM((n, rows, 2 * terms * width), jnp.bfloat16),
        ],
        compiler_params=params(32 if n <= 16 else 56),
        name="apply",
    )(*tables[2:4], *tables[5:], *tables[:2], *(pieces[k] for k in nearest_last(n)))


def joined(parts, count):
    if len(parts) == 1:
        return parts[0]
    height, width = parts[0].shape
    end = height // (8 * count) * 8 * count
    whole = jnp.concatenate([x[:end].reshape(count, -1, width) for x in parts], axis=1).reshape(-1, width)
    return whole if end == height else jnp.concatenate([whole, sum(x[end:] for x in parts)])


def swapped(x, k):
    n = lax.axis_size("term")
    return lax.ppermute(x, "term", [(i, i ^ k) for i in range(n)])


def local(kernel, name, out_shape, scalars, arrays):
    many = isinstance(out_shape, tuple)
    return pl.pallas_call(
        kernel,
        out_shape=out_shape,
        in_specs=[SMEM] * len(scalars) + [VMEM] * len(arrays),
        out_specs=[VMEM] * len(out_shape) if many else VMEM,
        compiler_params=params(16),
        name=name,
    )(*scalars, *arrays)


def fold_kernel(late, over_rows, place_ref, near_ref, far_in, far_ref, row_ref, row_far_ref, column_ref, column_far_ref,
                own_ref, step_ref, *send_refs):
    width = near_ref.shape[1]
    chips = place_ref.shape[0] // SENDERS
    end = len(late) * width
    over = len(over_rows) * width
    tile = far_in[end:] + far_ref[end:] + row_ref[over:] + row_far_ref[over:]
    for i, g in enumerate(late):
        come = [(0, near_ref, i), (1, far_ref, i)]
        if g == 1:
            come += [(4, column_ref, 0), (5, column_far_ref, 0)]
        if g + 1 in over_rows:
            come += [(2, row_ref, over_rows.index(g + 1)), (3, row_far_ref, over_rows.index(g + 1))]
        for b in range(2):
            block = sum(ref[at * width:(at + 1) * width] * (place_ref[q * chips + g] == b).astype(jnp.float32)
                        for q, ref, at in come)
            if g == 0:
                own_ref[b] = block
            elif g == 1:
                step_ref[b] = block
            else:
                send_refs[g // 2 - 1][b * width:(b + 1) * width] = block
    for send_ref in send_refs:
        send_ref[2 * width:] = tile


def landed(own_ref, step_ref, refs):
    width = own_ref.shape[2]
    sent, came = refs[0], refs[1:]
    tile = sent[2 * width:]
    for ref in came:
        tile = tile + ref[2 * width:]
    sums = []
    for b in range(2):
        total = own_ref[b] + step_ref[b]
        for ref in came:
            total = total + ref[b * width:(b + 1) * width]
        sums.append(total)
    return sums, jnp.sum(tile)


def step_kernel(own_ref, step_ref, square_ref, vector_ref, precond_ref, *refs):
    out_ref = refs[-1]
    sigma, product = landed(own_ref, step_ref, refs[:-1])
    theta = product / jnp.sum(square_ref[...])
    for b in range(2):
        v = vector_ref[b]
        out_ref[b] = v - precond_ref[b] * (sigma[b] - theta * v)


def last_kernel(cells, own_ref, step_ref, square_ref, vector_ref, precond_ref, *refs):
    residual_ref, out_ref, tile_ref = refs[-3:]
    sigma, product = landed(own_ref, step_ref, refs[:-3])
    square = jnp.sum(square_ref[...])
    theta = product / square
    scale = 1.0 / jnp.sqrt(square / cells + 1e-06)
    tile = jnp.zeros(tile_ref.shape, jnp.float32)
    for b in range(2):
        v = vector_ref[b]
        residual = (sigma[b] - theta * v) * scale
        residual_ref[b] = residual
        corrected = v * scale - precond_ref[b] * residual
        out_ref[b] = corrected
        tile = tile + tile_sum(corrected * corrected)
    tile_ref[...] = tile


def norm_kernel(cells, corrected_ref, tiles_ref, out_ref):
    scale = 1.0 / jnp.sqrt(jnp.sum(jnp.sum(tiles_ref[...], axis=0)) / cells + 1e-06)
    out_ref[...] = corrected_ref[...] * scale


def scattered(n, tables, pieces):
    width = pieces[0].shape[1]
    chips = n // 2
    rows = width if n <= 16 else width // 4
    over_rows = list(range(chips - 1, 3, -2))
    late = [g for g in range(chips) if g != 3 and g not in over_rows]
    shape = lambda *dims: jax.ShapeDtypeStruct(dims, jnp.float32)
    runs = [apply(n, over_rows, rows, start, tables, pieces) for start in range(0, width, rows)]
    counts = (len(late), len(late), len(over_rows), len(over_rows), 1, 1)
    near, far, row, row_far, column, column_far = (joined([x[i] for x in runs], k) for i, k in enumerate(counts))
    square = functools.reduce(jnp.add, [x[6] for x in runs])
    own, step, *sends = local(
        functools.partial(fold_kernel, late, over_rows), "fold",
        (shape(2, width, width),) * 2 + (shape(2 * width + 8, width),) * (chips // 2 - 1), tables[4:5],
        (near, far, swapped(far, CORE), swapped(row, ROW), swapped(row_far, ROW + CORE), swapped(column, COLUMN),
         swapped(column_far, COLUMN + CORE)))
    came = [swapped(sends[i], 2 * ROW * (i + 1)) for i in (*range(1, len(sends)), 0)]
    return square, (own, swapped(step, ROW)), [sends[0], *came]


def gathered(n, x, held=None):
    pieces = {0: x}
    for k in range(8, n, 4):
        pieces[k] = swapped(x, k)
    if held is not None:
        x, pieces[0] = lax.optimization_barrier((x, held))
    pieces[COLUMN] = swapped(x, COLUMN)
    pieces[ROW] = swapped(x, ROW)
    for k in range(8, n, 4):
        pieces[k + ROW] = swapped(pieces[k], ROW)
    pieces[COLUMN + ROW] = swapped(pieces[ROW], COLUMN)
    for k in range(0, n, 2):
        pieces[k + CORE] = swapped(pieces[k], CORE)
    return [pieces[k] for k in range(n)]


def shards(wavefn, left_ops, right_ops, precond, fetch_map, store_map, pair_list, live_count):
    n = lax.axis_size("term")
    me = lax.axis_index("term").astype(jnp.int32).reshape(1)
    width = wavefn.shape[1]
    cells = wavefn.size * n
    *tables, held = prep(n, me, fetch_map, store_map, pair_list[0].T.reshape(-1), live_count, wavefn, left_ops, right_ops)
    block = jax.ShapeDtypeStruct(wavefn.shape, jnp.float32)
    tile = jax.ShapeDtypeStruct((8, width), jnp.float32)
    vector = wavefn
    for iteration in range(ITERS):
        pieces = gathered(n, vector, held if iteration == 0 else None)
        vector = pieces[0]
        square, sums, parts = scattered(n, tables, pieces)
        arrays = (*sums, square, vector, precond, *parts)
        if iteration < ITERS - 1:
            vector = local(step_kernel, "step", block, (), arrays)
    residual, corrected, partial = local(
        functools.partial(last_kernel, cells), "last", (block, block, tile), (), arrays)
    tiles = lax.all_to_all(jnp.broadcast_to(partial[None], (n, 8, width)), "term",
                           split_axis=0, concat_axis=0, tiled=True)
    return local(functools.partial(norm_kernel, cells), "norm", block, (), (corrected, tiles)), residual


def solution(mesh):
    field = P(("group", "term"), None, None)
    return jax.shard_map(
        shards,
        mesh=mesh,
        in_specs=(field, field, field, field, P(), P(), P("term", None, None), P("term")),
        out_specs=(field, field),
        check_vma=False,
    )
```

```python
import functools

import jax
import jax.numpy as jnp
from jax import lax
from jax.experimental import pallas as pl
from jax.experimental.pallas import tpu as pltpu
from jax.sharding import PartitionSpec as P

ITERS = 2
CORE, ROW, COLUMN = 1, 2, 4
LAST = 5
SENDERS = 6
SMEM = pl.BlockSpec(memory_space=pltpu.SMEM)
VMEM = pl.BlockSpec(memory_space=pltpu.VMEM)


def params(mebibytes):
    return pltpu.CompilerParams(vmem_limit_bytes=mebibytes * 2**20)


def halves(x):
    high = x.astype(jnp.bfloat16)
    return high, (x - high.astype(jnp.float32)).astype(jnp.bfloat16)


def tile_sum(x):
    return jnp.sum(x.reshape(-1, 8, x.shape[-1]), axis=0)


def prep_kernel(n, spare, me_ref, fetch_in, store_in, pairs_in, live_in, vector_in, left_in, right_in, l4_ref, rr_ref,
                pick_ref, mine_ref, place_ref, first_ref, second_ref, dst_ref, one_ref, two_ref, count_ref, vector_ref,
                seen_ref, fetch_ref, store_ref, pairs_ref, live_ref, left_ref, right_ref, sems):
    copies = [pltpu.make_async_copy(source, target, sems.at[i]) for i, (source, target) in enumerate((
        (fetch_in, fetch_ref), (store_in, store_ref), (pairs_in, pairs_ref), (live_in, live_ref),
        (left_in, left_ref), (right_in, right_ref), (vector_in, vector_ref)))]
    for copy in copies:
        copy.start()
    me = me_ref[0]
    terms = left_ref.shape[0]
    width = left_ref.shape[1]
    zero = terms * n
    npairs = pairs_ref.shape[0] // 3

    def clear(cell, carry):
        first_ref[cell] = zero
        second_ref[cell] = zero
        seen_ref[cell] = 0
        return carry

    lax.fori_loop(0, terms * n, clear, 0, unroll=8)
    for copy in copies[:4]:
        copy.wait()

    def relative(r, carry):
        device = lax.bitwise_xor(me, r)
        pick_ref[r] = fetch_ref[device, me]
        mine_ref[r] = store_ref[me, device]
        return carry

    lax.fori_loop(0, n, relative, 0)

    def chip(g, carry):
        for q in range(SENDERS):
            place_ref[q * (n // 2) + g] = store_ref[lax.bitwise_xor(me, q), lax.bitwise_xor(me, 2 * g)]
        return carry

    lax.fori_loop(0, n // 2, chip, 0)

    def pair(p, carry):
        extra, ops = carry
        a = lax.bitwise_xor(pairs_ref[p], me)
        j = pairs_ref[npairs + p]
        o = lax.bitwise_xor(pairs_ref[2 * npairs + p], me)
        cell = j * n + o
        source = a * terms + j
        seen = seen_ref[cell]
        seen_ref[cell] = seen + 1
        before = second_ref[cell]
        place = jnp.where(seen == 2, spare + extra, before)
        first_ref[cell] = jnp.where(seen == 0, source, first_ref[cell])
        second_ref[cell] = jnp.where(seen == 0, before, jnp.where(seen == 1, source, place))
        dst_ref[ops] = place
        one_ref[ops] = before
        two_ref[ops] = source
        return extra + (seen == 2).astype(jnp.int32), ops + (seen >= 2).astype(jnp.int32)

    _, ops = lax.fori_loop(0, live_ref[0], pair, (jnp.int32(0), jnp.int32(0)))
    count_ref[0] = ops
    for copy in copies[4:]:
        copy.wait()

    for j in range(terms):
        high, low = halves(left_ref[j])
        for k, part in enumerate((high, low, high, low)):
            l4_ref[j, :, k * width:(k + 1) * width] = part
        high, low = halves(right_ref[j])
        for k in range(2):
            row = (k * terms + j) * width
            rr_ref[row:row + width, :width] = high
            rr_ref[row:row + width, width:] = low


def at_home(x):
    return pltpu.with_memory_space_constraint(x, pltpu.HBM)


def prep(n, me, fetch, store, pairs, live, vector, left_ops, right_ops):
    terms, width = left_ops.shape[:2]
    npairs = pairs.shape[0] // 3
    table = jax.ShapeDtypeStruct((terms * n,), jnp.int32)
    listed = jax.ShapeDtypeStruct((npairs,), jnp.int32)
    relative = jax.ShapeDtypeStruct((n,), jnp.int32)
    return pl.pallas_call(
        functools.partial(prep_kernel, n, terms * n + 1),
        out_shape=(
            jax.ShapeDtypeStruct((terms, width, 4 * width), jnp.bfloat16),
            jax.ShapeDtypeStruct((2 * terms * width, 2 * width), jnp.bfloat16),
            relative, relative, jax.ShapeDtypeStruct((SENDERS * n // 2,), jnp.int32), table, table, listed, listed, listed,
            jax.ShapeDtypeStruct((1,), jnp.int32),
            jax.ShapeDtypeStruct(vector.shape, jnp.float32),
        ),
        in_specs=[SMEM] + [pl.BlockSpec(memory_space=pltpu.HBM)] * 7,
        out_specs=[VMEM] * 2 + [SMEM] * 9 + [VMEM],
        scratch_shapes=[
            pltpu.SMEM((terms * n,), jnp.int32),
            pltpu.SMEM(fetch.shape, jnp.int32),
            pltpu.SMEM(store.shape, jnp.int32),
            pltpu.SMEM(pairs.shape, jnp.int32),
            pltpu.SMEM((1,), jnp.int32),
            pltpu.VMEM(left_ops.shape, jnp.float32),
            pltpu.VMEM(left_ops.shape, jnp.float32),
            pltpu.SemaphoreType.DMA((7,)),
        ],
        compiler_params=params(16),
        name="prep",
    )(me, at_home(fetch), at_home(store), at_home(pairs), live, at_home(vector), at_home(left_ops), at_home(right_ops))


def left_products(chunks, rows, start, pick_ref, l4_ref, pieces, block):
    terms, width = l4_ref.shape[:2]
    square = jnp.zeros((8, width), jnp.float32)
    left = l4_ref[:, start:start + rows, :].reshape(terms * rows, 4 * width)
    for c in chunks:
        columns = []
        for r in (2 * c, 2 * c + 1):
            high, low = halves(pieces[r][pick_ref[r]])
            columns.append(jnp.concatenate([high, high, low, low], axis=0))
            held = pieces[r][:, start:start + rows, :]
            square = square + tile_sum(held * held)
        both = jnp.dot(left, jnp.concatenate(columns, axis=1), preferred_element_type=jnp.float32)
        for k in range(2):
            at = (2 * c + k) * terms
            block[at:at + terms] = both[:, k * width:(k + 1) * width].reshape(terms, rows, width)
    return square


def early_kernel(chunks, rows, pick_ref, l4_ref, *refs):
    pieces, (square_ref, block) = dict(zip([r for c in chunks for r in (2 * c, 2 * c + 1)], refs[:-2])), refs[-2:]
    square_ref[...] = left_products(chunks, rows, 0, pick_ref, l4_ref, pieces, block)


def early(n, tables, pieces):
    terms, width = tables[0].shape[:2]
    chunks = [c for c in range(n // 2) if c != LAST]
    spare = tables[7].shape[0] // 3
    return pl.pallas_call(
        functools.partial(early_kernel, chunks, width),
        out_shape=(jax.ShapeDtypeStruct((8, width), jnp.float32),
                   pltpu.VMEM((terms * n + 1 + spare, width, width), jnp.float32)),
        in_specs=[SMEM] + [VMEM] * (1 + 2 * len(chunks)),
        out_specs=[VMEM] * 2,
        compiler_params=params(12),
        name="early",
    )(tables[2], tables[0], *(pieces[r] for c in chunks for r in (2 * c, 2 * c + 1)))


def apply_kernel(n, over_rows, rows, start, chunks, pick_ref, mine_ref, first_ref, second_ref, dst_ref, one_ref, two_ref,
                 count_ref, l4_ref, rr_ref, *refs):
    pieces, refs = refs[:n], refs[n:]
    if len(chunks) < n // 2:
        done_ref, refs = refs[0], refs[2:]
    near_ref, far_ref, row_ref, row_far_ref, column_ref, column_far_ref, square_ref, block, total = refs
    terms, width = l4_ref.shape[:2]
    product = jnp.zeros((8, width), jnp.float32)
    block[terms * n] = jnp.zeros((rows, width), jnp.float32)
    square = left_products(chunks, rows, start, pick_ref, l4_ref, pieces, block)
    if len(chunks) < n // 2:
        square = square + done_ref[...]
    square_ref[...] = square

    def add(i, carry):
        block[dst_ref[i]] = block[one_ref[i]] + block[two_ref[i]]
        return carry

    lax.fori_loop(0, count_ref[0], add, 0)
    late = 0
    for low_end in range(0, n, 4):
        for r in range(low_end, low_end + 4):
            for j in range(terms):
                at = j * n + r
                high, low = halves(block[first_ref[at]] + block[second_ref[at]])
                total[r, :, j * width:(j + 1) * width] = high
                total[r, :, (terms + j) * width:(terms + j + 1) * width] = low
        both = jnp.dot(total[low_end:low_end + 4].reshape(4 * rows, 2 * terms * width), rr_ref[...],
                       preferred_element_type=jnp.float32)
        slots = both[:, :width] + both[:, width:]
        for r in range(low_end, low_end + 4):
            slot = slots[(r - low_end) * rows:(r - low_end + 1) * rows]
            product = product + tile_sum(pieces[r][mine_ref[r], start:start + rows, :] * slot)
            g, core = divmod(r, 2)
            if g == 3:
                (column_far_ref if core else column_ref)[...] = slot
            elif g in over_rows:
                at = over_rows.index(g) * rows
                (row_far_ref if core else row_ref)[at:at + rows, :] = slot
            else:
                (far_ref if core else near_ref)[late * rows:(late + 1) * rows, :] = slot
                late += core
    for ref in (far_ref, row_ref, row_far_ref):
        ref[ref.shape[0] - 8:, :] = product


def apply(n, over_rows, rows, start, tables, pieces, done):
    terms, width = tables[0].shape[:2]
    spare = tables[7].shape[0] // 3
    late = n // 2 - 1 - len(over_rows)
    chunks = [LAST] if done else range(n // 2)
    shape = lambda *dims: jax.ShapeDtypeStruct(dims, jnp.float32)
    block = pltpu.VMEM((terms * n + 1 + spare, rows, width), jnp.float32)
    total = pltpu.VMEM((n, rows, 2 * terms * width), jnp.bfloat16)
    if done:
        done = (done[0], pltpu.with_memory_space_constraint(done[1], pltpu.VMEM))
    return pl.pallas_call(
        functools.partial(apply_kernel, n, over_rows, rows, start, chunks),
        out_shape=(shape(late * rows, width), shape(late * rows + 8, width)) + (shape(len(over_rows) * rows + 8, width),) * 2
        + (shape(rows, width),) * 2 + (shape(8, width),) + ((block,) if done else ()),
        in_specs=[SMEM] * 8 + [VMEM] * (2 + n + len(done)),
        out_specs=[VMEM] * (8 if done else 7),
        scratch_shapes=[total] if done else [block, total],
        input_output_aliases={8 + 2 + n + 1: 7} if done else {},
        compiler_params=params(20 if n <= 16 else 56),
        name="apply",
    )(*tables[2:4], *tables[5:], *tables[:2], *pieces, *done)


def joined(parts, count):
    if len(parts) == 1:
        return parts[0]
    height, width = parts[0].shape
    end = height // (8 * count) * 8 * count
    whole = jnp.concatenate([x[:end].reshape(count, -1, width) for x in parts], axis=1).reshape(-1, width)
    return whole if end == height else jnp.concatenate([whole, sum(x[end:] for x in parts)])


def swapped(x, k):
    n = lax.axis_size("term")
    return lax.ppermute(x, "term", [(i, i ^ k) for i in range(n)])


def local(kernel, name, out_shape, scalars, arrays):
    many = isinstance(out_shape, tuple)
    return pl.pallas_call(
        kernel,
        out_shape=out_shape,
        in_specs=[SMEM] * len(scalars) + [VMEM] * len(arrays),
        out_specs=[VMEM] * len(out_shape) if many else VMEM,
        compiler_params=params(16),
        name=name,
    )(*scalars, *arrays)


def fold_kernel(late, over_rows, place_ref, near_ref, far_in, far_ref, row_ref, row_far_ref, column_ref, column_far_ref,
                own_ref, step_ref, *send_refs):
    width = near_ref.shape[1]
    chips = place_ref.shape[0] // SENDERS
    end = len(late) * width
    over = len(over_rows) * width
    tile = far_in[end:] + far_ref[end:] + row_ref[over:] + row_far_ref[over:]
    for i, g in enumerate(late):
        come = [(0, near_ref, i), (1, far_ref, i)]
        if g == 1:
            come += [(4, column_ref, 0), (5, column_far_ref, 0)]
        if g + 1 in over_rows:
            come += [(2, row_ref, over_rows.index(g + 1)), (3, row_far_ref, over_rows.index(g + 1))]
        for b in range(2):
            block = sum(ref[at * width:(at + 1) * width] * (place_ref[q * chips + g] == b).astype(jnp.float32)
                        for q, ref, at in come)
            if g == 0:
                own_ref[b] = block
            elif g == 1:
                step_ref[b] = block
            else:
                send_refs[g // 2 - 1][b * width:(b + 1) * width] = block
    for send_ref in send_refs:
        send_ref[2 * width:] = tile


def landed(own_ref, step_ref, refs):
    width = own_ref.shape[2]
    sent, came = refs[0], refs[1:]
    tile = sent[2 * width:]
    for ref in came:
        tile = tile + ref[2 * width:]
    sums = []
    for b in range(2):
        total = own_ref[b] + step_ref[b]
        for ref in came:
            total = total + ref[b * width:(b + 1) * width]
        sums.append(total)
    return sums, jnp.sum(tile)


def step_kernel(own_ref, step_ref, square_ref, vector_ref, precond_ref, *refs):
    out_ref = refs[-1]
    sigma, product = landed(own_ref, step_ref, refs[:-1])
    theta = product / jnp.sum(square_ref[...])
    for b in range(2):
        v = vector_ref[b]
        out_ref[b] = v - precond_ref[b] * (sigma[b] - theta * v)


def last_kernel(cells, own_ref, step_ref, square_ref, vector_ref, precond_ref, *refs):
    residual_ref, out_ref, tile_ref = refs[-3:]
    sigma, product = landed(own_ref, step_ref, refs[:-3])
    square = jnp.sum(square_ref[...])
    theta = product / square
    scale = 1.0 / jnp.sqrt(square / cells + 1e-06)
    tile = jnp.zeros(tile_ref.shape, jnp.float32)
    for b in range(2):
        v = vector_ref[b]
        residual = (sigma[b] - theta * v) * scale
        residual_ref[b] = residual
        corrected = v * scale - precond_ref[b] * residual
        out_ref[b] = corrected
        tile = tile + tile_sum(corrected * corrected)
    tile_ref[...] = tile


def norm_kernel(cells, corrected_ref, tiles_ref, out_ref):
    scale = 1.0 / jnp.sqrt(jnp.sum(jnp.sum(tiles_ref[...], axis=0)) / cells + 1e-06)
    out_ref[...] = corrected_ref[...] * scale


def scattered(n, tables, pieces, done):
    width = pieces[0].shape[1]
    chips = n // 2
    rows = width if n <= 16 else width // 4
    over_rows = list(range(chips - 1, 3, -2))
    late = [g for g in range(chips) if g != 3 and g not in over_rows]
    shape = lambda *dims: jax.ShapeDtypeStruct(dims, jnp.float32)
    runs = [apply(n, over_rows, rows, start, tables, pieces, done) for start in range(0, width, rows)]
    counts = (len(late), len(late), len(over_rows), len(over_rows), 1, 1)
    near, far, row, row_far, column, column_far = (joined([x[i] for x in runs], k) for i, k in enumerate(counts))
    square = functools.reduce(jnp.add, [x[6] for x in runs])
    own, step, *sends = local(
        functools.partial(fold_kernel, late, over_rows), "fold",
        (shape(2, width, width),) * 2 + (shape(2 * width + 8, width),) * (chips // 2 - 1), tables[4:5],
        (near, far, swapped(far, CORE), swapped(row, ROW), swapped(row_far, ROW + CORE), swapped(column, COLUMN),
         swapped(column_far, COLUMN + CORE)))
    came = [swapped(sends[i], 2 * ROW * (i + 1)) for i in (*range(1, len(sends)), 0)]
    return square, (own, swapped(step, ROW)), [sends[0], *came]


def gathered(n, x, tables, held=None):
    pieces = {0: x}
    for k in reversed(range(8, n, 4)):
        pieces[k] = swapped(x, k)
    if held is not None:
        x, pieces[0] = lax.optimization_barrier((x, held))
    pieces[COLUMN] = swapped(x, COLUMN)
    pieces[ROW] = swapped(x, ROW)
    for k in reversed(range(8, n, 4)):
        pieces[k + ROW] = swapped(pieces[k], ROW)
    pieces[COLUMN + ROW] = swapped(pieces[ROW], COLUMN)
    for k in range(0, n, 2):
        if k != 2 * LAST:
            pieces[k + CORE] = swapped(pieces[k], CORE)
    done = ()
    if n <= 16:
        done = early(n, tables, pieces)
        pieces[2 * LAST], *done = lax.optimization_barrier((pieces[2 * LAST], *done))
    pieces[2 * LAST + CORE] = swapped(pieces[2 * LAST], CORE)
    return [pieces[k] for k in range(n)], done


def shards(wavefn, left_ops, right_ops, precond, fetch_map, store_map, pair_list, live_count):
    n = lax.axis_size("term")
    me = lax.axis_index("term").astype(jnp.int32).reshape(1)
    width = wavefn.shape[1]
    cells = wavefn.size * n
    *tables, held = prep(n, me, fetch_map, store_map, pair_list[0].T.reshape(-1), live_count, wavefn, left_ops, right_ops)
    block = jax.ShapeDtypeStruct(wavefn.shape, jnp.float32)
    tile = jax.ShapeDtypeStruct((8, width), jnp.float32)
    vector = wavefn
    for iteration in range(ITERS):
        pieces, done = gathered(n, vector, tables, held if iteration == 0 else None)
        vector = pieces[0]
        square, sums, parts = scattered(n, tables, pieces, done)
        arrays = (*sums, square, vector, precond, *parts)
        if iteration < ITERS - 1:
            vector = local(step_kernel, "step", block, (), arrays)
    residual, corrected, partial = local(
        functools.partial(last_kernel, cells), "last", (block, block, tile), (), arrays)
    tiles = lax.all_to_all(jnp.broadcast_to(partial[None], (n, 8, width)), "term",
                           split_axis=0, concat_axis=0, tiled=True)
    return local(functools.partial(norm_kernel, cells), "norm", block, (), (corrected, tiles)), residual


def solution(mesh):
    field = P(("group", "term"), None, None)
    return jax.shard_map(
        shards,
        mesh=mesh,
        in_specs=(field, field, field, field, P(), P(), P("term", None, None), P("term")),
        out_specs=(field, field),
        check_vma=False,
    )
```

```python
import functools

import jax
import jax.numpy as jnp
from jax import lax
from jax.experimental import pallas as pl
from jax.experimental.pallas import tpu as pltpu
from jax.sharding import PartitionSpec as P

ITERS = 2
CORE, ROW, COLUMN = 1, 2, 4
SENDERS = 6
SMEM = pl.BlockSpec(memory_space=pltpu.SMEM)
VMEM = pl.BlockSpec(memory_space=pltpu.VMEM)


def params(mebibytes):
    return pltpu.CompilerParams(vmem_limit_bytes=mebibytes * 2**20)


def halves(x):
    high = x.astype(jnp.bfloat16)
    return high, (x - high.astype(jnp.float32)).astype(jnp.bfloat16)


def tile_sum(x):
    return jnp.sum(x.reshape(-1, 8, x.shape[-1]), axis=0)


def prep_kernel(n, spare, me_ref, fetch_in, store_in, pairs_in, live_in, vector_in, left_in, right_in, l4_ref, rr_ref,
                pick_ref, mine_ref, place_ref, first_ref, second_ref, dst_ref, one_ref, two_ref, count_ref, vector_ref,
                seen_ref, fetch_ref, store_ref, pairs_ref, live_ref, left_ref, right_ref, sems):
    copies = [pltpu.make_async_copy(source, target, sems.at[i]) for i, (source, target) in enumerate((
        (fetch_in, fetch_ref), (store_in, store_ref), (pairs_in, pairs_ref), (live_in, live_ref),
        (left_in, left_ref), (right_in, right_ref), (vector_in, vector_ref)))]
    for copy in copies:
        copy.start()
    me = me_ref[0]
    terms = left_ref.shape[0]
    width = left_ref.shape[1]
    zero = terms * n
    npairs = pairs_ref.shape[0] // 3

    def clear(cell, carry):
        first_ref[cell] = zero
        second_ref[cell] = zero
        seen_ref[cell] = 0
        return carry

    lax.fori_loop(0, terms * n, clear, 0, unroll=8)
    for copy in copies[:4]:
        copy.wait()

    def relative(r, carry):
        device = lax.bitwise_xor(me, r)
        pick_ref[r] = fetch_ref[device, me]
        mine_ref[r] = store_ref[me, device]
        return carry

    lax.fori_loop(0, n, relative, 0)

    def chip(g, carry):
        for q in range(SENDERS):
            place_ref[q * (n // 2) + g] = store_ref[lax.bitwise_xor(me, q), lax.bitwise_xor(me, 2 * g)]
        return carry

    lax.fori_loop(0, n // 2, chip, 0)

    def pair(p, carry):
        extra, ops = carry
        a = lax.bitwise_xor(pairs_ref[p], me)
        j = pairs_ref[npairs + p]
        o = lax.bitwise_xor(pairs_ref[2 * npairs + p], me)
        cell = j * n + o
        source = a * terms + j
        seen = seen_ref[cell]
        seen_ref[cell] = seen + 1
        before = second_ref[cell]
        place = jnp.where(seen == 2, spare + extra, before)
        first_ref[cell] = jnp.where(seen == 0, source, first_ref[cell])
        second_ref[cell] = jnp.where(seen == 0, before, jnp.where(seen == 1, source, place))
        dst_ref[ops] = place
        one_ref[ops] = before
        two_ref[ops] = source
        return extra + (seen == 2).astype(jnp.int32), ops + (seen >= 2).astype(jnp.int32)

    _, ops = lax.fori_loop(0, live_ref[0], pair, (jnp.int32(0), jnp.int32(0)))
    count_ref[0] = ops
    for copy in copies[4:]:
        copy.wait()

    for j in range(terms):
        high, low = halves(left_ref[j])
        for k, part in enumerate((high, low, high, low)):
            l4_ref[j, :, k * width:(k + 1) * width] = part
        high, low = halves(right_ref[j])
        for k in range(2):
            row = (k * terms + j) * width
            rr_ref[row:row + width, :width] = high
            rr_ref[row:row + width, width:] = low


def at_home(x):
    return pltpu.with_memory_space_constraint(x, pltpu.HBM)


def prep(n, me, fetch, store, pairs, live, vector, left_ops, right_ops):
    terms, width = left_ops.shape[:2]
    npairs = pairs.shape[0] // 3
    table = jax.ShapeDtypeStruct((terms * n,), jnp.int32)
    listed = jax.ShapeDtypeStruct((npairs,), jnp.int32)
    relative = jax.ShapeDtypeStruct((n,), jnp.int32)
    return pl.pallas_call(
        functools.partial(prep_kernel, n, terms * n + 1),
        out_shape=(
            jax.ShapeDtypeStruct((terms, width, 4 * width), jnp.bfloat16),
            jax.ShapeDtypeStruct((2 * terms * width, 2 * width), jnp.bfloat16),
            relative, relative, jax.ShapeDtypeStruct((SENDERS * n // 2,), jnp.int32), table, table, listed, listed, listed,
            jax.ShapeDtypeStruct((1,), jnp.int32),
            jax.ShapeDtypeStruct(vector.shape, jnp.float32),
        ),
        in_specs=[SMEM] + [pl.BlockSpec(memory_space=pltpu.HBM)] * 7,
        out_specs=[VMEM] * 2 + [SMEM] * 9 + [VMEM],
        scratch_shapes=[
            pltpu.SMEM((terms * n,), jnp.int32),
            pltpu.SMEM(fetch.shape, jnp.int32),
            pltpu.SMEM(store.shape, jnp.int32),
            pltpu.SMEM(pairs.shape, jnp.int32),
            pltpu.SMEM((1,), jnp.int32),
            pltpu.VMEM(left_ops.shape, jnp.float32),
            pltpu.VMEM(left_ops.shape, jnp.float32),
            pltpu.SemaphoreType.DMA((7,)),
        ],
        compiler_params=params(16),
        name="prep",
    )(me, at_home(fetch), at_home(store), at_home(pairs), live, at_home(vector), at_home(left_ops), at_home(right_ops))


def apply_kernel(n, over_rows, rows, start, pick_ref, mine_ref, first_ref, second_ref, dst_ref, one_ref, two_ref, count_ref,
                 l4_ref, rr_ref, *refs):
    pieces, (near_ref, far_ref, row_ref, row_far_ref, column_ref, column_far_ref, square_ref, block, total) = refs[:n], refs[n:]
    terms, width = l4_ref.shape[:2]
    square = jnp.zeros((8, width), jnp.float32)
    product = jnp.zeros((8, width), jnp.float32)
    block[terms * n] = jnp.zeros((rows, width), jnp.float32)
    left = l4_ref[:, start:start + rows, :].reshape(terms * rows, 4 * width)
    for c in range(n // 2):
        columns = []
        for r in (2 * c, 2 * c + 1):
            high, low = halves(pieces[r][pick_ref[r]])
            columns.append(jnp.concatenate([high, high, low, low], axis=0))
            held = pieces[r][:, start:start + rows, :]
            square = square + tile_sum(held * held)
        both = jnp.dot(left, jnp.concatenate(columns, axis=1), preferred_element_type=jnp.float32)
        for k in range(2):
            at = (2 * c + k) * terms
            block[at:at + terms] = both[:, k * width:(k + 1) * width].reshape(terms, rows, width)
    square_ref[...] = square

    def add(i, carry):
        block[dst_ref[i]] = block[one_ref[i]] + block[two_ref[i]]
        return carry

    lax.fori_loop(0, count_ref[0], add, 0)
    late = 0
    for low_end in range(0, n, 4):
        for r in range(low_end, low_end + 4):
            for j in range(terms):
                at = j * n + r
                high, low = halves(block[first_ref[at]] + block[second_ref[at]])
                total[r, :, j * width:(j + 1) * width] = high
                total[r, :, (terms + j) * width:(terms + j + 1) * width] = low
        both = jnp.dot(total[low_end:low_end + 4].reshape(4 * rows, 2 * terms * width), rr_ref[...],
                       preferred_element_type=jnp.float32)
        slots = both[:, :width] + both[:, width:]
        for r in range(low_end, low_end + 4):
            slot = slots[(r - low_end) * rows:(r - low_end + 1) * rows]
            product = product + tile_sum(pieces[r][mine_ref[r], start:start + rows, :] * slot)
            g, core = divmod(r, 2)
            if g == 3:
                (column_far_ref if core else column_ref)[...] = slot
            elif g in over_rows:
                at = over_rows.index(g) * rows
                (row_far_ref if core else row_ref)[at:at + rows, :] = slot
            else:
                (far_ref if core else near_ref)[late * rows:(late + 1) * rows, :] = slot
                late += core
    for ref in (far_ref, row_ref, row_far_ref):
        ref[ref.shape[0] - 8:, :] = product


def apply(n, over_rows, rows, start, tables, pieces):
    terms, width = tables[0].shape[:2]
    spare = tables[7].shape[0] // 3
    late = n // 2 - 1 - len(over_rows)
    shape = lambda *dims: jax.ShapeDtypeStruct(dims, jnp.float32)
    return pl.pallas_call(
        functools.partial(apply_kernel, n, over_rows, rows, start),
        out_shape=(shape(late * rows, width), shape(late * rows + 8, width)) + (shape(len(over_rows) * rows + 8, width),) * 2
        + (shape(rows, width),) * 2 + (shape(8, width),),
        in_specs=[SMEM] * 8 + [VMEM] * (2 + n),
        out_specs=[VMEM] * 7,
        scratch_shapes=[
            pltpu.VMEM((terms * n + 1 + spare, rows, width), jnp.float32),
            pltpu.VMEM((n, rows, 2 * terms * width), jnp.bfloat16),
        ],
        compiler_params=params(32 if n <= 16 else 56),
        name="apply",
    )(*tables[2:4], *tables[5:], *tables[:2], *pieces)


def joined(parts, count):
    if len(parts) == 1:
        return parts[0]
    height, width = parts[0].shape
    end = height // (8 * count) * 8 * count
    whole = jnp.concatenate([x[:end].reshape(count, -1, width) for x in parts], axis=1).reshape(-1, width)
    return whole if end == height else jnp.concatenate([whole, sum(x[end:] for x in parts)])


def swapped(x, k):
    n = lax.axis_size("term")
    return lax.ppermute(x, "term", [(i, i ^ k) for i in range(n)])


def local(kernel, name, out_shape, scalars, arrays):
    many = isinstance(out_shape, tuple)
    return pl.pallas_call(
        kernel,
        out_shape=out_shape,
        in_specs=[SMEM] * len(scalars) + [VMEM] * len(arrays),
        out_specs=[VMEM] * len(out_shape) if many else VMEM,
        compiler_params=params(16),
        name=name,
    )(*scalars, *arrays)


def fold_kernel(late, over_rows, place_ref, near_ref, far_in, far_ref, row_ref, row_far_ref, column_ref, column_far_ref,
                own_ref, step_ref, *send_refs):
    width = near_ref.shape[1]
    chips = place_ref.shape[0] // SENDERS
    end = len(late) * width
    over = len(over_rows) * width
    tile = far_in[end:] + far_ref[end:] + row_ref[over:] + row_far_ref[over:]
    for i, g in enumerate(late):
        come = [(0, near_ref, i), (1, far_ref, i)]
        if g == 1:
            come += [(4, column_ref, 0), (5, column_far_ref, 0)]
        if g + 1 in over_rows:
            come += [(2, row_ref, over_rows.index(g + 1)), (3, row_far_ref, over_rows.index(g + 1))]
        for b in range(2):
            block = sum(ref[at * width:(at + 1) * width] * (place_ref[q * chips + g] == b).astype(jnp.float32)
                        for q, ref, at in come)
            if g == 0:
                own_ref[b] = block
            elif g == 1:
                step_ref[b] = block
            else:
                send_refs[g // 2 - 1][b * width:(b + 1) * width] = block
    for send_ref in send_refs:
        send_ref[2 * width:] = tile


def landed(own_ref, step_ref, refs):
    width = own_ref.shape[2]
    sent, came = refs[0], refs[1:]
    tile = sent[2 * width:]
    for ref in came:
        tile = tile + ref[2 * width:]
    sums = []
    for b in range(2):
        total = own_ref[b] + step_ref[b]
        for ref in came:
            total = total + ref[b * width:(b + 1) * width]
        sums.append(total)
    return sums, jnp.sum(tile)


def step_kernel(own_ref, step_ref, square_ref, vector_ref, precond_ref, *refs):
    out_ref = refs[-1]
    sigma, product = landed(own_ref, step_ref, refs[:-1])
    theta = product / jnp.sum(square_ref[...])
    for b in range(2):
        v = vector_ref[b]
        out_ref[b] = v - precond_ref[b] * (sigma[b] - theta * v)


def last_kernel(cells, own_ref, step_ref, square_ref, vector_ref, precond_ref, *refs):
    residual_ref, out_ref, tile_ref = refs[-3:]
    sigma, product = landed(own_ref, step_ref, refs[:-3])
    square = jnp.sum(square_ref[...])
    theta = product / square
    scale = 1.0 / jnp.sqrt(square / cells + 1e-06)
    tile = jnp.zeros(tile_ref.shape, jnp.float32)
    for b in range(2):
        v = vector_ref[b]
        residual = (sigma[b] - theta * v) * scale
        residual_ref[b] = residual
        corrected = v * scale - precond_ref[b] * residual
        out_ref[b] = corrected
        tile = tile + tile_sum(corrected * corrected)
    tile_ref[...] = tile


def norm_kernel(cells, corrected_ref, tiles_ref, out_ref):
    scale = 1.0 / jnp.sqrt(jnp.sum(jnp.sum(tiles_ref[...], axis=0)) / cells + 1e-06)
    out_ref[...] = corrected_ref[...] * scale


def scattered(n, tables, pieces):
    width = pieces[0].shape[1]
    chips = n // 2
    rows = width if n <= 16 else width // 4
    over_rows = list(range(chips - 1, 3, -2))
    late = [g for g in range(chips) if g != 3 and g not in over_rows]
    shape = lambda *dims: jax.ShapeDtypeStruct(dims, jnp.float32)
    runs = [apply(n, over_rows, rows, start, tables, pieces) for start in range(0, width, rows)]
    counts = (len(late), len(late), len(over_rows), len(over_rows), 1, 1)
    near, far, row, row_far, column, column_far = (joined([x[i] for x in runs], k) for i, k in enumerate(counts))
    square = functools.reduce(jnp.add, [x[6] for x in runs])
    own, step, *sends = local(
        functools.partial(fold_kernel, late, over_rows), "fold",
        (shape(2, width, width),) * 2 + (shape(2 * width + 8, width),) * (chips // 2 - 1), tables[4:5],
        (near, far, swapped(far, CORE), swapped(row, ROW), swapped(row_far, ROW + CORE), swapped(column, COLUMN),
         swapped(column_far, COLUMN + CORE)))
    came = [swapped(sends[i], 2 * ROW * (i + 1)) for i in (*range(1, len(sends)), 0)]
    return square, (own, swapped(step, ROW)), [sends[0], *came]


def gathered(n, x, held=None):
    pieces = {0: x}
    for k in reversed(range(8, n, 4)):
        pieces[k] = swapped(x, k)
    if held is not None:
        x, pieces[0] = lax.optimization_barrier((x, held))
    pieces[COLUMN] = swapped(x, COLUMN)
    pieces[ROW] = swapped(x, ROW)
    for k in reversed(range(8, n, 4)):
        pieces[k + ROW] = swapped(pieces[k], ROW)
    pieces[COLUMN + ROW] = swapped(pieces[ROW], COLUMN)
    for k in range(0, n, 2):
        pieces[k + CORE] = swapped(pieces[k], CORE)
    return [pieces[k] for k in range(n)]


def shards(wavefn, left_ops, right_ops, precond, fetch_map, store_map, pair_list, live_count):
    n = lax.axis_size("term")
    me = lax.axis_index("term").astype(jnp.int32).reshape(1)
    width = wavefn.shape[1]
    cells = wavefn.size * n
    *tables, held = prep(n, me, fetch_map, store_map, pair_list[0].T.reshape(-1), live_count, wavefn, left_ops, right_ops)
    block = jax.ShapeDtypeStruct(wavefn.shape, jnp.float32)
    tile = jax.ShapeDtypeStruct((8, width), jnp.float32)
    vector = wavefn
    for iteration in range(ITERS):
        pieces = gathered(n, vector, held if iteration == 0 else None)
        vector = pieces[0]
        square, sums, parts = scattered(n, tables, pieces)
        arrays = (*sums, square, vector, precond, *parts)
        if iteration < ITERS - 1:
            vector = local(step_kernel, "step", block, (), arrays)
    residual, corrected, partial = local(
        functools.partial(last_kernel, cells), "last", (block, block, tile), (), arrays)
    tiles = lax.all_to_all(jnp.broadcast_to(partial[None], (n, 8, width)), "term",
                           split_axis=0, concat_axis=0, tiled=True)
    return local(functools.partial(norm_kernel, cells), "norm", block, (), (corrected, tiles)), residual


def solution(mesh):
    field = P(("group", "term"), None, None)
    return jax.shard_map(
        shards,
        mesh=mesh,
        in_specs=(field, field, field, field, P(), P(), P("term", None, None), P("term")),
        out_specs=(field, field),
        check_vma=False,
    )
```

```python
import functools

import jax
import jax.numpy as jnp
from jax import lax
from jax.experimental import pallas as pl
from jax.experimental.pallas import tpu as pltpu
from jax.sharding import PartitionSpec as P

ITERS = 2
CORE, ROW, COLUMN = 1, 2, 4
SPLIT = 8
SENDERS = 6
SMEM = pl.BlockSpec(memory_space=pltpu.SMEM)
VMEM = pl.BlockSpec(memory_space=pltpu.VMEM)


def params(mebibytes):
    return pltpu.CompilerParams(vmem_limit_bytes=mebibytes * 2**20)


def halves(x):
    high = x.astype(jnp.bfloat16)
    return high, (x - high.astype(jnp.float32)).astype(jnp.bfloat16)


def tile_sum(x):
    return jnp.sum(x.reshape(-1, 8, x.shape[-1]), axis=0)


def prep_kernel(n, spare, me_ref, fetch_in, store_in, pairs_in, live_in, vector_in, left_in, right_in, l4_ref, rr_ref,
                pick_ref, mine_ref, place_ref, first_ref, second_ref, dst_ref, one_ref, two_ref, count_ref, vector_ref,
                seen_ref, fetch_ref, store_ref, pairs_ref, live_ref, left_ref, right_ref, sems):
    copies = [pltpu.make_async_copy(source, target, sems.at[i]) for i, (source, target) in enumerate((
        (fetch_in, fetch_ref), (store_in, store_ref), (pairs_in, pairs_ref), (live_in, live_ref),
        (left_in, left_ref), (right_in, right_ref), (vector_in, vector_ref)))]
    for copy in copies:
        copy.start()
    me = me_ref[0]
    terms = left_ref.shape[0]
    width = left_ref.shape[1]
    zero = terms * n
    npairs = pairs_ref.shape[0] // 3

    def clear(cell, carry):
        first_ref[cell] = zero
        second_ref[cell] = zero
        seen_ref[cell] = 0
        return carry

    lax.fori_loop(0, terms * n, clear, 0, unroll=8)
    for copy in copies[:4]:
        copy.wait()

    def relative(r, carry):
        device = lax.bitwise_xor(me, r)
        pick_ref[r] = fetch_ref[device, me]
        mine_ref[r] = store_ref[me, device]
        return carry

    lax.fori_loop(0, n, relative, 0)

    def chip(g, carry):
        for q in range(SENDERS):
            place_ref[q * (n // 2) + g] = store_ref[lax.bitwise_xor(me, q), lax.bitwise_xor(me, 2 * g)]
        return carry

    lax.fori_loop(0, n // 2, chip, 0)

    def pair(p, carry):
        extra, ops = carry
        a = lax.bitwise_xor(pairs_ref[p], me)
        j = pairs_ref[npairs + p]
        o = lax.bitwise_xor(pairs_ref[2 * npairs + p], me)
        cell = j * n + o
        source = a * terms + j
        seen = seen_ref[cell]
        seen_ref[cell] = seen + 1
        before = second_ref[cell]
        place = jnp.where(seen == 2, spare + extra, before)
        first_ref[cell] = jnp.where(seen == 0, source, first_ref[cell])
        second_ref[cell] = jnp.where(seen == 0, before, jnp.where(seen == 1, source, place))
        dst_ref[ops] = place
        one_ref[ops] = before
        two_ref[ops] = source
        return extra + (seen == 2).astype(jnp.int32), ops + (seen >= 2).astype(jnp.int32)

    _, ops = lax.fori_loop(0, live_ref[0], pair, (jnp.int32(0), jnp.int32(0)))
    count_ref[0] = ops
    for copy in copies[4:]:
        copy.wait()

    for j in range(terms):
        high, low = halves(left_ref[j])
        for k, part in enumerate((high, low, high, low)):
            l4_ref[j, :, k * width:(k + 1) * width] = part
        high, low = halves(right_ref[j])
        for k in range(2):
            row = (k * terms + j) * width
            rr_ref[row:row + width, :width] = high
            rr_ref[row:row + width, width:] = low


def at_home(x):
    return pltpu.with_memory_space_constraint(x, pltpu.HBM)


def prep(n, me, fetch, store, pairs, live, vector, left_ops, right_ops):
    terms, width = left_ops.shape[:2]
    npairs = pairs.shape[0] // 3
    table = jax.ShapeDtypeStruct((terms * n,), jnp.int32)
    listed = jax.ShapeDtypeStruct((npairs,), jnp.int32)
    relative = jax.ShapeDtypeStruct((n,), jnp.int32)
    return pl.pallas_call(
        functools.partial(prep_kernel, n, terms * n + 1),
        out_shape=(
            jax.ShapeDtypeStruct((terms, width, 4 * width), jnp.bfloat16),
            jax.ShapeDtypeStruct((2 * terms * width, 2 * width), jnp.bfloat16),
            relative, relative, jax.ShapeDtypeStruct((SENDERS * n // 2,), jnp.int32), table, table, listed, listed, listed,
            jax.ShapeDtypeStruct((1,), jnp.int32),
            jax.ShapeDtypeStruct(vector.shape, jnp.float32),
        ),
        in_specs=[SMEM] + [pl.BlockSpec(memory_space=pltpu.HBM)] * 7,
        out_specs=[VMEM] * 2 + [SMEM] * 9 + [VMEM],
        scratch_shapes=[
            pltpu.SMEM((terms * n,), jnp.int32),
            pltpu.SMEM(fetch.shape, jnp.int32),
            pltpu.SMEM(store.shape, jnp.int32),
            pltpu.SMEM(pairs.shape, jnp.int32),
            pltpu.SMEM((1,), jnp.int32),
            pltpu.VMEM(left_ops.shape, jnp.float32),
            pltpu.VMEM(left_ops.shape, jnp.float32),
            pltpu.SemaphoreType.DMA((7,)),
        ],
        compiler_params=params(16),
        name="prep",
    )(me, at_home(fetch), at_home(store), at_home(pairs), live, at_home(vector), at_home(left_ops), at_home(right_ops))


def block_of(refs, which):
    if len(refs) == 1:
        return refs[0][which]
    first = (which == 0).astype(jnp.float32)
    return refs[0][0] * first + refs[1][0] * (1.0 - first)


def apply_kernel(n, over_rows, rows, start, pick_ref, mine_ref, first_ref, second_ref, dst_ref, one_ref, two_ref, count_ref,
                 l4_ref, rr_ref, *refs):
    refs = list(refs)
    pieces, refs = [], refs
    for r in range(n):
        pieces.append([refs.pop(0) for _ in range(2 if SPLIT <= r < SPLIT + 4 else 1)])
    (near_ref, far_ref, row_ref, row_far_ref, column_ref, column_far_ref, square_ref, block, total) = refs
    terms, width = l4_ref.shape[:2]
    square = jnp.zeros((8, width), jnp.float32)
    product = jnp.zeros((8, width), jnp.float32)
    block[terms * n] = jnp.zeros((rows, width), jnp.float32)
    left = l4_ref[:, start:start + rows, :].reshape(terms * rows, 4 * width)
    for c in range(n // 2):
        columns = []
        for r in (2 * c, 2 * c + 1):
            high, low = halves(block_of(pieces[r], pick_ref[r]))
            columns.append(jnp.concatenate([high, high, low, low], axis=0))
            for ref in pieces[r]:
                held = ref[:, start:start + rows, :]
                square = square + tile_sum(held * held)
        both = jnp.dot(left, jnp.concatenate(columns, axis=1), preferred_element_type=jnp.float32)
        for k in range(2):
            at = (2 * c + k) * terms
            block[at:at + terms] = both[:, k * width:(k + 1) * width].reshape(terms, rows, width)
    square_ref[...] = square

    def add(i, carry):
        block[dst_ref[i]] = block[one_ref[i]] + block[two_ref[i]]
        return carry

    lax.fori_loop(0, count_ref[0], add, 0)
    late = 0
    for low_end in range(0, n, 4):
        for r in range(low_end, low_end + 4):
            for j in range(terms):
                at = j * n + r
                high, low = halves(block[first_ref[at]] + block[second_ref[at]])
                total[r, :, j * width:(j + 1) * width] = high
                total[r, :, (terms + j) * width:(terms + j + 1) * width] = low
        both = jnp.dot(total[low_end:low_end + 4].reshape(4 * rows, 2 * terms * width), rr_ref[...],
                       preferred_element_type=jnp.float32)
        slots = both[:, :width] + both[:, width:]
        for r in range(low_end, low_end + 4):
            slot = slots[(r - low_end) * rows:(r - low_end + 1) * rows]
            product = product + tile_sum(block_of(pieces[r], mine_ref[r])[start:start + rows] * slot)
            g, core = divmod(r, 2)
            if g == 3:
                (column_far_ref if core else column_ref)[...] = slot
            elif g in over_rows:
                at = over_rows.index(g) * rows
                (row_far_ref if core else row_ref)[at:at + rows, :] = slot
            else:
                (far_ref if core else near_ref)[late * rows:(late + 1) * rows, :] = slot
                late += core
    for ref in (far_ref, row_ref, row_far_ref):
        ref[ref.shape[0] - 8:, :] = product


def apply(n, over_rows, rows, start, tables, pieces):
    terms, width = tables[0].shape[:2]
    spare = tables[7].shape[0] // 3
    late = n // 2 - 1 - len(over_rows)
    shape = lambda *dims: jax.ShapeDtypeStruct(dims, jnp.float32)
    return pl.pallas_call(
        functools.partial(apply_kernel, n, over_rows, rows, start),
        out_shape=(shape(late * rows, width), shape(late * rows + 8, width)) + (shape(len(over_rows) * rows + 8, width),) * 2
        + (shape(rows, width),) * 2 + (shape(8, width),),
        in_specs=[SMEM] * 8 + [VMEM] * (2 + n + 4),
        out_specs=[VMEM] * 7,
        scratch_shapes=[
            pltpu.VMEM((terms * n + 1 + spare, rows, width), jnp.float32),
            pltpu.VMEM((n, rows, 2 * terms * width), jnp.bfloat16),
        ],
        compiler_params=params(32 if n <= 16 else 56),
        name="apply",
    )(*tables[2:4], *tables[5:], *tables[:2], *(x for piece in pieces for x in piece))


def joined(parts, count):
    if len(parts) == 1:
        return parts[0]
    height, width = parts[0].shape
    end = height // (8 * count) * 8 * count
    whole = jnp.concatenate([x[:end].reshape(count, -1, width) for x in parts], axis=1).reshape(-1, width)
    return whole if end == height else jnp.concatenate([whole, sum(x[end:] for x in parts)])


def swapped(x, k):
    n = lax.axis_size("term")
    return lax.ppermute(x, "term", [(i, i ^ k) for i in range(n)])


def local(kernel, name, out_shape, scalars, arrays):
    many = isinstance(out_shape, tuple)
    return pl.pallas_call(
        kernel,
        out_shape=out_shape,
        in_specs=[SMEM] * len(scalars) + [VMEM] * len(arrays),
        out_specs=[VMEM] * len(out_shape) if many else VMEM,
        compiler_params=params(16),
        name=name,
    )(*scalars, *arrays)


def fold_kernel(late, over_rows, place_ref, near_ref, far_in, far_ref, row_ref, row_far_ref, column_ref, column_far_ref,
                own_ref, step_ref, *send_refs):
    width = near_ref.shape[1]
    chips = place_ref.shape[0] // SENDERS
    end = len(late) * width
    over = len(over_rows) * width
    tile = far_in[end:] + far_ref[end:] + row_ref[over:] + row_far_ref[over:]
    for i, g in enumerate(late):
        come = [(0, near_ref, i), (1, far_ref, i)]
        if g == 1:
            come += [(4, column_ref, 0), (5, column_far_ref, 0)]
        if g + 1 in over_rows:
            come += [(2, row_ref, over_rows.index(g + 1)), (3, row_far_ref, over_rows.index(g + 1))]
        for b in range(2):
            block = sum(ref[at * width:(at + 1) * width] * (place_ref[q * chips + g] == b).astype(jnp.float32)
                        for q, ref, at in come)
            if g == 0:
                own_ref[b] = block
            elif g == 1:
                step_ref[b] = block
            else:
                send_refs[g // 2 - 1][b * width:(b + 1) * width] = block
    for send_ref in send_refs:
        send_ref[2 * width:] = tile


def landed(own_ref, step_ref, refs):
    width = own_ref.shape[2]
    sent, came = refs[0], refs[1:]
    tile = sent[2 * width:]
    for ref in came:
        tile = tile + ref[2 * width:]
    sums = []
    for b in range(2):
        total = own_ref[b] + step_ref[b]
        for ref in came:
            total = total + ref[b * width:(b + 1) * width]
        sums.append(total)
    return sums, jnp.sum(tile)


def step_kernel(own_ref, step_ref, square_ref, vector_ref, precond_ref, *refs):
    out_ref, *half_refs = refs[-3:]
    sigma, product = landed(own_ref, step_ref, refs[:-3])
    theta = product / jnp.sum(square_ref[...])
    for b in range(2):
        v = vector_ref[b]
        corrected = v - precond_ref[b] * (sigma[b] - theta * v)
        out_ref[b] = corrected
        half_refs[b][0] = corrected


def last_kernel(cells, own_ref, step_ref, square_ref, vector_ref, precond_ref, *refs):
    residual_ref, out_ref, tile_ref = refs[-3:]
    sigma, product = landed(own_ref, step_ref, refs[:-3])
    square = jnp.sum(square_ref[...])
    theta = product / square
    scale = 1.0 / jnp.sqrt(square / cells + 1e-06)
    tile = jnp.zeros(tile_ref.shape, jnp.float32)
    for b in range(2):
        v = vector_ref[b]
        residual = (sigma[b] - theta * v) * scale
        residual_ref[b] = residual
        corrected = v * scale - precond_ref[b] * residual
        out_ref[b] = corrected
        tile = tile + tile_sum(corrected * corrected)
    tile_ref[...] = tile


def norm_kernel(cells, corrected_ref, tiles_ref, out_ref):
    scale = 1.0 / jnp.sqrt(jnp.sum(jnp.sum(tiles_ref[...], axis=0)) / cells + 1e-06)
    out_ref[...] = corrected_ref[...] * scale


def scattered(n, tables, pieces):
    width = pieces[0][0].shape[1]
    chips = n // 2
    rows = width if n <= 16 else width // 4
    over_rows = list(range(chips - 1, 3, -2))
    late = [g for g in range(chips) if g != 3 and g not in over_rows]
    shape = lambda *dims: jax.ShapeDtypeStruct(dims, jnp.float32)
    runs = [apply(n, over_rows, rows, start, tables, pieces) for start in range(0, width, rows)]
    counts = (len(late), len(late), len(over_rows), len(over_rows), 1, 1)
    near, far, row, row_far, column, column_far = (joined([x[i] for x in runs], k) for i, k in enumerate(counts))
    square = functools.reduce(jnp.add, [x[6] for x in runs])
    own, step, *sends = local(
        functools.partial(fold_kernel, late, over_rows), "fold",
        (shape(2, width, width),) * 2 + (shape(2 * width + 8, width),) * (chips // 2 - 1), tables[4:5],
        (near, far, swapped(far, CORE), swapped(row, ROW), swapped(row_far, ROW + CORE), swapped(column, COLUMN),
         swapped(column_far, COLUMN + CORE)))
    came = [swapped(sends[i], 2 * ROW * (i + 1)) for i in (*range(1, len(sends)), 0)]
    return square, (own, swapped(step, ROW)), [sends[0], *came]


def gathered(n, x, blocks, held=None):
    def through(arrays, k):
        return [swapped(array, k) for array in arrays]

    pieces = {0: [x]}
    for k in reversed(range(8, n, 4)):
        pieces[k] = through(blocks if k == SPLIT else [x], k)
    pieces[ROW] = through([x], ROW)
    pieces[COLUMN] = through([x], COLUMN)
    if held is not None:
        (pieces[n - 4][0], held) = lax.optimization_barrier((pieces[n - 4][0], held))
        pieces[0] = [held]
    for k in reversed(range(8, n, 4)):
        pieces[k + ROW] = through(pieces[k], ROW)
    pieces[COLUMN + ROW] = through(pieces[ROW], COLUMN)
    for k in range(0, n, 2):
        pieces[k + CORE] = through(pieces[k], CORE)
    return [pieces[k] for k in range(n)]


def shards(wavefn, left_ops, right_ops, precond, fetch_map, store_map, pair_list, live_count):
    n = lax.axis_size("term")
    me = lax.axis_index("term").astype(jnp.int32).reshape(1)
    width = wavefn.shape[1]
    cells = wavefn.size * n
    *tables, held = prep(n, me, fetch_map, store_map, pair_list[0].T.reshape(-1), live_count, wavefn, left_ops, right_ops)
    block = jax.ShapeDtypeStruct(wavefn.shape, jnp.float32)
    tile = jax.ShapeDtypeStruct((8, width), jnp.float32)
    vector = wavefn
    blocks = [wavefn[b:b + 1] for b in range(2)]
    for iteration in range(ITERS):
        pieces = gathered(n, vector, blocks, held if iteration == 0 else None)
        vector = pieces[0][0]
        square, sums, parts = scattered(n, tables, pieces)
        arrays = (*sums, square, vector, precond, *parts)
        if iteration < ITERS - 1:
            half = jax.ShapeDtypeStruct((1, width, width), jnp.float32)
            vector, *blocks = local(step_kernel, "step", (block, half, half), (), arrays)
    residual, corrected, partial = local(
        functools.partial(last_kernel, cells), "last", (block, block, tile), (), arrays)
    tiles = lax.all_to_all(jnp.broadcast_to(partial[None], (n, 8, width)), "term",
                           split_axis=0, concat_axis=0, tiled=True)
    return local(functools.partial(norm_kernel, cells), "norm", block, (), (corrected, tiles)), residual


def solution(mesh):
    field = P(("group", "term"), None, None)
    return jax.shard_map(
        shards,
        mesh=mesh,
        in_specs=(field, field, field, field, P(), P(), P("term", None, None), P("term")),
        out_specs=(field, field),
        check_vma=False,
    )
```

```python
import functools

import jax
import jax.numpy as jnp
from jax import lax
from jax.experimental import pallas as pl
from jax.experimental.pallas import tpu as pltpu
from jax.sharding import PartitionSpec as P

ITERS = 2
CORE, ROW, COLUMN = 1, 2, 4
SENDERS = 6
SMEM = pl.BlockSpec(memory_space=pltpu.SMEM)
VMEM = pl.BlockSpec(memory_space=pltpu.VMEM)


def params(mebibytes):
    return pltpu.CompilerParams(vmem_limit_bytes=mebibytes * 2**20)


def halves(x):
    high = x.astype(jnp.bfloat16)
    return high, (x - high.astype(jnp.float32)).astype(jnp.bfloat16)


def tile_sum(x):
    return jnp.sum(x.reshape(-1, 8, x.shape[-1]), axis=0)


class Part:
    def __init__(self, ref, start):
        self.ref, self.start = ref, start

    def __getitem__(self, i):
        return self.ref[self.start + i]

    def __setitem__(self, i, value):
        self.ref[self.start + i] = value


def lengths(n, terms, npairs):
    return n, n, SENDERS * n // 2, terms * n, terms * n, npairs, npairs, npairs, 1


def parts(ref, n, terms, npairs):
    sizes = lengths(n, terms, npairs)
    return [Part(ref, sum(sizes[:i])) for i in range(len(sizes))]


def prep_kernel(n, spare, me_ref, fetch_in, store_in, pairs_in, live_in, vector_in, left_in, right_in, l4_ref, rr_ref,
                table_ref, vector_ref,
                seen_ref, fetch_ref, store_ref, pairs_ref, live_ref, left_ref, right_ref, sems):
    copies = [pltpu.make_async_copy(source, target, sems.at[i]) for i, (source, target) in enumerate((
        (fetch_in, fetch_ref), (store_in, store_ref), (pairs_in, pairs_ref), (live_in, live_ref),
        (left_in, left_ref), (right_in, right_ref), (vector_in, vector_ref)))]
    for copy in copies:
        copy.start()
    me = me_ref[0]
    terms = left_ref.shape[0]
    width = left_ref.shape[1]
    zero = terms * n
    npairs = pairs_ref.shape[0] // 3
    pick_ref, mine_ref, place_ref, first_ref, second_ref, dst_ref, one_ref, two_ref, count_ref = parts(
        table_ref, n, terms, npairs)

    def clear(cell, carry):
        first_ref[cell] = zero
        second_ref[cell] = zero
        seen_ref[cell] = 0
        return carry

    lax.fori_loop(0, terms * n, clear, 0, unroll=8)
    for copy in copies[:4]:
        copy.wait()

    def relative(r, carry):
        device = lax.bitwise_xor(me, r)
        pick_ref[r] = fetch_ref[device, me]
        mine_ref[r] = store_ref[me, device]
        return carry

    lax.fori_loop(0, n, relative, 0)

    def chip(g, carry):
        for q in range(SENDERS):
            place_ref[q * (n // 2) + g] = store_ref[lax.bitwise_xor(me, q), lax.bitwise_xor(me, 2 * g)]
        return carry

    lax.fori_loop(0, n // 2, chip, 0)

    def pair(p, carry):
        extra, ops = carry
        a = lax.bitwise_xor(pairs_ref[p], me)
        j = pairs_ref[npairs + p]
        o = lax.bitwise_xor(pairs_ref[2 * npairs + p], me)
        cell = j * n + o
        source = a * terms + j
        seen = seen_ref[cell]
        seen_ref[cell] = seen + 1
        before = second_ref[cell]
        place = jnp.where(seen == 2, spare + extra, before)
        first_ref[cell] = jnp.where(seen == 0, source, first_ref[cell])
        second_ref[cell] = jnp.where(seen == 0, before, jnp.where(seen == 1, source, place))
        dst_ref[ops] = place
        one_ref[ops] = before
        two_ref[ops] = source
        return extra + (seen == 2).astype(jnp.int32), ops + (seen >= 2).astype(jnp.int32)

    _, ops = lax.fori_loop(0, live_ref[0], pair, (jnp.int32(0), jnp.int32(0)))
    count_ref[0] = ops
    for copy in copies[4:]:
        copy.wait()

    for j in range(terms):
        high, low = halves(left_ref[j])
        for k, part in enumerate((high, low, high, low)):
            l4_ref[j, :, k * width:(k + 1) * width] = part
        high, low = halves(right_ref[j])
        for k in range(2):
            row = (k * terms + j) * width
            rr_ref[row:row + width, :width] = high
            rr_ref[row:row + width, width:] = low


def at_home(x):
    return pltpu.with_memory_space_constraint(x, pltpu.HBM)


def prep(n, me, fetch, store, pairs, live, vector, left_ops, right_ops):
    terms, width = left_ops.shape[:2]
    npairs = pairs.shape[0] // 3
    return pl.pallas_call(
        functools.partial(prep_kernel, n, terms * n + 1),
        out_shape=(
            jax.ShapeDtypeStruct((terms, width, 4 * width), jnp.bfloat16),
            jax.ShapeDtypeStruct((2 * terms * width, 2 * width), jnp.bfloat16),
            jax.ShapeDtypeStruct((sum(lengths(n, terms, npairs)),), jnp.int32),
            jax.ShapeDtypeStruct(vector.shape, jnp.float32),
        ),
        in_specs=[SMEM] + [pl.BlockSpec(memory_space=pltpu.HBM)] * 7,
        out_specs=[VMEM] * 2 + [SMEM, VMEM],
        scratch_shapes=[
            pltpu.SMEM((terms * n,), jnp.int32),
            pltpu.SMEM(fetch.shape, jnp.int32),
            pltpu.SMEM(store.shape, jnp.int32),
            pltpu.SMEM(pairs.shape, jnp.int32),
            pltpu.SMEM((1,), jnp.int32),
            pltpu.VMEM(left_ops.shape, jnp.float32),
            pltpu.VMEM(left_ops.shape, jnp.float32),
            pltpu.SemaphoreType.DMA((7,)),
        ],
        compiler_params=params(16),
        name="prep",
    )(me, at_home(fetch), at_home(store), at_home(pairs), live, at_home(vector), at_home(left_ops), at_home(right_ops))


def apply_kernel(n, npairs, over_rows, rows, start, table_ref, l4_ref, rr_ref, *refs):
    pieces, (near_ref, far_ref, row_ref, row_far_ref, column_ref, column_far_ref, square_ref, block, total) = refs[:n], refs[n:]
    terms, width = l4_ref.shape[:2]
    pick_ref, mine_ref, _, first_ref, second_ref, dst_ref, one_ref, two_ref, count_ref = parts(table_ref, n, terms, npairs)
    square = jnp.zeros((8, width), jnp.float32)
    product = jnp.zeros((8, width), jnp.float32)
    block[terms * n] = jnp.zeros((rows, width), jnp.float32)
    left = l4_ref[:, start:start + rows, :].reshape(terms * rows, 4 * width)
    for c in range(n // 2):
        columns = []
        for r in (2 * c, 2 * c + 1):
            high, low = halves(pieces[r][pick_ref[r]])
            columns.append(jnp.concatenate([high, high, low, low], axis=0))
            held = pieces[r][:, start:start + rows, :]
            square = square + tile_sum(held * held)
        both = jnp.dot(left, jnp.concatenate(columns, axis=1), preferred_element_type=jnp.float32)
        for k in range(2):
            at = (2 * c + k) * terms
            block[at:at + terms] = both[:, k * width:(k + 1) * width].reshape(terms, rows, width)
    square_ref[...] = square

    def add(i, carry):
        block[dst_ref[i]] = block[one_ref[i]] + block[two_ref[i]]
        return carry

    lax.fori_loop(0, count_ref[0], add, 0)
    late = 0
    for low_end in range(0, n, 4):
        for r in range(low_end, low_end + 4):
            for j in range(terms):
                at = j * n + r
                high, low = halves(block[first_ref[at]] + block[second_ref[at]])
                total[r, :, j * width:(j + 1) * width] = high
                total[r, :, (terms + j) * width:(terms + j + 1) * width] = low
        both = jnp.dot(total[low_end:low_end + 4].reshape(4 * rows, 2 * terms * width), rr_ref[...],
                       preferred_element_type=jnp.float32)
        slots = both[:, :width] + both[:, width:]
        for r in range(low_end, low_end + 4):
            slot = slots[(r - low_end) * rows:(r - low_end + 1) * rows]
            product = product + tile_sum(pieces[r][mine_ref[r], start:start + rows, :] * slot)
            g, core = divmod(r, 2)
            if g == 3:
                (column_far_ref if core else column_ref)[...] = slot
            elif g in over_rows:
                at = over_rows.index(g) * rows
                (row_far_ref if core else row_ref)[at:at + rows, :] = slot
            else:
                (far_ref if core else near_ref)[late * rows:(late + 1) * rows, :] = slot
                late += core
    for ref in (far_ref, row_ref, row_far_ref):
        ref[ref.shape[0] - 8:, :] = product


def apply(n, over_rows, rows, start, tables, pieces):
    terms, width = tables[0].shape[:2]
    npairs = (tables[2].shape[0] - sum(lengths(n, terms, 0))) // 3
    spare = npairs // 3
    late = n // 2 - 1 - len(over_rows)
    shape = lambda *dims: jax.ShapeDtypeStruct(dims, jnp.float32)
    return pl.pallas_call(
        functools.partial(apply_kernel, n, npairs, over_rows, rows, start),
        out_shape=(shape(late * rows, width), shape(late * rows + 8, width)) + (shape(len(over_rows) * rows + 8, width),) * 2
        + (shape(rows, width),) * 2 + (shape(8, width),),
        in_specs=[SMEM] + [VMEM] * (2 + n),
        out_specs=[VMEM] * 7,
        scratch_shapes=[
            pltpu.VMEM((terms * n + 1 + spare, rows, width), jnp.float32),
            pltpu.VMEM((n, rows, 2 * terms * width), jnp.bfloat16),
        ],
        compiler_params=params(32 if n <= 16 else 56),
        name="apply",
    )(tables[2], *tables[:2], *pieces)


def joined(parts, count):
    if len(parts) == 1:
        return parts[0]
    height, width = parts[0].shape
    end = height // (8 * count) * 8 * count
    whole = jnp.concatenate([x[:end].reshape(count, -1, width) for x in parts], axis=1).reshape(-1, width)
    return whole if end == height else jnp.concatenate([whole, sum(x[end:] for x in parts)])


def swapped(x, k):
    n = lax.axis_size("term")
    return lax.ppermute(x, "term", [(i, i ^ k) for i in range(n)])


def local(kernel, name, out_shape, scalars, arrays):
    many = isinstance(out_shape, tuple)
    return pl.pallas_call(
        kernel,
        out_shape=out_shape,
        in_specs=[SMEM] * len(scalars) + [VMEM] * len(arrays),
        out_specs=[VMEM] * len(out_shape) if many else VMEM,
        compiler_params=params(16),
        name=name,
    )(*scalars, *arrays)


def fold_kernel(n, late, over_rows, table_ref, near_ref, far_in, far_ref, row_ref, row_far_ref, column_ref, column_far_ref,
                own_ref, step_ref, *send_refs):
    width = near_ref.shape[1]
    chips = n // 2
    place_ref = Part(table_ref, 2 * n)
    end = len(late) * width
    over = len(over_rows) * width
    tile = far_in[end:] + far_ref[end:] + row_ref[over:] + row_far_ref[over:]
    for i, g in enumerate(late):
        come = [(0, near_ref, i), (1, far_ref, i)]
        if g == 1:
            come += [(4, column_ref, 0), (5, column_far_ref, 0)]
        if g + 1 in over_rows:
            come += [(2, row_ref, over_rows.index(g + 1)), (3, row_far_ref, over_rows.index(g + 1))]
        for b in range(2):
            block = sum(ref[at * width:(at + 1) * width] * (place_ref[q * chips + g] == b).astype(jnp.float32)
                        for q, ref, at in come)
            if g == 0:
                own_ref[b] = block
            elif g == 1:
                step_ref[b] = block
            else:
                send_refs[g // 2 - 1][b * width:(b + 1) * width] = block
    for send_ref in send_refs:
        send_ref[2 * width:] = tile


def landed(own_ref, step_ref, refs):
    width = own_ref.shape[2]
    sent, came = refs[0], refs[1:]
    tile = sent[2 * width:]
    for ref in came:
        tile = tile + ref[2 * width:]
    sums = []
    for b in range(2):
        total = own_ref[b] + step_ref[b]
        for ref in came:
            total = total + ref[b * width:(b + 1) * width]
        sums.append(total)
    return sums, jnp.sum(tile)


def step_kernel(own_ref, step_ref, square_ref, vector_ref, precond_ref, *refs):
    out_ref = refs[-1]
    sigma, product = landed(own_ref, step_ref, refs[:-1])
    theta = product / jnp.sum(square_ref[...])
    for b in range(2):
        v = vector_ref[b]
        out_ref[b] = v - precond_ref[b] * (sigma[b] - theta * v)


def last_kernel(cells, own_ref, step_ref, square_ref, vector_ref, precond_ref, *refs):
    residual_ref, out_ref, tile_ref = refs[-3:]
    sigma, product = landed(own_ref, step_ref, refs[:-3])
    square = jnp.sum(square_ref[...])
    theta = product / square
    scale = 1.0 / jnp.sqrt(square / cells + 1e-06)
    tile = jnp.zeros(tile_ref.shape, jnp.float32)
    for b in range(2):
        v = vector_ref[b]
        residual = (sigma[b] - theta * v) * scale
        residual_ref[b] = residual
        corrected = v * scale - precond_ref[b] * residual
        out_ref[b] = corrected
        tile = tile + tile_sum(corrected * corrected)
    tile_ref[...] = tile


def norm_kernel(cells, corrected_ref, tiles_ref, out_ref):
    scale = 1.0 / jnp.sqrt(jnp.sum(jnp.sum(tiles_ref[...], axis=0)) / cells + 1e-06)
    out_ref[...] = corrected_ref[...] * scale


def scattered(n, tables, pieces):
    width = pieces[0].shape[1]
    chips = n // 2
    rows = width if n <= 16 else width // 4
    over_rows = list(range(chips - 1, 3, -2))
    late = [g for g in range(chips) if g != 3 and g not in over_rows]
    shape = lambda *dims: jax.ShapeDtypeStruct(dims, jnp.float32)
    runs = [apply(n, over_rows, rows, start, tables, pieces) for start in range(0, width, rows)]
    counts = (len(late), len(late), len(over_rows), len(over_rows), 1, 1)
    near, far, row, row_far, column, column_far = (joined([x[i] for x in runs], k) for i, k in enumerate(counts))
    square = functools.reduce(jnp.add, [x[6] for x in runs])
    own, step, *sends = local(
        functools.partial(fold_kernel, n, late, over_rows), "fold",
        (shape(2, width, width),) * 2 + (shape(2 * width + 8, width),) * (chips // 2 - 1), tables[2:3],
        (near, far, swapped(far, CORE), swapped(row, ROW), swapped(row_far, ROW + CORE), swapped(column, COLUMN),
         swapped(column_far, COLUMN + CORE)))
    came = [swapped(sends[i], 2 * ROW * (i + 1)) for i in (*range(1, len(sends)), 0)]
    return square, (own, swapped(step, ROW)), [sends[0], *came]


def gathered(n, x, held=None):
    pieces = {0: x}
    for k in reversed(range(8, n, 4)):
        pieces[k] = swapped(x, k)
    pieces[ROW] = swapped(x, ROW)
    pieces[COLUMN] = swapped(x, COLUMN)
    if held is not None:
        pieces[COLUMN], pieces[0] = lax.optimization_barrier((pieces[COLUMN], held))
    for k in reversed(range(8, n, 4)):
        pieces[k + ROW] = swapped(pieces[k], ROW)
    pieces[COLUMN + ROW] = swapped(pieces[ROW], COLUMN)
    for k in range(0, n, 2):
        pieces[k + CORE] = swapped(pieces[k], CORE)
    return [pieces[k] for k in range(n)]


def shards(wavefn, left_ops, right_ops, precond, fetch_map, store_map, pair_list, live_count):
    n = lax.axis_size("term")
    me = lax.axis_index("term").astype(jnp.int32).reshape(1)
    width = wavefn.shape[1]
    cells = wavefn.size * n
    *tables, held = prep(n, me, fetch_map, store_map, pair_list[0].T.reshape(-1), live_count, wavefn, left_ops, right_ops)
    block = jax.ShapeDtypeStruct(wavefn.shape, jnp.float32)
    tile = jax.ShapeDtypeStruct((8, width), jnp.float32)
    vector = wavefn
    for iteration in range(ITERS):
        pieces = gathered(n, vector, held if iteration == 0 else None)
        vector = pieces[0]
        square, sums, parts = scattered(n, tables, pieces)
        arrays = (*sums, square, vector, precond, *parts)
        if iteration < ITERS - 1:
            vector = local(step_kernel, "step", block, (), arrays)
    residual, corrected, partial = local(
        functools.partial(last_kernel, cells), "last", (block, block, tile), (), arrays)
    tiles = lax.all_to_all(jnp.broadcast_to(partial[None], (n, 8, width)), "term",
                           split_axis=0, concat_axis=0, tiled=True)
    return local(functools.partial(norm_kernel, cells), "norm", block, (), (corrected, tiles)), residual


def solution(mesh):
    field = P(("group", "term"), None, None)
    return jax.shard_map(
        shards,
        mesh=mesh,
        in_specs=(field, field, field, field, P(), P(), P("term", None, None), P("term")),
        out_specs=(field, field),
        check_vma=False,
    )
```

```python
import functools

import jax
import jax.numpy as jnp
from jax import lax
from jax.experimental import pallas as pl
from jax.experimental.pallas import tpu as pltpu
from jax.sharding import PartitionSpec as P

ITERS = 2
CORE, ROW, COLUMN = 1, 2, 4
SENDERS = 6
SMEM = pl.BlockSpec(memory_space=pltpu.SMEM)
VMEM = pl.BlockSpec(memory_space=pltpu.VMEM)


def params(mebibytes):
    return pltpu.CompilerParams(vmem_limit_bytes=mebibytes * 2**20)


def halves(x):
    high = x.astype(jnp.bfloat16)
    return high, (x - high.astype(jnp.float32)).astype(jnp.bfloat16)


def tile_sum(x):
    return jnp.sum(x.reshape(-1, 8, x.shape[-1]), axis=0)


class Part:
    def __init__(self, ref, start):
        self.ref, self.start = ref, start

    def __getitem__(self, i):
        return self.ref[self.start + i]

    def __setitem__(self, i, value):
        self.ref[self.start + i] = value


def lengths(n, terms, npairs):
    return n, n, SENDERS * n // 2, terms * n, terms * n, npairs, npairs, npairs, 1


def parts(ref, n, terms, npairs):
    sizes = lengths(n, terms, npairs)
    return [Part(ref, sum(sizes[:i])) for i in range(len(sizes))]


def prep_kernel(n, spare, me_ref, fetch_in, store_in, pairs_in, live_in, vector_in, left_in, right_in, l4_ref, rr_ref,
                table_ref, vector_ref,
                seen_ref, fetch_ref, store_ref, pairs_ref, live_ref, left_ref, right_ref, sems):
    copies = [pltpu.make_async_copy(source, target, sems.at[i]) for i, (source, target) in enumerate((
        (fetch_in, fetch_ref), (store_in, store_ref), (pairs_in, pairs_ref), (live_in, live_ref),
        (left_in, left_ref), (right_in, right_ref), (vector_in, vector_ref)))]
    for copy in copies:
        copy.start()
    me = me_ref[0]
    terms = left_ref.shape[0]
    width = left_ref.shape[1]
    zero = terms * n
    npairs = pairs_ref.shape[0] // 3
    pick_ref, mine_ref, place_ref, first_ref, second_ref, dst_ref, one_ref, two_ref, count_ref = parts(
        table_ref, n, terms, npairs)

    def clear(cell, carry):
        first_ref[cell] = zero
        second_ref[cell] = zero
        seen_ref[cell] = 0
        return carry

    lax.fori_loop(0, terms * n, clear, 0, unroll=8)
    for copy in copies[:4]:
        copy.wait()

    def relative(r, carry):
        device = lax.bitwise_xor(me, r)
        pick_ref[r] = fetch_ref[device, me]
        mine_ref[r] = store_ref[me, device]
        return carry

    lax.fori_loop(0, n, relative, 0)

    def chip(g, carry):
        for q in range(SENDERS):
            place_ref[q * (n // 2) + g] = store_ref[lax.bitwise_xor(me, q), lax.bitwise_xor(me, 2 * g)]
        return carry

    lax.fori_loop(0, n // 2, chip, 0)

    def pair(p, carry):
        extra, ops = carry
        a = lax.bitwise_xor(pairs_ref[p], me)
        j = pairs_ref[npairs + p]
        o = lax.bitwise_xor(pairs_ref[2 * npairs + p], me)
        cell = j * n + o
        source = a * terms + j
        seen = seen_ref[cell]
        seen_ref[cell] = seen + 1
        before = second_ref[cell]
        place = jnp.where(seen == 2, spare + extra, before)
        first_ref[cell] = jnp.where(seen == 0, source, first_ref[cell])
        second_ref[cell] = jnp.where(seen == 0, before, jnp.where(seen == 1, source, place))
        dst_ref[ops] = place
        one_ref[ops] = before
        two_ref[ops] = source
        return extra + (seen == 2).astype(jnp.int32), ops + (seen >= 2).astype(jnp.int32)

    _, ops = lax.fori_loop(0, live_ref[0], pair, (jnp.int32(0), jnp.int32(0)))
    count_ref[0] = ops
    for copy in copies[4:]:
        copy.wait()

    for j in range(terms):
        high, low = halves(left_ref[j])
        for k, part in enumerate((high, low, high, low)):
            l4_ref[j, :, k * width:(k + 1) * width] = part
        high, low = halves(right_ref[j])
        for k in range(2):
            row = (k * terms + j) * width
            rr_ref[row:row + width, :width] = high
            rr_ref[row:row + width, width:] = low


def at_home(x):
    return pltpu.with_memory_space_constraint(x, pltpu.HBM)


def prep(n, me, fetch, store, pairs, live, vector, left_ops, right_ops):
    terms, width = left_ops.shape[:2]
    npairs = pairs.shape[0] // 3
    return pl.pallas_call(
        functools.partial(prep_kernel, n, terms * n + 1),
        out_shape=(
            jax.ShapeDtypeStruct((terms, width, 4 * width), jnp.bfloat16),
            jax.ShapeDtypeStruct((2 * terms * width, 2 * width), jnp.bfloat16),
            jax.ShapeDtypeStruct((sum(lengths(n, terms, npairs)),), jnp.int32),
            jax.ShapeDtypeStruct(vector.shape, jnp.float32),
        ),
        in_specs=[SMEM] + [pl.BlockSpec(memory_space=pltpu.HBM)] * 7,
        out_specs=[VMEM] * 2 + [SMEM, VMEM],
        scratch_shapes=[
            pltpu.SMEM((terms * n,), jnp.int32),
            pltpu.SMEM(fetch.shape, jnp.int32),
            pltpu.SMEM(store.shape, jnp.int32),
            pltpu.SMEM(pairs.shape, jnp.int32),
            pltpu.SMEM((1,), jnp.int32),
            pltpu.VMEM(left_ops.shape, jnp.float32),
            pltpu.VMEM(left_ops.shape, jnp.float32),
            pltpu.SemaphoreType.DMA((7,)),
        ],
        compiler_params=params(16),
        name="prep",
    )(me, at_home(fetch), at_home(store), at_home(pairs), live, at_home(vector), at_home(left_ops), at_home(right_ops))


def apply_kernel(n, npairs, over_rows, rows, start, table_ref, l4_ref, rr_ref, *refs):
    pieces, (near_ref, far_ref, row_ref, row_far_ref, column_ref, column_far_ref, square_ref, block, total) = refs[:n], refs[n:]
    terms, width = l4_ref.shape[:2]
    pick_ref, mine_ref, _, first_ref, second_ref, dst_ref, one_ref, two_ref, count_ref = parts(table_ref, n, terms, npairs)
    square = jnp.zeros((8, width), jnp.float32)
    product = jnp.zeros((8, width), jnp.float32)
    block[terms * n] = jnp.zeros((rows, width), jnp.float32)
    left = l4_ref[:, start:start + rows, :].reshape(terms * rows, 4 * width)
    for c in range(n // 2):
        columns = []
        for r in (2 * c, 2 * c + 1):
            high, low = halves(pieces[r][pick_ref[r]])
            columns.append(jnp.concatenate([high, high, low, low], axis=0))
            held = pieces[r][:, start:start + rows, :]
            square = square + tile_sum(held * held)
        both = jnp.dot(left, jnp.concatenate(columns, axis=1), preferred_element_type=jnp.float32)
        for k in range(2):
            at = (2 * c + k) * terms
            block[at:at + terms] = both[:, k * width:(k + 1) * width].reshape(terms, rows, width)
    square_ref[...] = square

    def add(i, carry):
        block[dst_ref[i]] = block[one_ref[i]] + block[two_ref[i]]
        return carry

    lax.fori_loop(0, count_ref[0], add, 0)
    late = 0
    for low_end in range(0, n, 4):
        for r in range(low_end, low_end + 4):
            for j in range(terms):
                at = j * n + r
                high, low = halves(block[first_ref[at]] + block[second_ref[at]])
                total[r, :, j * width:(j + 1) * width] = high
                total[r, :, (terms + j) * width:(terms + j + 1) * width] = low
        both = jnp.dot(total[low_end:low_end + 4].reshape(4 * rows, 2 * terms * width), rr_ref[...],
                       preferred_element_type=jnp.float32)
        slots = both[:, :width] + both[:, width:]
        for r in range(low_end, low_end + 4):
            slot = slots[(r - low_end) * rows:(r - low_end + 1) * rows]
            product = product + tile_sum(pieces[r][mine_ref[r], start:start + rows, :] * slot)
            g, core = divmod(r, 2)
            if g == 3:
                (column_far_ref if core else column_ref)[...] = slot
            elif g in over_rows:
                at = over_rows.index(g) * rows
                (row_far_ref if core else row_ref)[at:at + rows, :] = slot
            else:
                (far_ref if core else near_ref)[late * rows:(late + 1) * rows, :] = slot
                late += core
    for ref in (far_ref, row_ref, row_far_ref):
        ref[ref.shape[0] - 8:, :] = product


def apply(n, over_rows, rows, start, tables, pieces):
    terms, width = tables[0].shape[:2]
    npairs = (tables[2].shape[0] - sum(lengths(n, terms, 0))) // 3
    spare = npairs // 3
    late = n // 2 - 1 - len(over_rows)
    shape = lambda *dims: jax.ShapeDtypeStruct(dims, jnp.float32)
    return pl.pallas_call(
        functools.partial(apply_kernel, n, npairs, over_rows, rows, start),
        out_shape=(shape(late * rows, width), shape(late * rows + 8, width)) + (shape(len(over_rows) * rows + 8, width),) * 2
        + (shape(rows, width),) * 2 + (shape(8, width),),
        in_specs=[SMEM] + [VMEM] * (2 + n),
        out_specs=[VMEM] * 7,
        scratch_shapes=[
            pltpu.VMEM((terms * n + 1 + spare, rows, width), jnp.float32),
            pltpu.VMEM((n, rows, 2 * terms * width), jnp.bfloat16),
        ],
        compiler_params=params(32 if n <= 16 else 56),
        name="apply",
    )(tables[2], *tables[:2], *pieces)


def joined(parts, count):
    if len(parts) == 1:
        return parts[0]
    height, width = parts[0].shape
    end = height // (8 * count) * 8 * count
    whole = jnp.concatenate([x[:end].reshape(count, -1, width) for x in parts], axis=1).reshape(-1, width)
    return whole if end == height else jnp.concatenate([whole, sum(x[end:] for x in parts)])


def swapped(x, k):
    n = lax.axis_size("term")
    return lax.ppermute(x, "term", [(i, i ^ k) for i in range(n)])


def local(kernel, name, out_shape, scalars, arrays):
    many = isinstance(out_shape, tuple)
    return pl.pallas_call(
        kernel,
        out_shape=out_shape,
        in_specs=[SMEM] * len(scalars) + [VMEM] * len(arrays),
        out_specs=[VMEM] * len(out_shape) if many else VMEM,
        compiler_params=params(16),
        name=name,
    )(*scalars, *arrays)


def fold_kernel(n, late, over_rows, table_ref, near_ref, far_in, far_ref, row_ref, row_far_ref, column_ref, column_far_ref,
                own_ref, step_ref, *send_refs):
    width = near_ref.shape[1]
    chips = n // 2
    place_ref = Part(table_ref, 2 * n)
    end = len(late) * width
    over = len(over_rows) * width
    tile = far_in[end:] + far_ref[end:] + row_ref[over:] + row_far_ref[over:]
    for i, g in enumerate(late):
        come = [(0, near_ref, i), (1, far_ref, i)]
        if g == 1:
            come += [(4, column_ref, 0), (5, column_far_ref, 0)]
        if g + 1 in over_rows:
            come += [(2, row_ref, over_rows.index(g + 1)), (3, row_far_ref, over_rows.index(g + 1))]
        for b in range(2):
            block = sum(ref[at * width:(at + 1) * width] * (place_ref[q * chips + g] == b).astype(jnp.float32)
                        for q, ref, at in come)
            if g == 0:
                own_ref[b] = block
            elif g == 1:
                step_ref[b] = block
            else:
                send_refs[g // 2 - 1][b * width:(b + 1) * width] = block
    for send_ref in send_refs:
        send_ref[2 * width:] = tile


def landed(own_ref, step_ref, refs):
    width = own_ref.shape[2]
    sent, came = refs[0], refs[1:]
    tile = sent[2 * width:]
    for ref in came:
        tile = tile + ref[2 * width:]
    sums = []
    for b in range(2):
        total = own_ref[b] + step_ref[b]
        for ref in came:
            total = total + ref[b * width:(b + 1) * width]
        sums.append(total)
    return sums, jnp.sum(tile)


def step_kernel(own_ref, step_ref, square_ref, vector_ref, precond_ref, *refs):
    out_ref = refs[-1]
    sigma, product = landed(own_ref, step_ref, refs[:-1])
    theta = product / jnp.sum(square_ref[...])
    for b in range(2):
        v = vector_ref[b]
        out_ref[b] = v - precond_ref[b] * (sigma[b] - theta * v)


def last_kernel(cells, own_ref, step_ref, square_ref, vector_ref, precond_ref, *refs):
    residual_ref, out_ref, tile_ref = refs[-3:]
    sigma, product = landed(own_ref, step_ref, refs[:-3])
    square = jnp.sum(square_ref[...])
    theta = product / square
    scale = 1.0 / jnp.sqrt(square / cells + 1e-06)
    tile = jnp.zeros(tile_ref.shape, jnp.float32)
    for b in range(2):
        v = vector_ref[b]
        residual = (sigma[b] - theta * v) * scale
        residual_ref[b] = residual
        corrected = v * scale - precond_ref[b] * residual
        out_ref[b] = corrected
        tile = tile + tile_sum(corrected * corrected)
    tile_ref[...] = tile


def norm_kernel(cells, corrected_ref, tiles_ref, out_ref):
    scale = 1.0 / jnp.sqrt(jnp.sum(jnp.sum(tiles_ref[...], axis=0)) / cells + 1e-06)
    out_ref[...] = corrected_ref[...] * scale


def scattered(n, tables, pieces, last):
    width = pieces[0].shape[1]
    chips = n // 2
    rows = width if n <= 16 else width // 4
    over_rows = list(range(chips - 1, 3, -2))
    late = [g for g in range(chips) if g != 3 and g not in over_rows]
    shape = lambda *dims: jax.ShapeDtypeStruct(dims, jnp.float32)
    runs = [apply(n, over_rows, rows, start, tables, pieces) for start in range(0, width, rows)]
    counts = (len(late), len(late), len(over_rows), len(over_rows), 1, 1)
    near, far, row, row_far, column, column_far = (joined([x[i] for x in runs], k) for i, k in enumerate(counts))
    square = functools.reduce(jnp.add, [x[6] for x in runs])
    own, step, *sends = local(
        functools.partial(fold_kernel, n, late, over_rows), "fold",
        (shape(2, width, width),) * 2 + (shape(2 * width + 8, width),) * (chips // 2 - 1), tables[2:3],
        (near, far, swapped(far, CORE), swapped(row, ROW), swapped(row_far, ROW + CORE), swapped(column, COLUMN),
         swapped(column_far, COLUMN + CORE)))
    order = range(len(sends))
    came = [swapped(sends[i], 2 * ROW * (i + 1)) for i in ((*order[1:], 0) if last else order[::-1])]
    return square, (own, swapped(step, ROW)), [sends[0], *came]


def gathered(n, x, held=None):
    pieces = {0: x}
    for k in reversed(range(8, n, 4)):
        pieces[k] = swapped(x, k)
    pieces[ROW] = swapped(x, ROW)
    pieces[COLUMN] = swapped(x, COLUMN)
    for k in reversed(range(8, n, 4)):
        pieces[k + ROW] = swapped(pieces[k], ROW)
    pieces[COLUMN + ROW] = swapped(pieces[ROW], COLUMN)
    if held is not None:
        pieces[n - 4 + ROW], pieces[0] = lax.optimization_barrier((pieces[n - 4 + ROW], held))
    for k in range(0, n, 2):
        pieces[k + CORE] = swapped(pieces[k], CORE)
    return [pieces[k] for k in range(n)]


def shards(wavefn, left_ops, right_ops, precond, fetch_map, store_map, pair_list, live_count):
    n = lax.axis_size("term")
    me = lax.axis_index("term").astype(jnp.int32).reshape(1)
    width = wavefn.shape[1]
    cells = wavefn.size * n
    *tables, held = prep(n, me, fetch_map, store_map, pair_list[0].T.reshape(-1), live_count, wavefn, left_ops, right_ops)
    block = jax.ShapeDtypeStruct(wavefn.shape, jnp.float32)
    tile = jax.ShapeDtypeStruct((8, width), jnp.float32)
    vector = wavefn
    for iteration in range(ITERS):
        pieces = gathered(n, vector, held if iteration == 0 else None)
        vector = pieces[0]
        square, sums, parts = scattered(n, tables, pieces, iteration == ITERS - 1)
        arrays = (*sums, square, vector, precond, *parts)
        if iteration < ITERS - 1:
            vector = local(step_kernel, "step", block, (), arrays)
    residual, corrected, partial = local(
        functools.partial(last_kernel, cells), "last", (block, block, tile), (), arrays)
    tiles = lax.all_to_all(jnp.broadcast_to(partial[None], (n, 8, width)), "term",
                           split_axis=0, concat_axis=0, tiled=True)
    return local(functools.partial(norm_kernel, cells), "norm", block, (), (corrected, tiles)), residual


def solution(mesh):
    field = P(("group", "term"), None, None)
    return jax.shard_map(
        shards,
        mesh=mesh,
        in_specs=(field, field, field, field, P(), P(), P("term", None, None), P("term")),
        out_specs=(field, field),
        check_vma=False,
    )
```

```python
import functools

import jax
import jax.numpy as jnp
from jax import lax
from jax.experimental import pallas as pl
from jax.experimental.pallas import tpu as pltpu
from jax.sharding import PartitionSpec as P

ITERS = 2
CORE, ROW, COLUMN = 1, 2, 4
SENDERS = 6
SMEM = pl.BlockSpec(memory_space=pltpu.SMEM)
VMEM = pl.BlockSpec(memory_space=pltpu.VMEM)


def params(mebibytes):
    return pltpu.CompilerParams(vmem_limit_bytes=mebibytes * 2**20)


def halves(x):
    high = x.astype(jnp.bfloat16)
    return high, (x - high.astype(jnp.float32)).astype(jnp.bfloat16)


def tile_sum(x):
    return jnp.sum(x.reshape(-1, 8, x.shape[-1]), axis=0)


class Part:
    def __init__(self, ref, start):
        self.ref, self.start = ref, start

    def __getitem__(self, i):
        return self.ref[self.start + i]

    def __setitem__(self, i, value):
        self.ref[self.start + i] = value


def lengths(n, terms, npairs):
    return n, n, SENDERS * n // 2, terms * n, terms * n, npairs, npairs, npairs, 1


def parts(ref, n, terms, npairs):
    sizes = lengths(n, terms, npairs)
    return [Part(ref, sum(sizes[:i])) for i in range(len(sizes))]


def prep_kernel(n, spare, me_ref, fetch_in, store_in, pairs_in, live_in, vector_in, left_in, right_in, l4_ref, rr_ref,
                table_ref, vector_ref,
                seen_ref, fetch_ref, store_ref, pairs_ref, live_ref, left_ref, right_ref, sems):
    copies = [pltpu.make_async_copy(source, target, sems.at[i]) for i, (source, target) in enumerate((
        (fetch_in, fetch_ref), (store_in, store_ref), (pairs_in, pairs_ref), (live_in, live_ref),
        (left_in, left_ref), (right_in, right_ref), (vector_in, vector_ref)))]
    for copy in copies:
        copy.start()
    me = me_ref[0]
    terms = left_ref.shape[0]
    width = left_ref.shape[1]
    zero = terms * n
    npairs = pairs_ref.shape[0] // 3
    pick_ref, mine_ref, place_ref, first_ref, second_ref, dst_ref, one_ref, two_ref, count_ref = parts(
        table_ref, n, terms, npairs)

    def clear(cell, carry):
        first_ref[cell] = zero
        second_ref[cell] = zero
        seen_ref[cell] = 0
        return carry

    lax.fori_loop(0, terms * n, clear, 0, unroll=8)
    for copy in copies[:4]:
        copy.wait()

    def relative(r, carry):
        device = lax.bitwise_xor(me, r)
        pick_ref[r] = fetch_ref[device, me]
        mine_ref[r] = store_ref[me, device]
        return carry

    lax.fori_loop(0, n, relative, 0)

    def chip(g, carry):
        for q in range(SENDERS):
            place_ref[q * (n // 2) + g] = store_ref[lax.bitwise_xor(me, q), lax.bitwise_xor(me, 2 * g)]
        return carry

    lax.fori_loop(0, n // 2, chip, 0)

    def pair(p, carry):
        extra, ops = carry
        a = lax.bitwise_xor(pairs_ref[p], me)
        j = pairs_ref[npairs + p]
        o = lax.bitwise_xor(pairs_ref[2 * npairs + p], me)
        cell = j * n + o
        source = a * terms + j
        seen = seen_ref[cell]
        seen_ref[cell] = seen + 1
        before = second_ref[cell]
        place = jnp.where(seen == 2, spare + extra, before)
        first_ref[cell] = jnp.where(seen == 0, source, first_ref[cell])
        second_ref[cell] = jnp.where(seen == 0, before, jnp.where(seen == 1, source, place))
        dst_ref[ops] = place
        one_ref[ops] = before
        two_ref[ops] = source
        return extra + (seen == 2).astype(jnp.int32), ops + (seen >= 2).astype(jnp.int32)

    _, ops = lax.fori_loop(0, live_ref[0], pair, (jnp.int32(0), jnp.int32(0)))
    count_ref[0] = ops
    for copy in copies[4:]:
        copy.wait()

    for j in range(terms):
        high, low = halves(left_ref[j])
        for k, part in enumerate((high, low, high, low)):
            l4_ref[j, :, k * width:(k + 1) * width] = part
        high, low = halves(right_ref[j])
        for k in range(2):
            row = (k * terms + j) * width
            rr_ref[row:row + width, :width] = high
            rr_ref[row:row + width, width:] = low


def at_home(x):
    return pltpu.with_memory_space_constraint(x, pltpu.HBM)


def prep(n, me, fetch, store, pairs, live, vector, left_ops, right_ops):
    terms, width = left_ops.shape[:2]
    npairs = pairs.shape[0] // 3
    return pl.pallas_call(
        functools.partial(prep_kernel, n, terms * n + 1),
        out_shape=(
            jax.ShapeDtypeStruct((terms, width, 4 * width), jnp.bfloat16),
            jax.ShapeDtypeStruct((2 * terms * width, 2 * width), jnp.bfloat16),
            jax.ShapeDtypeStruct((sum(lengths(n, terms, npairs)),), jnp.int32),
            jax.ShapeDtypeStruct(vector.shape, jnp.float32),
        ),
        in_specs=[SMEM] + [pl.BlockSpec(memory_space=pltpu.HBM)] * 7,
        out_specs=[VMEM] * 2 + [SMEM, VMEM],
        scratch_shapes=[
            pltpu.SMEM((terms * n,), jnp.int32),
            pltpu.SMEM(fetch.shape, jnp.int32),
            pltpu.SMEM(store.shape, jnp.int32),
            pltpu.SMEM(pairs.shape, jnp.int32),
            pltpu.SMEM((1,), jnp.int32),
            pltpu.VMEM(left_ops.shape, jnp.float32),
            pltpu.VMEM(left_ops.shape, jnp.float32),
            pltpu.SemaphoreType.DMA((7,)),
        ],
        compiler_params=params(16),
        name="prep",
    )(me, at_home(fetch), at_home(store), at_home(pairs), live, at_home(vector), at_home(left_ops), at_home(right_ops))


def apply_kernel(n, npairs, over_rows, rows, start, table_ref, l4_ref, rr_ref, *refs):
    pieces, (near_ref, far_ref, row_ref, row_far_ref, column_ref, column_far_ref, square_ref, block, total) = refs[:n], refs[n:]
    terms, width = l4_ref.shape[:2]
    pick_ref, mine_ref, _, first_ref, second_ref, dst_ref, one_ref, two_ref, count_ref = parts(table_ref, n, terms, npairs)
    square = jnp.zeros((8, width), jnp.float32)
    product = jnp.zeros((8, width), jnp.float32)
    block[terms * n] = jnp.zeros((rows, width), jnp.float32)
    left = l4_ref[:, start:start + rows, :].reshape(terms * rows, 4 * width)
    for c in range(n // 2):
        columns = []
        for r in (2 * c, 2 * c + 1):
            high, low = halves(pieces[r][pick_ref[r]])
            columns.append(jnp.concatenate([high, high, low, low], axis=0))
            held = pieces[r][:, start:start + rows, :]
            square = square + tile_sum(held * held)
        both = jnp.dot(left, jnp.concatenate(columns, axis=1), preferred_element_type=jnp.float32)
        for k in range(2):
            at = (2 * c + k) * terms
            block[at:at + terms] = both[:, k * width:(k + 1) * width].reshape(terms, rows, width)
    square_ref[...] = square

    def add(i, carry):
        block[dst_ref[i]] = block[one_ref[i]] + block[two_ref[i]]
        return carry

    lax.fori_loop(0, count_ref[0], add, 0)
    late = 0
    for low_end in range(0, n, 4):
        for r in range(low_end, low_end + 4):
            for j in range(terms):
                at = j * n + r
                high, low = halves(block[first_ref[at]] + block[second_ref[at]])
                total[r, :, j * width:(j + 1) * width] = high
                total[r, :, (terms + j) * width:(terms + j + 1) * width] = low
        both = jnp.dot(total[low_end:low_end + 4].reshape(4 * rows, 2 * terms * width), rr_ref[...],
                       preferred_element_type=jnp.float32)
        slots = both[:, :width] + both[:, width:]
        for r in range(low_end, low_end + 4):
            slot = slots[(r - low_end) * rows:(r - low_end + 1) * rows]
            product = product + tile_sum(pieces[r][mine_ref[r], start:start + rows, :] * slot)
            g, core = divmod(r, 2)
            if g == 3:
                (column_far_ref if core else column_ref)[...] = slot
            elif g in over_rows:
                at = over_rows.index(g) * rows
                (row_far_ref if core else row_ref)[at:at + rows, :] = slot
            else:
                (far_ref if core else near_ref)[late * rows:(late + 1) * rows, :] = slot
                late += core
    for ref in (far_ref, row_ref, row_far_ref):
        ref[ref.shape[0] - 8:, :] = product


def apply(n, over_rows, rows, start, tables, pieces):
    terms, width = tables[0].shape[:2]
    npairs = (tables[2].shape[0] - sum(lengths(n, terms, 0))) // 3
    spare = npairs // 3
    late = n // 2 - 1 - len(over_rows)
    shape = lambda *dims: jax.ShapeDtypeStruct(dims, jnp.float32)
    return pl.pallas_call(
        functools.partial(apply_kernel, n, npairs, over_rows, rows, start),
        out_shape=(shape(late * rows, width), shape(late * rows + 8, width)) + (shape(len(over_rows) * rows + 8, width),) * 2
        + (shape(rows, width),) * 2 + (shape(8, width),),
        in_specs=[SMEM] + [VMEM] * (2 + n),
        out_specs=[VMEM] * 7,
        scratch_shapes=[
            pltpu.VMEM((terms * n + 1 + spare, rows, width), jnp.float32),
            pltpu.VMEM((n, rows, 2 * terms * width), jnp.bfloat16),
        ],
        compiler_params=params(32 if n <= 16 else 56),
        name="apply",
    )(tables[2], *tables[:2], *pieces)


def joined(parts, count):
    if len(parts) == 1:
        return parts[0]
    height, width = parts[0].shape
    end = height // (8 * count) * 8 * count
    whole = jnp.concatenate([x[:end].reshape(count, -1, width) for x in parts], axis=1).reshape(-1, width)
    return whole if end == height else jnp.concatenate([whole, sum(x[end:] for x in parts)])


def swapped(x, k):
    n = lax.axis_size("term")
    return lax.ppermute(x, "term", [(i, i ^ k) for i in range(n)])


def local(kernel, name, out_shape, scalars, arrays):
    many = isinstance(out_shape, tuple)
    return pl.pallas_call(
        kernel,
        out_shape=out_shape,
        in_specs=[SMEM] * len(scalars) + [VMEM] * len(arrays),
        out_specs=[VMEM] * len(out_shape) if many else VMEM,
        compiler_params=params(16),
        name=name,
    )(*scalars, *arrays)


def fold_kernel(n, late, over_rows, table_ref, near_ref, far_in, far_ref, row_ref, row_far_ref, column_ref, column_far_ref,
                own_ref, step_ref, *send_refs):
    width = near_ref.shape[1]
    chips = n // 2
    place_ref = Part(table_ref, 2 * n)
    end = len(late) * width
    over = len(over_rows) * width
    tile = far_in[end:] + far_ref[end:] + row_ref[over:] + row_far_ref[over:]
    for i, g in enumerate(late):
        come = [(0, near_ref, i), (1, far_ref, i)]
        if g == 1:
            come += [(4, column_ref, 0), (5, column_far_ref, 0)]
        if g + 1 in over_rows:
            come += [(2, row_ref, over_rows.index(g + 1)), (3, row_far_ref, over_rows.index(g + 1))]
        for b in range(2):
            block = sum(ref[at * width:(at + 1) * width] * (place_ref[q * chips + g] == b).astype(jnp.float32)
                        for q, ref, at in come)
            if g == 0:
                own_ref[b] = block
            elif g == 1:
                step_ref[b] = block
            else:
                send_refs[g // 2 - 1][b * width:(b + 1) * width] = block
    for send_ref in send_refs:
        send_ref[2 * width:] = tile


def landed(own_ref, step_ref, refs):
    width = own_ref.shape[2]
    sent, came = refs[0], refs[1:]
    tile = sent[2 * width:]
    for ref in came:
        tile = tile + ref[2 * width:]
    sums = []
    for b in range(2):
        total = own_ref[b] + step_ref[b]
        for ref in came:
            total = total + ref[b * width:(b + 1) * width]
        sums.append(total)
    return sums, jnp.sum(tile)


def step_kernel(own_ref, step_ref, square_ref, vector_ref, precond_ref, *refs):
    out_ref = refs[-1]
    sigma, product = landed(own_ref, step_ref, refs[:-1])
    theta = product / jnp.sum(square_ref[...])
    for b in range(2):
        v = vector_ref[b]
        out_ref[b] = v - precond_ref[b] * (sigma[b] - theta * v)


def last_kernel(cells, own_ref, step_ref, square_ref, vector_ref, precond_ref, *refs):
    residual_ref, out_ref, tile_ref = refs[-3:]
    sigma, product = landed(own_ref, step_ref, refs[:-3])
    square = jnp.sum(square_ref[...])
    theta = product / square
    scale = 1.0 / jnp.sqrt(square / cells + 1e-06)
    tile = jnp.zeros(tile_ref.shape, jnp.float32)
    for b in range(2):
        v = vector_ref[b]
        residual = (sigma[b] - theta * v) * scale
        residual_ref[b] = residual
        corrected = v * scale - precond_ref[b] * residual
        out_ref[b] = corrected
        tile = tile + tile_sum(corrected * corrected)
    tile_ref[...] = tile


def norm_kernel(cells, corrected_ref, tiles_ref, out_ref):
    scale = 1.0 / jnp.sqrt(jnp.sum(jnp.sum(tiles_ref[...], axis=0)) / cells + 1e-06)
    out_ref[...] = corrected_ref[...] * scale


def scattered(n, tables, pieces):
    width = pieces[0].shape[1]
    chips = n // 2
    rows = width if n <= 16 else width // 4
    over_rows = list(range(chips - 1, 3, -2))
    late = [g for g in range(chips) if g != 3 and g not in over_rows]
    shape = lambda *dims: jax.ShapeDtypeStruct(dims, jnp.float32)
    runs = [apply(n, over_rows, rows, start, tables, pieces) for start in range(0, width, rows)]
    counts = (len(late), len(late), len(over_rows), len(over_rows), 1, 1)
    near, far, row, row_far, column, column_far = (joined([x[i] for x in runs], k) for i, k in enumerate(counts))
    square = functools.reduce(jnp.add, [x[6] for x in runs])
    own, step, *sends = local(
        functools.partial(fold_kernel, n, late, over_rows), "fold",
        (shape(2, width, width),) * 2 + (shape(2 * width + 8, width),) * (chips // 2 - 1), tables[2:3],
        (near, far, swapped(far, CORE), swapped(row, ROW), swapped(row_far, ROW + CORE), swapped(column, COLUMN),
         swapped(column_far, COLUMN + CORE)))
    came = [swapped(x, 2 * ROW * (i + 1)) for i, x in reversed(list(enumerate(sends)))]
    return square, (own, swapped(step, ROW)), [sends[0], *came]


def gathered(n, x, held=None):
    pieces = {0: x}
    for k in reversed(range(8, n, 4)):
        pieces[k] = swapped(x, k)
    pieces[ROW] = swapped(x, ROW)
    pieces[COLUMN] = swapped(x, COLUMN)
    if held is not None:
        pieces[n - 4], pieces[0] = lax.optimization_barrier((pieces[n - 4], held))
    for k in reversed(range(8, n, 4)):
        pieces[k + ROW] = swapped(pieces[k], ROW)
    pieces[COLUMN + ROW] = swapped(pieces[ROW], COLUMN)
    for k in range(0, n, 2):
        pieces[k + CORE] = swapped(pieces[k], CORE)
    return [pieces[k] for k in range(n)]


def shards(wavefn, left_ops, right_ops, precond, fetch_map, store_map, pair_list, live_count):
    n = lax.axis_size("term")
    me = lax.axis_index("term").astype(jnp.int32).reshape(1)
    width = wavefn.shape[1]
    cells = wavefn.size * n
    *tables, held = prep(n, me, fetch_map, store_map, pair_list[0].T.reshape(-1), live_count, wavefn, left_ops, right_ops)
    block = jax.ShapeDtypeStruct(wavefn.shape, jnp.float32)
    tile = jax.ShapeDtypeStruct((8, width), jnp.float32)
    vector = wavefn
    for iteration in range(ITERS):
        pieces = gathered(n, vector, held if iteration == 0 else None)
        vector = pieces[0]
        square, sums, parts = scattered(n, tables, pieces)
        arrays = (*sums, square, vector, precond, *parts)
        if iteration < ITERS - 1:
            vector = local(step_kernel, "step", block, (), arrays)
    residual, corrected, partial = local(
        functools.partial(last_kernel, cells), "last", (block, block, tile), (), arrays)
    tiles = lax.all_to_all(jnp.broadcast_to(partial[None], (n, 8, width)), "term",
                           split_axis=0, concat_axis=0, tiled=True)
    return local(functools.partial(norm_kernel, cells), "norm", block, (), (corrected, tiles)), residual


def solution(mesh):
    field = P(("group", "term"), None, None)
    return jax.shard_map(
        shards,
        mesh=mesh,
        in_specs=(field, field, field, field, P(), P(), P("term", None, None), P("term")),
        out_specs=(field, field),
        check_vma=False,
    )
```

```python
import functools

import jax
import jax.numpy as jnp
from jax import lax
from jax.experimental import pallas as pl
from jax.experimental.pallas import tpu as pltpu
from jax.sharding import PartitionSpec as P

ITERS = 2
CORE, ROW, COLUMN = 1, 2, 4
SENDERS = 6
SMEM = pl.BlockSpec(memory_space=pltpu.SMEM)
VMEM = pl.BlockSpec(memory_space=pltpu.VMEM)


def params(mebibytes):
    return pltpu.CompilerParams(vmem_limit_bytes=mebibytes * 2**20)


def halves(x):
    high = x.astype(jnp.bfloat16)
    return high, (x - high.astype(jnp.float32)).astype(jnp.bfloat16)


def tile_sum(x):
    return jnp.sum(x.reshape(-1, 8, x.shape[-1]), axis=0)


class Part:
    def __init__(self, ref, start):
        self.ref, self.start = ref, start

    def __getitem__(self, i):
        return self.ref[self.start + i]

    def __setitem__(self, i, value):
        self.ref[self.start + i] = value


def lengths(n, terms, npairs):
    return n, n, SENDERS * n // 2, terms * n, terms * n, npairs, npairs, npairs, 1


def parts(ref, n, terms, npairs):
    sizes = lengths(n, terms, npairs)
    return [Part(ref, sum(sizes[:i])) for i in range(len(sizes))]


def prep_kernel(n, spare, me_ref, fetch_in, store_in, pairs_in, live_in, vector_in, left_in, right_in, l4_ref, rr_ref,
                table_ref, vector_ref,
                seen_ref, fetch_ref, store_ref, pairs_ref, live_ref, left_ref, right_ref, sems):
    copies = [pltpu.make_async_copy(source, target, sems.at[i]) for i, (source, target) in enumerate((
        (fetch_in, fetch_ref), (store_in, store_ref), (pairs_in, pairs_ref), (live_in, live_ref),
        (left_in, left_ref), (right_in, right_ref), (vector_in, vector_ref)))]
    for copy in copies:
        copy.start()
    me = me_ref[0]
    terms = left_ref.shape[0]
    width = left_ref.shape[1]
    zero = terms * n
    npairs = pairs_ref.shape[0] // 3
    pick_ref, mine_ref, place_ref, first_ref, second_ref, dst_ref, one_ref, two_ref, count_ref = parts(
        table_ref, n, terms, npairs)

    def clear(cell, carry):
        first_ref[cell] = zero
        second_ref[cell] = zero
        seen_ref[cell] = 0
        return carry

    lax.fori_loop(0, terms * n, clear, 0, unroll=8)
    for copy in copies[:4]:
        copy.wait()

    def relative(r, carry):
        device = lax.bitwise_xor(me, r)
        pick_ref[r] = fetch_ref[device, me]
        mine_ref[r] = store_ref[me, device]
        return carry

    lax.fori_loop(0, n, relative, 0)

    def chip(g, carry):
        for q in range(SENDERS):
            place_ref[q * (n // 2) + g] = store_ref[lax.bitwise_xor(me, q), lax.bitwise_xor(me, 2 * g)]
        return carry

    lax.fori_loop(0, n // 2, chip, 0)

    def pair(p, carry):
        extra, ops = carry
        a = lax.bitwise_xor(pairs_ref[p], me)
        j = pairs_ref[npairs + p]
        o = lax.bitwise_xor(pairs_ref[2 * npairs + p], me)
        cell = j * n + o
        source = a * terms + j
        seen = seen_ref[cell]
        seen_ref[cell] = seen + 1
        before = second_ref[cell]
        place = jnp.where(seen == 2, spare + extra, before)
        first_ref[cell] = jnp.where(seen == 0, source, first_ref[cell])
        second_ref[cell] = jnp.where(seen == 0, before, jnp.where(seen == 1, source, place))
        dst_ref[ops] = place
        one_ref[ops] = before
        two_ref[ops] = source
        return extra + (seen == 2).astype(jnp.int32), ops + (seen >= 2).astype(jnp.int32)

    _, ops = lax.fori_loop(0, live_ref[0], pair, (jnp.int32(0), jnp.int32(0)))
    count_ref[0] = ops
    for copy in copies[4:]:
        copy.wait()

    for j in range(terms):
        high, low = halves(left_ref[j])
        for k, part in enumerate((high, low, high, low)):
            l4_ref[j, :, k * width:(k + 1) * width] = part
        high, low = halves(right_ref[j])
        for k in range(2):
            row = (k * terms + j) * width
            rr_ref[row:row + width, :width] = high
            rr_ref[row:row + width, width:] = low


def at_home(x):
    return pltpu.with_memory_space_constraint(x, pltpu.HBM)


def prep(n, me, fetch, store, pairs, live, vector, left_ops, right_ops):
    terms, width = left_ops.shape[:2]
    npairs = pairs.shape[0] // 3
    return pl.pallas_call(
        functools.partial(prep_kernel, n, terms * n + 1),
        out_shape=(
            jax.ShapeDtypeStruct((terms, width, 4 * width), jnp.bfloat16),
            jax.ShapeDtypeStruct((2 * terms * width, 2 * width), jnp.bfloat16),
            jax.ShapeDtypeStruct((sum(lengths(n, terms, npairs)),), jnp.int32),
            jax.ShapeDtypeStruct(vector.shape, jnp.float32),
        ),
        in_specs=[SMEM] + [pl.BlockSpec(memory_space=pltpu.HBM)] * 7,
        out_specs=[VMEM] * 2 + [SMEM, VMEM],
        scratch_shapes=[
            pltpu.SMEM((terms * n,), jnp.int32),
            pltpu.SMEM(fetch.shape, jnp.int32),
            pltpu.SMEM(store.shape, jnp.int32),
            pltpu.SMEM(pairs.shape, jnp.int32),
            pltpu.SMEM((1,), jnp.int32),
            pltpu.VMEM(left_ops.shape, jnp.float32),
            pltpu.VMEM(left_ops.shape, jnp.float32),
            pltpu.SemaphoreType.DMA((7,)),
        ],
        compiler_params=params(16),
        name="prep",
    )(me, at_home(fetch), at_home(store), at_home(pairs), live, at_home(vector), at_home(left_ops), at_home(right_ops))


def apply_kernel(n, npairs, over_rows, rows, start, table_ref, l4_ref, rr_ref, *refs):
    pieces, (near_ref, far_ref, row_ref, row_far_ref, column_ref, column_far_ref, square_ref, block, total) = refs[:n], refs[n:]
    terms, width = l4_ref.shape[:2]
    pick_ref, mine_ref, _, first_ref, second_ref, dst_ref, one_ref, two_ref, count_ref = parts(table_ref, n, terms, npairs)
    square = jnp.zeros((8, width), jnp.float32)
    product = jnp.zeros((8, width), jnp.float32)
    block[terms * n] = jnp.zeros((rows, width), jnp.float32)
    left = l4_ref[:, start:start + rows, :].reshape(terms * rows, 4 * width)
    for c in range(n // 2):
        columns = []
        for r in (2 * c, 2 * c + 1):
            high, low = halves(pieces[r][pick_ref[r]])
            columns.append(jnp.concatenate([high, high, low, low], axis=0))
            held = pieces[r][:, start:start + rows, :]
            square = square + tile_sum(held * held)
        both = jnp.dot(left, jnp.concatenate(columns, axis=1), preferred_element_type=jnp.float32)
        for k in range(2):
            at = (2 * c + k) * terms
            block[at:at + terms] = both[:, k * width:(k + 1) * width].reshape(terms, rows, width)
    square_ref[...] = square

    def add(i, carry):
        block[dst_ref[i]] = block[one_ref[i]] + block[two_ref[i]]
        return carry

    lax.fori_loop(0, count_ref[0], add, 0)
    late = 0
    for low_end in range(0, n, 4):
        for r in range(low_end, low_end + 4):
            for j in range(terms):
                at = j * n + r
                high, low = halves(block[first_ref[at]] + block[second_ref[at]])
                total[r, :, j * width:(j + 1) * width] = high
                total[r, :, (terms + j) * width:(terms + j + 1) * width] = low
        both = jnp.dot(total[low_end:low_end + 4].reshape(4 * rows, 2 * terms * width), rr_ref[...],
                       preferred_element_type=jnp.float32)
        slots = both[:, :width] + both[:, width:]
        for r in range(low_end, low_end + 4):
            slot = slots[(r - low_end) * rows:(r - low_end + 1) * rows]
            product = product + tile_sum(pieces[r][mine_ref[r], start:start + rows, :] * slot)
            g, core = divmod(r, 2)
            if g == 3:
                (column_far_ref if core else column_ref)[...] = slot
            elif g in over_rows:
                at = over_rows.index(g) * rows
                (row_far_ref if core else row_ref)[at:at + rows, :] = slot
            else:
                (far_ref if core else near_ref)[late * rows:(late + 1) * rows, :] = slot
                late += core
    for ref in (far_ref, row_ref, row_far_ref):
        ref[ref.shape[0] - 8:, :] = product


def apply(n, over_rows, rows, start, tables, pieces):
    terms, width = tables[0].shape[:2]
    npairs = (tables[2].shape[0] - sum(lengths(n, terms, 0))) // 3
    spare = npairs // 3
    late = n // 2 - 1 - len(over_rows)
    shape = lambda *dims: jax.ShapeDtypeStruct(dims, jnp.float32)
    return pl.pallas_call(
        functools.partial(apply_kernel, n, npairs, over_rows, rows, start),
        out_shape=(shape(late * rows, width), shape(late * rows + 8, width)) + (shape(len(over_rows) * rows + 8, width),) * 2
        + (shape(rows, width),) * 2 + (shape(8, width),),
        in_specs=[SMEM] + [VMEM] * (2 + n),
        out_specs=[VMEM] * 7,
        scratch_shapes=[
            pltpu.VMEM((terms * n + 1 + spare, rows, width), jnp.float32),
            pltpu.VMEM((n, rows, 2 * terms * width), jnp.bfloat16),
        ],
        compiler_params=params(32 if n <= 16 else 56),
        name="apply",
    )(tables[2], *tables[:2], *pieces)


def joined(parts, count):
    if len(parts) == 1:
        return parts[0]
    height, width = parts[0].shape
    end = height // (8 * count) * 8 * count
    whole = jnp.concatenate([x[:end].reshape(count, -1, width) for x in parts], axis=1).reshape(-1, width)
    return whole if end == height else jnp.concatenate([whole, sum(x[end:] for x in parts)])


def swapped(x, k):
    n = lax.axis_size("term")
    return lax.ppermute(x, "term", [(i, i ^ k) for i in range(n)])


def local(kernel, name, out_shape, scalars, arrays):
    many = isinstance(out_shape, tuple)
    return pl.pallas_call(
        kernel,
        out_shape=out_shape,
        in_specs=[SMEM] * len(scalars) + [VMEM] * len(arrays),
        out_specs=[VMEM] * len(out_shape) if many else VMEM,
        compiler_params=params(16),
        name=name,
    )(*scalars, *arrays)


def fold_kernel(n, late, over_rows, table_ref, near_ref, far_in, far_ref, row_ref, row_far_ref, column_ref, column_far_ref,
                own_ref, step_ref, *send_refs):
    width = near_ref.shape[1]
    chips = n // 2
    place_ref = Part(table_ref, 2 * n)
    end = len(late) * width
    over = len(over_rows) * width
    tile = far_in[end:] + far_ref[end:] + row_ref[over:] + row_far_ref[over:]
    for i, g in enumerate(late):
        come = [(0, near_ref, i), (1, far_ref, i)]
        if g == 1:
            come += [(4, column_ref, 0), (5, column_far_ref, 0)]
        if g + 1 in over_rows:
            come += [(2, row_ref, over_rows.index(g + 1)), (3, row_far_ref, over_rows.index(g + 1))]
        for b in range(2):
            block = sum(ref[at * width:(at + 1) * width] * (place_ref[q * chips + g] == b).astype(jnp.float32)
                        for q, ref, at in come)
            if g == 0:
                own_ref[b] = block
            elif g == 1:
                step_ref[b] = block
            else:
                send_refs[g // 2 - 1][b * width:(b + 1) * width] = block
    for send_ref in send_refs:
        send_ref[2 * width:] = tile


def landed(own_ref, step_ref, refs):
    width = own_ref.shape[2]
    sent, came = refs[0], refs[1:]
    tile = sent[2 * width:]
    for ref in came:
        tile = tile + ref[2 * width:]
    sums = []
    for b in range(2):
        total = own_ref[b] + step_ref[b]
        for ref in came:
            total = total + ref[b * width:(b + 1) * width]
        sums.append(total)
    return sums, jnp.sum(tile)


def step_kernel(own_ref, step_ref, square_ref, vector_ref, precond_ref, *refs):
    out_ref = refs[-1]
    sigma, product = landed(own_ref, step_ref, refs[:-1])
    theta = product / jnp.sum(square_ref[...])
    for b in range(2):
        v = vector_ref[b]
        out_ref[b] = v - precond_ref[b] * (sigma[b] - theta * v)


def last_kernel(cells, own_ref, step_ref, square_ref, vector_ref, precond_ref, *refs):
    residual_ref, out_ref, tile_ref = refs[-3:]
    sigma, product = landed(own_ref, step_ref, refs[:-3])
    square = jnp.sum(square_ref[...])
    theta = product / square
    scale = 1.0 / jnp.sqrt(square / cells + 1e-06)
    tile = jnp.zeros(tile_ref.shape, jnp.float32)
    for b in range(2):
        v = vector_ref[b]
        residual = (sigma[b] - theta * v) * scale
        residual_ref[b] = residual
        corrected = v * scale - precond_ref[b] * residual
        out_ref[b] = corrected
        tile = tile + tile_sum(corrected * corrected)
    tile_ref[...] = tile


def norm_kernel(cells, corrected_ref, tiles_ref, out_ref):
    scale = 1.0 / jnp.sqrt(jnp.sum(jnp.sum(tiles_ref[...], axis=0)) / cells + 1e-06)
    out_ref[...] = corrected_ref[...] * scale


def scattered(n, tables, pieces):
    width = pieces[0].shape[1]
    chips = n // 2
    rows = width if n <= 16 else width // 4
    over_rows = list(range(chips - 1, 3, -2))
    late = [g for g in range(chips) if g != 3 and g not in over_rows]
    shape = lambda *dims: jax.ShapeDtypeStruct(dims, jnp.float32)
    runs = [apply(n, over_rows, rows, start, tables, pieces) for start in range(0, width, rows)]
    counts = (len(late), len(late), len(over_rows), len(over_rows), 1, 1)
    near, far, row, row_far, column, column_far = (joined([x[i] for x in runs], k) for i, k in enumerate(counts))
    square = functools.reduce(jnp.add, [x[6] for x in runs])
    own, step, *sends = local(
        functools.partial(fold_kernel, n, late, over_rows), "fold",
        (shape(2, width, width),) * 2 + (shape(2 * width + 8, width),) * (chips // 2 - 1), tables[2:3],
        (near, far, swapped(far, CORE), swapped(row, ROW), swapped(row_far, ROW + CORE), swapped(column, COLUMN),
         swapped(column_far, COLUMN + CORE)))
    came = [swapped(x, 2 * ROW * (i + 1)) for i, x in reversed(list(enumerate(sends)))]
    return square, (own, swapped(step, ROW)), [sends[0], *came]


def gathered(n, x, held=None):
    pieces = {0: x}
    for k in reversed(range(8, n, 4)):
        pieces[k] = swapped(x, k)
    pieces[ROW] = swapped(x, ROW)
    pieces[COLUMN] = swapped(x, COLUMN)
    if held is not None:
        pieces[n - 4], pieces[0] = lax.optimization_barrier((pieces[n - 4], held))
    else:
        pieces[COLUMN + ROW] = swapped(x, COLUMN + ROW)
        pieces[0], pieces[8] = lax.optimization_barrier((pieces[0], pieces[8]))
    for k in reversed(range(8, n, 4)):
        pieces[k + ROW] = swapped(pieces[k], ROW)
    if held is not None:
        pieces[COLUMN + ROW] = swapped(pieces[ROW], COLUMN)
    for k in range(0, n, 2):
        pieces[k + CORE] = swapped(pieces[k], CORE)
    return [pieces[k] for k in range(n)]


def shards(wavefn, left_ops, right_ops, precond, fetch_map, store_map, pair_list, live_count):
    n = lax.axis_size("term")
    me = lax.axis_index("term").astype(jnp.int32).reshape(1)
    width = wavefn.shape[1]
    cells = wavefn.size * n
    *tables, held = prep(n, me, fetch_map, store_map, pair_list[0].T.reshape(-1), live_count, wavefn, left_ops, right_ops)
    block = jax.ShapeDtypeStruct(wavefn.shape, jnp.float32)
    tile = jax.ShapeDtypeStruct((8, width), jnp.float32)
    vector = wavefn
    for iteration in range(ITERS):
        pieces = gathered(n, vector, held if iteration == 0 else None)
        vector = pieces[0]
        square, sums, parts = scattered(n, tables, pieces)
        arrays = (*sums, square, vector, precond, *parts)
        if iteration < ITERS - 1:
            vector = local(step_kernel, "step", block, (), arrays)
    residual, corrected, partial = local(
        functools.partial(last_kernel, cells), "last", (block, block, tile), (), arrays)
    tiles = lax.all_to_all(jnp.broadcast_to(partial[None], (n, 8, width)), "term",
                           split_axis=0, concat_axis=0, tiled=True)
    return local(functools.partial(norm_kernel, cells), "norm", block, (), (corrected, tiles)), residual


def solution(mesh):
    field = P(("group", "term"), None, None)
    return jax.shard_map(
        shards,
        mesh=mesh,
        in_specs=(field, field, field, field, P(), P(), P("term", None, None), P("term")),
        out_specs=(field, field),
        check_vma=False,
    )
```

```python
import functools

import jax
import jax.numpy as jnp
from jax import lax
from jax.experimental import pallas as pl
from jax.experimental.pallas import tpu as pltpu
from jax.sharding import PartitionSpec as P

ITERS = 2
CORE, ROW, COLUMN = 1, 2, 4
SENDERS = 6
SMEM = pl.BlockSpec(memory_space=pltpu.SMEM)
VMEM = pl.BlockSpec(memory_space=pltpu.VMEM)


def params(mebibytes):
    return pltpu.CompilerParams(vmem_limit_bytes=mebibytes * 2**20)


def halves(x):
    high = x.astype(jnp.bfloat16)
    return high, (x - high.astype(jnp.float32)).astype(jnp.bfloat16)


def tile_sum(x):
    return jnp.sum(x.reshape(-1, 8, x.shape[-1]), axis=0)


class Part:
    def __init__(self, ref, start):
        self.ref, self.start = ref, start

    def __getitem__(self, i):
        return self.ref[self.start + i]

    def __setitem__(self, i, value):
        self.ref[self.start + i] = value


def lengths(n, terms, npairs):
    return n, n, SENDERS * n // 2, terms * n, terms * n, npairs, npairs, npairs, 1


def parts(ref, n, terms, npairs):
    sizes = lengths(n, terms, npairs)
    return [Part(ref, sum(sizes[:i])) for i in range(len(sizes))]


def prep_kernel(n, spare, me_ref, fetch_in, store_in, pairs_in, live_in, vector_in, left_in, right_in, l4_ref, rr_ref,
                table_ref, vector_ref,
                seen_ref, fetch_ref, store_ref, pairs_ref, live_ref, left_ref, right_ref, sems):
    copies = [pltpu.make_async_copy(source, target, sems.at[i]) for i, (source, target) in enumerate((
        (fetch_in, fetch_ref), (store_in, store_ref), (pairs_in, pairs_ref), (live_in, live_ref),
        (left_in, left_ref), (right_in, right_ref), (vector_in, vector_ref)))]
    for copy in copies:
        copy.start()
    me = me_ref[0]
    terms = left_ref.shape[0]
    width = left_ref.shape[1]
    zero = terms * n
    npairs = pairs_ref.shape[0] // 3
    pick_ref, mine_ref, place_ref, first_ref, second_ref, dst_ref, one_ref, two_ref, count_ref = parts(
        table_ref, n, terms, npairs)

    def clear(cell, carry):
        first_ref[cell] = zero
        second_ref[cell] = zero
        seen_ref[cell] = 0
        return carry

    lax.fori_loop(0, terms * n, clear, 0, unroll=8)
    for copy in copies[:4]:
        copy.wait()

    def relative(r, carry):
        device = lax.bitwise_xor(me, r)
        pick_ref[r] = fetch_ref[device, me]
        mine_ref[r] = store_ref[me, device]
        return carry

    lax.fori_loop(0, n, relative, 0)

    def chip(g, carry):
        for q in range(SENDERS):
            place_ref[q * (n // 2) + g] = store_ref[lax.bitwise_xor(me, q), lax.bitwise_xor(me, 2 * g)]
        return carry

    lax.fori_loop(0, n // 2, chip, 0)

    def pair(p, carry):
        extra, ops = carry
        a = lax.bitwise_xor(pairs_ref[p], me)
        j = pairs_ref[npairs + p]
        o = lax.bitwise_xor(pairs_ref[2 * npairs + p], me)
        cell = j * n + o
        source = a * terms + j
        seen = seen_ref[cell]
        seen_ref[cell] = seen + 1
        before = second_ref[cell]
        place = jnp.where(seen == 2, spare + extra, before)
        first_ref[cell] = jnp.where(seen == 0, source, first_ref[cell])
        second_ref[cell] = jnp.where(seen == 0, before, jnp.where(seen == 1, source, place))
        dst_ref[ops] = place
        one_ref[ops] = before
        two_ref[ops] = source
        return extra + (seen == 2).astype(jnp.int32), ops + (seen >= 2).astype(jnp.int32)

    _, ops = lax.fori_loop(0, live_ref[0], pair, (jnp.int32(0), jnp.int32(0)))
    count_ref[0] = ops
    for copy in copies[4:]:
        copy.wait()

    for j in range(terms):
        high, low = halves(left_ref[j])
        for k, part in enumerate((high, low, high, low)):
            l4_ref[j, :, k * width:(k + 1) * width] = part
        high, low = halves(right_ref[j])
        for k in range(2):
            row = (k * terms + j) * width
            rr_ref[row:row + width, :width] = high
            rr_ref[row:row + width, width:] = low


def at_home(x):
    return pltpu.with_memory_space_constraint(x, pltpu.HBM)


def prep(n, me, fetch, store, pairs, live, vector, left_ops, right_ops):
    terms, width = left_ops.shape[:2]
    npairs = pairs.shape[0] // 3
    return pl.pallas_call(
        functools.partial(prep_kernel, n, terms * n + 1),
        out_shape=(
            jax.ShapeDtypeStruct((terms, width, 4 * width), jnp.bfloat16),
            jax.ShapeDtypeStruct((2 * terms * width, 2 * width), jnp.bfloat16),
            jax.ShapeDtypeStruct((sum(lengths(n, terms, npairs)),), jnp.int32),
            jax.ShapeDtypeStruct(vector.shape, jnp.float32),
        ),
        in_specs=[SMEM] + [pl.BlockSpec(memory_space=pltpu.HBM)] * 7,
        out_specs=[VMEM] * 2 + [SMEM, VMEM],
        scratch_shapes=[
            pltpu.SMEM((terms * n,), jnp.int32),
            pltpu.SMEM(fetch.shape, jnp.int32),
            pltpu.SMEM(store.shape, jnp.int32),
            pltpu.SMEM(pairs.shape, jnp.int32),
            pltpu.SMEM((1,), jnp.int32),
            pltpu.VMEM(left_ops.shape, jnp.float32),
            pltpu.VMEM(left_ops.shape, jnp.float32),
            pltpu.SemaphoreType.DMA((7,)),
        ],
        compiler_params=params(16),
        name="prep",
    )(me, at_home(fetch), at_home(store), at_home(pairs), live, at_home(vector), at_home(left_ops), at_home(right_ops))


def apply_kernel(n, npairs, over_rows, rows, start, table_ref, l4_ref, rr_ref, *refs):
    pieces, (near_ref, far_ref, row_ref, row_far_ref, column_ref, column_far_ref, square_ref, block, total) = refs[:n], refs[n:]
    terms, width = l4_ref.shape[:2]
    pick_ref, mine_ref, _, first_ref, second_ref, dst_ref, one_ref, two_ref, count_ref = parts(table_ref, n, terms, npairs)
    square = jnp.zeros((8, width), jnp.float32)
    product = jnp.zeros((8, width), jnp.float32)
    block[terms * n] = jnp.zeros((rows, width), jnp.float32)
    left = l4_ref[:, start:start + rows, :].reshape(terms * rows, 4 * width)
    for c in range(n // 2):
        columns = []
        for r in (2 * c, 2 * c + 1):
            high, low = halves(pieces[r][pick_ref[r]])
            columns.append(jnp.concatenate([high, high, low, low], axis=0))
            held = pieces[r][:, start:start + rows, :]
            square = square + tile_sum(held * held)
        both = jnp.dot(left, jnp.concatenate(columns, axis=1), preferred_element_type=jnp.float32)
        for k in range(2):
            at = (2 * c + k) * terms
            block[at:at + terms] = both[:, k * width:(k + 1) * width].reshape(terms, rows, width)
    square_ref[...] = square

    def add(i, carry):
        block[dst_ref[i]] = block[one_ref[i]] + block[two_ref[i]]
        return carry

    lax.fori_loop(0, count_ref[0], add, 0)
    late = 0
    for low_end in range(0, n, 4):
        for r in range(low_end, low_end + 4):
            for j in range(terms):
                at = j * n + r
                high, low = halves(block[first_ref[at]] + block[second_ref[at]])
                total[r, :, j * width:(j + 1) * width] = high
                total[r, :, (terms + j) * width:(terms + j + 1) * width] = low
        both = jnp.dot(total[low_end:low_end + 4].reshape(4 * rows, 2 * terms * width), rr_ref[...],
                       preferred_element_type=jnp.float32)
        slots = both[:, :width] + both[:, width:]
        for r in range(low_end, low_end + 4):
            slot = slots[(r - low_end) * rows:(r - low_end + 1) * rows]
            product = product + tile_sum(pieces[r][mine_ref[r], start:start + rows, :] * slot)
            g, core = divmod(r, 2)
            if g == 3:
                (column_far_ref if core else column_ref)[...] = slot
            elif g in over_rows:
                at = over_rows.index(g) * rows
                (row_far_ref if core else row_ref)[at:at + rows, :] = slot
            else:
                (far_ref if core else near_ref)[late * rows:(late + 1) * rows, :] = slot
                late += core
    for ref in (far_ref, row_ref, row_far_ref):
        ref[ref.shape[0] - 8:, :] = product


def apply(n, over_rows, rows, start, tables, pieces):
    terms, width = tables[0].shape[:2]
    npairs = (tables[2].shape[0] - sum(lengths(n, terms, 0))) // 3
    spare = npairs // 3
    late = n // 2 - 1 - len(over_rows)
    shape = lambda *dims: jax.ShapeDtypeStruct(dims, jnp.float32)
    return pl.pallas_call(
        functools.partial(apply_kernel, n, npairs, over_rows, rows, start),
        out_shape=(shape(late * rows, width), shape(late * rows + 8, width)) + (shape(len(over_rows) * rows + 8, width),) * 2
        + (shape(rows, width),) * 2 + (shape(8, width),),
        in_specs=[SMEM] + [VMEM] * (2 + n),
        out_specs=[VMEM] * 7,
        scratch_shapes=[
            pltpu.VMEM((terms * n + 1 + spare, rows, width), jnp.float32),
            pltpu.VMEM((n, rows, 2 * terms * width), jnp.bfloat16),
        ],
        compiler_params=params(32 if n <= 16 else 56),
        name="apply",
    )(tables[2], *tables[:2], *pieces)


def joined(parts, count):
    if len(parts) == 1:
        return parts[0]
    height, width = parts[0].shape
    end = height // (8 * count) * 8 * count
    whole = jnp.concatenate([x[:end].reshape(count, -1, width) for x in parts], axis=1).reshape(-1, width)
    return whole if end == height else jnp.concatenate([whole, sum(x[end:] for x in parts)])


def swapped(x, k):
    n = lax.axis_size("term")
    return lax.ppermute(x, "term", [(i, i ^ k) for i in range(n)])


def local(kernel, name, out_shape, scalars, arrays):
    many = isinstance(out_shape, tuple)
    return pl.pallas_call(
        kernel,
        out_shape=out_shape,
        in_specs=[SMEM] * len(scalars) + [VMEM] * len(arrays),
        out_specs=[VMEM] * len(out_shape) if many else VMEM,
        compiler_params=params(16),
        name=name,
    )(*scalars, *arrays)


def fold_kernel(n, late, over_rows, table_ref, near_ref, far_in, far_ref, row_ref, row_far_ref, column_ref, column_far_ref,
                own_ref, step_ref, *send_refs):
    width = near_ref.shape[1]
    chips = n // 2
    place_ref = Part(table_ref, 2 * n)
    end = len(late) * width
    over = len(over_rows) * width
    tile = far_in[end:] + far_ref[end:] + row_ref[over:] + row_far_ref[over:]
    for i, g in enumerate(late):
        come = [(0, near_ref, i), (1, far_ref, i)]
        if g == 1:
            come += [(4, column_ref, 0), (5, column_far_ref, 0)]
        if g + 1 in over_rows:
            come += [(2, row_ref, over_rows.index(g + 1)), (3, row_far_ref, over_rows.index(g + 1))]
        for b in range(2):
            block = sum(ref[at * width:(at + 1) * width] * (place_ref[q * chips + g] == b).astype(jnp.float32)
                        for q, ref, at in come)
            if g == 0:
                own_ref[b] = block
            elif g == 1:
                step_ref[b] = block
            else:
                send_refs[g // 2 - 1][b * width:(b + 1) * width] = block
    for send_ref in send_refs:
        send_ref[2 * width:] = tile


def landed(own_ref, step_ref, refs):
    width = own_ref.shape[2]
    sent, came = refs[0], refs[1:]
    tile = sent[2 * width:]
    for ref in came:
        tile = tile + ref[2 * width:]
    sums = []
    for b in range(2):
        total = own_ref[b] + step_ref[b]
        for ref in came:
            total = total + ref[b * width:(b + 1) * width]
        sums.append(total)
    return sums, jnp.sum(tile)


def step_kernel(own_ref, step_ref, square_ref, vector_ref, precond_ref, *refs):
    out_ref = refs[-1]
    sigma, product = landed(own_ref, step_ref, refs[:-1])
    theta = product / jnp.sum(square_ref[...])
    for b in range(2):
        v = vector_ref[b]
        out_ref[b] = v - precond_ref[b] * (sigma[b] - theta * v)


def last_kernel(cells, own_ref, step_ref, square_ref, vector_ref, precond_ref, *refs):
    residual_ref, out_ref, tile_ref = refs[-3:]
    sigma, product = landed(own_ref, step_ref, refs[:-3])
    square = jnp.sum(square_ref[...])
    theta = product / square
    scale = 1.0 / jnp.sqrt(square / cells + 1e-06)
    tile = jnp.zeros(tile_ref.shape, jnp.float32)
    for b in range(2):
        v = vector_ref[b]
        residual = (sigma[b] - theta * v) * scale
        residual_ref[b] = residual
        corrected = v * scale - precond_ref[b] * residual
        out_ref[b] = corrected
        tile = tile + tile_sum(corrected * corrected)
    tile_ref[...] = tile


def norm_kernel(cells, corrected_ref, tiles_ref, out_ref):
    scale = 1.0 / jnp.sqrt(jnp.sum(jnp.sum(tiles_ref[...], axis=0)) / cells + 1e-06)
    out_ref[...] = corrected_ref[...] * scale


def scattered(n, tables, pieces):
    width = pieces[0].shape[1]
    chips = n // 2
    rows = width if n <= 16 else width // 4
    over_rows = list(range(chips - 1, 3, -2))
    late = [g for g in range(chips) if g != 3 and g not in over_rows]
    shape = lambda *dims: jax.ShapeDtypeStruct(dims, jnp.float32)
    runs = [apply(n, over_rows, rows, start, tables, pieces) for start in range(0, width, rows)]
    counts = (len(late), len(late), len(over_rows), len(over_rows), 1, 1)
    near, far, row, row_far, column, column_far = (joined([x[i] for x in runs], k) for i, k in enumerate(counts))
    square = functools.reduce(jnp.add, [x[6] for x in runs])
    own, step, *sends = local(
        functools.partial(fold_kernel, n, late, over_rows), "fold",
        (shape(2, width, width),) * 2 + (shape(2 * width + 8, width),) * (chips // 2 - 1), tables[2:3],
        (near, far, swapped(far, CORE), swapped(row, ROW), swapped(row_far, ROW + CORE), swapped(column, COLUMN),
         swapped(column_far, COLUMN + CORE)))
    came = [swapped(x, 2 * ROW * (i + 1)) for i, x in reversed(list(enumerate(sends)))]
    return square, (own, swapped(step, ROW)), [sends[0], *came]


def gathered(n, x, held=None):
    pieces = {0: x}
    for k in reversed(range(8, n, 4)):
        pieces[k] = swapped(x, k)
    pieces[ROW] = swapped(x, ROW)
    pieces[COLUMN] = swapped(x, COLUMN)
    if held is not None:
        pieces[n - 4], pieces[0] = lax.optimization_barrier((pieces[n - 4], held))
    for k in reversed(range(8, n, 4)):
        pieces[k + ROW] = swapped(pieces[k], ROW)
    pieces[COLUMN + ROW] = swapped(x, COLUMN + ROW) if held is None else swapped(pieces[ROW], COLUMN)
    if held is None:
        late = [0, 8, n - 4, n - 4 + ROW]
        pieces.update(zip(late, lax.optimization_barrier([pieces[k] for k in late])))
    for k in range(0, n, 2):
        pieces[k + CORE] = swapped(pieces[k], CORE)
    return [pieces[k] for k in range(n)]


def shards(wavefn, left_ops, right_ops, precond, fetch_map, store_map, pair_list, live_count):
    n = lax.axis_size("term")
    me = lax.axis_index("term").astype(jnp.int32).reshape(1)
    width = wavefn.shape[1]
    cells = wavefn.size * n
    *tables, held = prep(n, me, fetch_map, store_map, pair_list[0].T.reshape(-1), live_count, wavefn, left_ops, right_ops)
    block = jax.ShapeDtypeStruct(wavefn.shape, jnp.float32)
    tile = jax.ShapeDtypeStruct((8, width), jnp.float32)
    vector = wavefn
    for iteration in range(ITERS):
        pieces = gathered(n, vector, held if iteration == 0 else None)
        vector = pieces[0]
        square, sums, parts = scattered(n, tables, pieces)
        arrays = (*sums, square, vector, precond, *parts)
        if iteration < ITERS - 1:
            vector = local(step_kernel, "step", block, (), arrays)
    residual, corrected, partial = local(
        functools.partial(last_kernel, cells), "last", (block, block, tile), (), arrays)
    tiles = lax.all_to_all(jnp.broadcast_to(partial[None], (n, 8, width)), "term",
                           split_axis=0, concat_axis=0, tiled=True)
    return local(functools.partial(norm_kernel, cells), "norm", block, (), (corrected, tiles)), residual


def solution(mesh):
    field = P(("group", "term"), None, None)
    return jax.shard_map(
        shards,
        mesh=mesh,
        in_specs=(field, field, field, field, P(), P(), P("term", None, None), P("term")),
        out_specs=(field, field),
        check_vma=False,
    )
```

```python
import functools

import jax
import jax.numpy as jnp
from jax import lax
from jax.experimental import pallas as pl
from jax.experimental.pallas import tpu as pltpu
from jax.sharding import PartitionSpec as P

ITERS = 2
CORE, ROW, COLUMN = 1, 2, 4
SENDERS = 6
SMEM = pl.BlockSpec(memory_space=pltpu.SMEM)
VMEM = pl.BlockSpec(memory_space=pltpu.VMEM)


def params(mebibytes):
    return pltpu.CompilerParams(vmem_limit_bytes=mebibytes * 2**20)


def halves(x):
    high = x.astype(jnp.bfloat16)
    return high, (x - high.astype(jnp.float32)).astype(jnp.bfloat16)


def tile_sum(x):
    return jnp.sum(x.reshape(-1, 8, x.shape[-1]), axis=0)


class Part:
    def __init__(self, ref, start):
        self.ref, self.start = ref, start

    def __getitem__(self, i):
        return self.ref[self.start + i]

    def __setitem__(self, i, value):
        self.ref[self.start + i] = value


def lengths(n, terms, npairs):
    return n, n, SENDERS * n // 2, terms * n, terms * n, npairs, npairs, npairs, 1


def parts(ref, n, terms, npairs):
    sizes = lengths(n, terms, npairs)
    return [Part(ref, sum(sizes[:i])) for i in range(len(sizes))]


def prep_kernel(n, spare, me_ref, fetch_in, store_in, pairs_in, live_in, vector_in, left_in, right_in, l4_ref, rr_ref,
                table_ref, vector_ref,
                seen_ref, fetch_ref, store_ref, pairs_ref, live_ref, left_ref, right_ref, sems):
    copies = [pltpu.make_async_copy(source, target, sems.at[i]) for i, (source, target) in enumerate((
        (fetch_in, fetch_ref), (store_in, store_ref), (pairs_in, pairs_ref), (live_in, live_ref),
        (left_in, left_ref), (right_in, right_ref), (vector_in, vector_ref)))]
    for copy in copies:
        copy.start()
    me = me_ref[0]
    terms = left_ref.shape[0]
    width = left_ref.shape[1]
    zero = terms * n
    npairs = pairs_ref.shape[0] // 3
    pick_ref, mine_ref, place_ref, first_ref, second_ref, dst_ref, one_ref, two_ref, count_ref = parts(
        table_ref, n, terms, npairs)

    def clear(cell, carry):
        first_ref[cell] = zero
        second_ref[cell] = zero
        seen_ref[cell] = 0
        return carry

    lax.fori_loop(0, terms * n, clear, 0, unroll=8)
    for copy in copies[:4]:
        copy.wait()

    def relative(r, carry):
        device = lax.bitwise_xor(me, r)
        pick_ref[r] = fetch_ref[device, me]
        mine_ref[r] = store_ref[me, device]
        return carry

    lax.fori_loop(0, n, relative, 0)

    def chip(g, carry):
        for q in range(SENDERS):
            place_ref[q * (n // 2) + g] = store_ref[lax.bitwise_xor(me, q), lax.bitwise_xor(me, 2 * g)]
        return carry

    lax.fori_loop(0, n // 2, chip, 0)

    def pair(p, carry):
        extra, ops = carry
        a = lax.bitwise_xor(pairs_ref[p], me)
        j = pairs_ref[npairs + p]
        o = lax.bitwise_xor(pairs_ref[2 * npairs + p], me)
        cell = j * n + o
        source = a * terms + j
        seen = seen_ref[cell]
        seen_ref[cell] = seen + 1
        before = second_ref[cell]
        place = jnp.where(seen == 2, spare + extra, before)
        first_ref[cell] = jnp.where(seen == 0, source, first_ref[cell])
        second_ref[cell] = jnp.where(seen == 0, before, jnp.where(seen == 1, source, place))
        dst_ref[ops] = place
        one_ref[ops] = before
        two_ref[ops] = source
        return extra + (seen == 2).astype(jnp.int32), ops + (seen >= 2).astype(jnp.int32)

    _, ops = lax.fori_loop(0, live_ref[0], pair, (jnp.int32(0), jnp.int32(0)))
    count_ref[0] = ops
    for copy in copies[4:]:
        copy.wait()

    for j in range(terms):
        high, low = halves(left_ref[j])
        for k, part in enumerate((high, low, high, low)):
            l4_ref[j, :, k * width:(k + 1) * width] = part
        high, low = halves(right_ref[j])
        for k in range(2):
            row = (k * terms + j) * width
            rr_ref[row:row + width, :width] = high
            rr_ref[row:row + width, width:] = low


def at_home(x):
    return pltpu.with_memory_space_constraint(x, pltpu.HBM)


def prep(n, me, fetch, store, pairs, live, vector, left_ops, right_ops):
    terms, width = left_ops.shape[:2]
    npairs = pairs.shape[0] // 3
    return pl.pallas_call(
        functools.partial(prep_kernel, n, terms * n + 1),
        out_shape=(
            jax.ShapeDtypeStruct((terms, width, 4 * width), jnp.bfloat16),
            jax.ShapeDtypeStruct((2 * terms * width, 2 * width), jnp.bfloat16),
            jax.ShapeDtypeStruct((sum(lengths(n, terms, npairs)),), jnp.int32),
            jax.ShapeDtypeStruct(vector.shape, jnp.float32),
        ),
        in_specs=[SMEM] + [pl.BlockSpec(memory_space=pltpu.HBM)] * 7,
        out_specs=[VMEM] * 2 + [SMEM, VMEM],
        scratch_shapes=[
            pltpu.SMEM((terms * n,), jnp.int32),
            pltpu.SMEM(fetch.shape, jnp.int32),
            pltpu.SMEM(store.shape, jnp.int32),
            pltpu.SMEM(pairs.shape, jnp.int32),
            pltpu.SMEM((1,), jnp.int32),
            pltpu.VMEM(left_ops.shape, jnp.float32),
            pltpu.VMEM(left_ops.shape, jnp.float32),
            pltpu.SemaphoreType.DMA((7,)),
        ],
        compiler_params=params(16),
        name="prep",
    )(me, at_home(fetch), at_home(store), at_home(pairs), live, at_home(vector), at_home(left_ops), at_home(right_ops))


def apply_kernel(n, npairs, over_rows, rows, start, table_ref, l4_ref, rr_ref, *refs):
    pieces, (near_ref, far_ref, row_ref, row_far_ref, column_ref, column_far_ref, square_ref, block, total) = refs[:n], refs[n:]
    terms, width = l4_ref.shape[:2]
    pick_ref, mine_ref, _, first_ref, second_ref, dst_ref, one_ref, two_ref, count_ref = parts(table_ref, n, terms, npairs)
    square = jnp.zeros((8, width), jnp.float32)
    product = jnp.zeros((8, width), jnp.float32)
    block[terms * n] = jnp.zeros((rows, width), jnp.float32)
    left = l4_ref[:, start:start + rows, :].reshape(terms * rows, 4 * width)
    for c in range(n // 2):
        columns = []
        for r in (2 * c, 2 * c + 1):
            high, low = halves(pieces[r][pick_ref[r]])
            columns.append(jnp.concatenate([high, high, low, low], axis=0))
            held = pieces[r][:, start:start + rows, :]
            square = square + tile_sum(held * held)
        both = jnp.dot(left, jnp.concatenate(columns, axis=1), preferred_element_type=jnp.float32)
        for k in range(2):
            at = (2 * c + k) * terms
            block[at:at + terms] = both[:, k * width:(k + 1) * width].reshape(terms, rows, width)
    square_ref[...] = square

    def add(i, carry):
        block[dst_ref[i]] = block[one_ref[i]] + block[two_ref[i]]
        return carry

    lax.fori_loop(0, count_ref[0], add, 0)
    late = 0
    for low_end in range(0, n, 4):
        for r in range(low_end, low_end + 4):
            for j in range(terms):
                at = j * n + r
                high, low = halves(block[first_ref[at]] + block[second_ref[at]])
                total[r, :, j * width:(j + 1) * width] = high
                total[r, :, (terms + j) * width:(terms + j + 1) * width] = low
        both = jnp.dot(total[low_end:low_end + 4].reshape(4 * rows, 2 * terms * width), rr_ref[...],
                       preferred_element_type=jnp.float32)
        slots = both[:, :width] + both[:, width:]
        for r in range(low_end, low_end + 4):
            slot = slots[(r - low_end) * rows:(r - low_end + 1) * rows]
            product = product + tile_sum(pieces[r][mine_ref[r], start:start + rows, :] * slot)
            g, core = divmod(r, 2)
            if g == 3:
                (column_far_ref if core else column_ref)[...] = slot
            elif g in over_rows:
                at = over_rows.index(g) * rows
                (row_far_ref if core else row_ref)[at:at + rows, :] = slot
            else:
                (far_ref if core else near_ref)[late * rows:(late + 1) * rows, :] = slot
                late += core
    for ref in (far_ref, row_ref, row_far_ref):
        ref[ref.shape[0] - 8:, :] = product


def apply(n, over_rows, rows, start, tables, pieces):
    terms, width = tables[0].shape[:2]
    npairs = (tables[2].shape[0] - sum(lengths(n, terms, 0))) // 3
    spare = npairs // 3
    late = n // 2 - 1 - len(over_rows)
    shape = lambda *dims: jax.ShapeDtypeStruct(dims, jnp.float32)
    return pl.pallas_call(
        functools.partial(apply_kernel, n, npairs, over_rows, rows, start),
        out_shape=(shape(late * rows, width), shape(late * rows + 8, width)) + (shape(len(over_rows) * rows + 8, width),) * 2
        + (shape(rows, width),) * 2 + (shape(8, width),),
        in_specs=[SMEM] + [VMEM] * (2 + n),
        out_specs=[VMEM] * 7,
        scratch_shapes=[
            pltpu.VMEM((terms * n + 1 + spare, rows, width), jnp.float32),
            pltpu.VMEM((n, rows, 2 * terms * width), jnp.bfloat16),
        ],
        compiler_params=params(32 if n <= 16 else 56),
        name="apply",
    )(tables[2], *tables[:2], *pieces)


def joined(parts, count):
    if len(parts) == 1:
        return parts[0]
    height, width = parts[0].shape
    end = height // (8 * count) * 8 * count
    whole = jnp.concatenate([x[:end].reshape(count, -1, width) for x in parts], axis=1).reshape(-1, width)
    return whole if end == height else jnp.concatenate([whole, sum(x[end:] for x in parts)])


def swapped(x, k):
    n = lax.axis_size("term")
    return lax.ppermute(x, "term", [(i, i ^ k) for i in range(n)])


def local(kernel, name, out_shape, scalars, arrays):
    many = isinstance(out_shape, tuple)
    return pl.pallas_call(
        kernel,
        out_shape=out_shape,
        in_specs=[SMEM] * len(scalars) + [VMEM] * len(arrays),
        out_specs=[VMEM] * len(out_shape) if many else VMEM,
        compiler_params=params(16),
        name=name,
    )(*scalars, *arrays)


def fold_kernel(n, late, over_rows, table_ref, near_ref, far_in, far_ref, row_ref, row_far_ref, column_ref, column_far_ref,
                own_ref, step_ref, *send_refs):
    width = near_ref.shape[1]
    chips = n // 2
    place_ref = Part(table_ref, 2 * n)
    end = len(late) * width
    over = len(over_rows) * width
    tile = far_in[end:] + far_ref[end:] + row_ref[over:] + row_far_ref[over:]
    for i, g in enumerate(late):
        come = [(0, near_ref, i), (1, far_ref, i)]
        if g == 1:
            come += [(4, column_ref, 0), (5, column_far_ref, 0)]
        if g + 1 in over_rows:
            come += [(2, row_ref, over_rows.index(g + 1)), (3, row_far_ref, over_rows.index(g + 1))]
        for b in range(2):
            block = sum(ref[at * width:(at + 1) * width] * (place_ref[q * chips + g] == b).astype(jnp.float32)
                        for q, ref, at in come)
            if g == 0:
                own_ref[b] = block
            elif g == 1:
                step_ref[b] = block
            else:
                send_refs[g // 2 - 1][b * width:(b + 1) * width] = block
    for send_ref in send_refs:
        send_ref[2 * width:] = tile


def landed(own_ref, step_ref, refs):
    width = own_ref.shape[2]
    sent, came = refs[0], refs[1:]
    tile = sent[2 * width:]
    for ref in came:
        tile = tile + ref[2 * width:]
    sums = []
    for b in range(2):
        total = own_ref[b] + step_ref[b]
        for ref in came:
            total = total + ref[b * width:(b + 1) * width]
        sums.append(total)
    return sums, jnp.sum(tile)


def step_kernel(own_ref, step_ref, square_ref, vector_ref, precond_ref, *refs):
    out_ref = refs[-1]
    sigma, product = landed(own_ref, step_ref, refs[:-1])
    theta = product / jnp.sum(square_ref[...])
    for b in range(2):
        v = vector_ref[b]
        out_ref[b] = v - precond_ref[b] * (sigma[b] - theta * v)


def last_kernel(cells, own_ref, step_ref, square_ref, vector_ref, precond_ref, *refs):
    residual_ref, out_ref, tile_ref = refs[-3:]
    sigma, product = landed(own_ref, step_ref, refs[:-3])
    square = jnp.sum(square_ref[...])
    theta = product / square
    scale = 1.0 / jnp.sqrt(square / cells + 1e-06)
    tile = jnp.zeros(tile_ref.shape, jnp.float32)
    for b in range(2):
        v = vector_ref[b]
        residual = (sigma[b] - theta * v) * scale
        residual_ref[b] = residual
        corrected = v * scale - precond_ref[b] * residual
        out_ref[b] = corrected
        tile = tile + tile_sum(corrected * corrected)
    tile_ref[...] = tile


def norm_kernel(cells, corrected_ref, tiles_ref, out_ref):
    scale = 1.0 / jnp.sqrt(jnp.sum(jnp.sum(tiles_ref[...], axis=0)) / cells + 1e-06)
    out_ref[...] = corrected_ref[...] * scale


def scattered(n, tables, pieces):
    width = pieces[0].shape[1]
    chips = n // 2
    rows = width if n <= 16 else width // 4
    over_rows = list(range(chips - 1, 3, -2))
    late = [g for g in range(chips) if g != 3 and g not in over_rows]
    shape = lambda *dims: jax.ShapeDtypeStruct(dims, jnp.float32)
    runs = [apply(n, over_rows, rows, start, tables, pieces) for start in range(0, width, rows)]
    counts = (len(late), len(late), len(over_rows), len(over_rows), 1, 1)
    near, far, row, row_far, column, column_far = (joined([x[i] for x in runs], k) for i, k in enumerate(counts))
    square = functools.reduce(jnp.add, [x[6] for x in runs])
    own, step, *sends = local(
        functools.partial(fold_kernel, n, late, over_rows), "fold",
        (shape(2, width, width),) * 2 + (shape(2 * width + 8, width),) * (chips // 2 - 1), tables[2:3],
        (near, far, swapped(far, CORE), swapped(row, ROW), swapped(row_far, ROW + CORE), swapped(column, COLUMN),
         swapped(column_far, COLUMN + CORE)))
    came = [swapped(x, 2 * ROW * (i + 1)) for i, x in reversed(list(enumerate(sends)))]
    return square, (own, swapped(step, ROW)), [sends[0], *came]


def gathered(n, x, held=None):
    pieces = {0: x}
    for k in reversed(range(8, n, 4)):
        pieces[k] = swapped(x, k)
    pieces[ROW] = swapped(x, ROW)
    pieces[COLUMN] = swapped(x, COLUMN)
    pieces[COLUMN + ROW] = swapped(x, COLUMN + ROW)
    for k in reversed(range(8, n, 4)):
        pieces[k + ROW] = swapped(pieces[k], ROW)
    late = [0, 8, n - 4, n - 4 + ROW]
    pieces.update(zip(late, lax.optimization_barrier([pieces[k] for k in late])))
    if held is not None:
        pieces[COLUMN], pieces[0] = lax.optimization_barrier((pieces[COLUMN], held))
    for k in range(0, n, 2):
        pieces[k + CORE] = swapped(pieces[k], CORE)
    return [pieces[k] for k in range(n)]


def shards(wavefn, left_ops, right_ops, precond, fetch_map, store_map, pair_list, live_count):
    n = lax.axis_size("term")
    me = lax.axis_index("term").astype(jnp.int32).reshape(1)
    width = wavefn.shape[1]
    cells = wavefn.size * n
    *tables, held = prep(n, me, fetch_map, store_map, pair_list[0].T.reshape(-1), live_count, wavefn, left_ops, right_ops)
    block = jax.ShapeDtypeStruct(wavefn.shape, jnp.float32)
    tile = jax.ShapeDtypeStruct((8, width), jnp.float32)
    vector = wavefn
    for iteration in range(ITERS):
        pieces = gathered(n, vector, held if iteration == 0 else None)
        vector = pieces[0]
        square, sums, parts = scattered(n, tables, pieces)
        arrays = (*sums, square, vector, precond, *parts)
        if iteration < ITERS - 1:
            vector = local(step_kernel, "step", block, (), arrays)
    residual, corrected, partial = local(
        functools.partial(last_kernel, cells), "last", (block, block, tile), (), arrays)
    tiles = lax.all_to_all(jnp.broadcast_to(partial[None], (n, 8, width)), "term",
                           split_axis=0, concat_axis=0, tiled=True)
    return local(functools.partial(norm_kernel, cells), "norm", block, (), (corrected, tiles)), residual


def solution(mesh):
    field = P(("group", "term"), None, None)
    return jax.shard_map(
        shards,
        mesh=mesh,
        in_specs=(field, field, field, field, P(), P(), P("term", None, None), P("term")),
        out_specs=(field, field),
        check_vma=False,
    )
```

```python
import functools

import jax
import jax.numpy as jnp
from jax import lax
from jax.experimental import pallas as pl
from jax.experimental.pallas import tpu as pltpu
from jax.sharding import PartitionSpec as P

ITERS = 2
CORE, ROW, COLUMN = 1, 2, 4
SENDERS = 6
SMEM = pl.BlockSpec(memory_space=pltpu.SMEM)
VMEM = pl.BlockSpec(memory_space=pltpu.VMEM)


def params(mebibytes):
    return pltpu.CompilerParams(vmem_limit_bytes=mebibytes * 2**20)


def halves(x):
    high = x.astype(jnp.bfloat16)
    return high, (x - high.astype(jnp.float32)).astype(jnp.bfloat16)


def tile_sum(x):
    return jnp.sum(x.reshape(-1, 8, x.shape[-1]), axis=0)


class Part:
    def __init__(self, ref, start):
        self.ref, self.start = ref, start

    def __getitem__(self, i):
        return self.ref[self.start + i]

    def __setitem__(self, i, value):
        self.ref[self.start + i] = value


def lengths(n, terms, npairs):
    return n, n, SENDERS * n // 2, terms * n, terms * n, npairs, npairs, npairs, 1


def parts(ref, n, terms, npairs):
    sizes = lengths(n, terms, npairs)
    return [Part(ref, sum(sizes[:i])) for i in range(len(sizes))]


def prep_kernel(n, spare, me_ref, fetch_in, store_in, pairs_in, live_in, vector_in, left_in, right_in, l4_ref, rr_ref,
                table_ref, vector_ref,
                seen_ref, fetch_ref, store_ref, pairs_ref, live_ref, left_ref, right_ref, sems):
    copies = [pltpu.make_async_copy(source, target, sems.at[i]) for i, (source, target) in enumerate((
        (fetch_in, fetch_ref), (store_in, store_ref), (pairs_in, pairs_ref), (live_in, live_ref),
        (left_in, left_ref), (right_in, right_ref), (vector_in, vector_ref)))]
    for copy in copies:
        copy.start()
    me = me_ref[0]
    terms = left_ref.shape[0]
    width = left_ref.shape[1]
    zero = terms * n
    npairs = pairs_ref.shape[0] // 3
    pick_ref, mine_ref, place_ref, first_ref, second_ref, dst_ref, one_ref, two_ref, count_ref = parts(
        table_ref, n, terms, npairs)

    def clear(cell, carry):
        first_ref[cell] = zero
        second_ref[cell] = zero
        seen_ref[cell] = 0
        return carry

    lax.fori_loop(0, terms * n, clear, 0, unroll=8)
    for copy in copies[:4]:
        copy.wait()

    def relative(r, carry):
        device = lax.bitwise_xor(me, r)
        pick_ref[r] = fetch_ref[device, me]
        mine_ref[r] = store_ref[me, device]
        return carry

    lax.fori_loop(0, n, relative, 0)

    def chip(g, carry):
        for q in range(SENDERS):
            place_ref[q * (n // 2) + g] = store_ref[lax.bitwise_xor(me, q), lax.bitwise_xor(me, 2 * g)]
        return carry

    lax.fori_loop(0, n // 2, chip, 0)

    def pair(p, carry):
        extra, ops = carry
        a = lax.bitwise_xor(pairs_ref[p], me)
        j = pairs_ref[npairs + p]
        o = lax.bitwise_xor(pairs_ref[2 * npairs + p], me)
        cell = j * n + o
        source = a * terms + j
        seen = seen_ref[cell]
        seen_ref[cell] = seen + 1
        before = second_ref[cell]
        place = jnp.where(seen == 2, spare + extra, before)
        first_ref[cell] = jnp.where(seen == 0, source, first_ref[cell])
        second_ref[cell] = jnp.where(seen == 0, before, jnp.where(seen == 1, source, place))
        dst_ref[ops] = place
        one_ref[ops] = before
        two_ref[ops] = source
        return extra + (seen == 2).astype(jnp.int32), ops + (seen >= 2).astype(jnp.int32)

    _, ops = lax.fori_loop(0, live_ref[0], pair, (jnp.int32(0), jnp.int32(0)))
    count_ref[0] = ops
    for copy in copies[4:]:
        copy.wait()

    for j in range(terms):
        high, low = halves(left_ref[j])
        for k, part in enumerate((high, low, high, low)):
            l4_ref[j, :, k * width:(k + 1) * width] = part
        high, low = halves(right_ref[j])
        for k in range(2):
            row = (k * terms + j) * width
            rr_ref[row:row + width, :width] = high
            rr_ref[row:row + width, width:] = low


def at_home(x):
    return pltpu.with_memory_space_constraint(x, pltpu.HBM)


def prep(n, me, fetch, store, pairs, live, vector, left_ops, right_ops):
    terms, width = left_ops.shape[:2]
    npairs = pairs.shape[0] // 3
    return pl.pallas_call(
        functools.partial(prep_kernel, n, terms * n + 1),
        out_shape=(
            jax.ShapeDtypeStruct((terms, width, 4 * width), jnp.bfloat16),
            jax.ShapeDtypeStruct((2 * terms * width, 2 * width), jnp.bfloat16),
            jax.ShapeDtypeStruct((sum(lengths(n, terms, npairs)),), jnp.int32),
            jax.ShapeDtypeStruct(vector.shape, jnp.float32),
        ),
        in_specs=[SMEM] + [pl.BlockSpec(memory_space=pltpu.HBM)] * 7,
        out_specs=[VMEM] * 2 + [SMEM, VMEM],
        scratch_shapes=[
            pltpu.SMEM((terms * n,), jnp.int32),
            pltpu.SMEM(fetch.shape, jnp.int32),
            pltpu.SMEM(store.shape, jnp.int32),
            pltpu.SMEM(pairs.shape, jnp.int32),
            pltpu.SMEM((1,), jnp.int32),
            pltpu.VMEM(left_ops.shape, jnp.float32),
            pltpu.VMEM(left_ops.shape, jnp.float32),
            pltpu.SemaphoreType.DMA((7,)),
        ],
        compiler_params=params(16),
        name="prep",
    )(me, at_home(fetch), at_home(store), at_home(pairs), live, at_home(vector), at_home(left_ops), at_home(right_ops))


def apply_kernel(n, npairs, over_rows, rows, start, table_ref, l4_ref, rr_ref, *refs):
    pieces, (near_ref, far_ref, row_ref, row_far_ref, column_ref, column_far_ref, square_ref, block, total) = refs[:n], refs[n:]
    terms, width = l4_ref.shape[:2]
    pick_ref, mine_ref, _, first_ref, second_ref, dst_ref, one_ref, two_ref, count_ref = parts(table_ref, n, terms, npairs)
    square = jnp.zeros((8, width), jnp.float32)
    product = jnp.zeros((8, width), jnp.float32)
    block[terms * n] = jnp.zeros((rows, width), jnp.float32)
    left = l4_ref[:, start:start + rows, :].reshape(terms * rows, 4 * width)
    for c in range(n // 2):
        columns = []
        for r in (2 * c, 2 * c + 1):
            high, low = halves(pieces[r][pick_ref[r]])
            columns.append(jnp.concatenate([high, high, low, low], axis=0))
            held = pieces[r][:, start:start + rows, :]
            square = square + tile_sum(held * held)
        both = jnp.dot(left, jnp.concatenate(columns, axis=1), preferred_element_type=jnp.float32)
        for k in range(2):
            at = (2 * c + k) * terms
            block[at:at + terms] = both[:, k * width:(k + 1) * width].reshape(terms, rows, width)
    square_ref[...] = square

    def add(i, carry):
        block[dst_ref[i]] = block[one_ref[i]] + block[two_ref[i]]
        return carry

    lax.fori_loop(0, count_ref[0], add, 0)
    late = 0
    for low_end in range(0, n, 4):
        for r in range(low_end, low_end + 4):
            for j in range(terms):
                at = j * n + r
                high, low = halves(block[first_ref[at]] + block[second_ref[at]])
                total[r, :, j * width:(j + 1) * width] = high
                total[r, :, (terms + j) * width:(terms + j + 1) * width] = low
        both = jnp.dot(total[low_end:low_end + 4].reshape(4 * rows, 2 * terms * width), rr_ref[...],
                       preferred_element_type=jnp.float32)
        slots = both[:, :width] + both[:, width:]
        for r in range(low_end, low_end + 4):
            slot = slots[(r - low_end) * rows:(r - low_end + 1) * rows]
            product = product + tile_sum(pieces[r][mine_ref[r], start:start + rows, :] * slot)
            g, core = divmod(r, 2)
            if g == 3:
                (column_far_ref if core else column_ref)[...] = slot
            elif g in over_rows:
                at = over_rows.index(g) * rows
                (row_far_ref if core else row_ref)[at:at + rows, :] = slot
            else:
                (far_ref if core else near_ref)[late * rows:(late + 1) * rows, :] = slot
                late += core
    for ref in (far_ref, row_ref, row_far_ref):
        ref[ref.shape[0] - 8:, :] = product


def apply(n, over_rows, rows, start, tables, pieces):
    terms, width = tables[0].shape[:2]
    npairs = (tables[2].shape[0] - sum(lengths(n, terms, 0))) // 3
    spare = npairs // 3
    late = n // 2 - 1 - len(over_rows)
    shape = lambda *dims: jax.ShapeDtypeStruct(dims, jnp.float32)
    return pl.pallas_call(
        functools.partial(apply_kernel, n, npairs, over_rows, rows, start),
        out_shape=(shape(late * rows, width), shape(late * rows + 8, width)) + (shape(len(over_rows) * rows + 8, width),) * 2
        + (shape(rows, width),) * 2 + (shape(8, width),),
        in_specs=[SMEM] + [VMEM] * (2 + n),
        out_specs=[VMEM] * 7,
        scratch_shapes=[
            pltpu.VMEM((terms * n + 1 + spare, rows, width), jnp.float32),
            pltpu.VMEM((n, rows, 2 * terms * width), jnp.bfloat16),
        ],
        compiler_params=params(32 if n <= 16 else 56),
        name="apply",
    )(tables[2], *tables[:2], *pieces)


def joined(parts, count):
    if len(parts) == 1:
        return parts[0]
    height, width = parts[0].shape
    end = height // (8 * count) * 8 * count
    whole = jnp.concatenate([x[:end].reshape(count, -1, width) for x in parts], axis=1).reshape(-1, width)
    return whole if end == height else jnp.concatenate([whole, sum(x[end:] for x in parts)])


def swapped(x, k):
    n = lax.axis_size("term")
    return lax.ppermute(x, "term", [(i, i ^ k) for i in range(n)])


def local(kernel, name, out_shape, scalars, arrays):
    many = isinstance(out_shape, tuple)
    return pl.pallas_call(
        kernel,
        out_shape=out_shape,
        in_specs=[SMEM] * len(scalars) + [VMEM] * len(arrays),
        out_specs=[VMEM] * len(out_shape) if many else VMEM,
        compiler_params=params(16),
        name=name,
    )(*scalars, *arrays)


def fold_kernel(n, late, over_rows, table_ref, near_ref, far_in, far_ref, row_ref, row_far_ref, column_ref, column_far_ref,
                own_ref, step_ref, *send_refs):
    width = near_ref.shape[1]
    chips = n // 2
    place_ref = Part(table_ref, 2 * n)
    end = len(late) * width
    over = len(over_rows) * width
    tile = far_in[end:] + far_ref[end:] + row_ref[over:] + row_far_ref[over:]
    for i, g in enumerate(late):
        come = [(0, near_ref, i), (1, far_ref, i)]
        if g == 1:
            come += [(4, column_ref, 0), (5, column_far_ref, 0)]
        if g + 1 in over_rows:
            come += [(2, row_ref, over_rows.index(g + 1)), (3, row_far_ref, over_rows.index(g + 1))]
        for b in range(2):
            block = sum(ref[at * width:(at + 1) * width] * (place_ref[q * chips + g] == b).astype(jnp.float32)
                        for q, ref, at in come)
            if g == 0:
                own_ref[b] = block
            elif g == 1:
                step_ref[b] = block
            else:
                send_refs[g // 2 - 1][b * width:(b + 1) * width] = block
    for send_ref in send_refs:
        send_ref[2 * width:] = tile


def landed(own_ref, step_ref, refs):
    width = own_ref.shape[2]
    sent, came = refs[0], refs[1:]
    tile = sent[2 * width:]
    for ref in came:
        tile = tile + ref[2 * width:]
    sums = []
    for b in range(2):
        total = own_ref[b] + step_ref[b]
        for ref in came:
            total = total + ref[b * width:(b + 1) * width]
        sums.append(total)
    return sums, jnp.sum(tile)


def step_kernel(own_ref, step_ref, square_ref, vector_ref, precond_ref, *refs):
    out_ref = refs[-1]
    sigma, product = landed(own_ref, step_ref, refs[:-1])
    theta = product / jnp.sum(square_ref[...])
    for b in range(2):
        v = vector_ref[b]
        out_ref[b] = v - precond_ref[b] * (sigma[b] - theta * v)


def last_kernel(cells, own_ref, step_ref, square_ref, vector_ref, precond_ref, *refs):
    residual_ref, out_ref, tile_ref = refs[-3:]
    sigma, product = landed(own_ref, step_ref, refs[:-3])
    square = jnp.sum(square_ref[...])
    theta = product / square
    scale = 1.0 / jnp.sqrt(square / cells + 1e-06)
    tile = jnp.zeros(tile_ref.shape, jnp.float32)
    for b in range(2):
        v = vector_ref[b]
        residual = (sigma[b] - theta * v) * scale
        residual_ref[b] = residual
        corrected = v * scale - precond_ref[b] * residual
        out_ref[b] = corrected
        tile = tile + tile_sum(corrected * corrected)
    tile_ref[...] = tile


def norm_kernel(cells, corrected_ref, tiles_ref, out_ref):
    scale = 1.0 / jnp.sqrt(jnp.sum(jnp.sum(tiles_ref[...], axis=0)) / cells + 1e-06)
    out_ref[...] = corrected_ref[...] * scale


def scattered(n, tables, pieces, last):
    width = pieces[0].shape[1]
    chips = n // 2
    rows = width if n <= 16 else width // 4
    over_rows = list(range(chips - 1, 3, -2))
    late = [g for g in range(chips) if g != 3 and g not in over_rows]
    shape = lambda *dims: jax.ShapeDtypeStruct(dims, jnp.float32)
    runs = [apply(n, over_rows, rows, start, tables, pieces) for start in range(0, width, rows)]
    counts = (len(late), len(late), len(over_rows), len(over_rows), 1, 1)
    near, far, row, row_far, column, column_far = (joined([x[i] for x in runs], k) for i, k in enumerate(counts))
    square = functools.reduce(jnp.add, [x[6] for x in runs])
    own, step, *sends = local(
        functools.partial(fold_kernel, n, late, over_rows), "fold",
        (shape(2, width, width),) * 2 + (shape(2 * width + 8, width),) * (chips // 2 - 1), tables[2:3],
        (near, far, swapped(far, CORE), swapped(row, ROW), swapped(row_far, ROW + CORE), swapped(column, COLUMN),
         swapped(column_far, COLUMN + CORE)))
    order = range(len(sends))
    came = [swapped(sends[i], 2 * ROW * (i + 1)) for i in ((*order[1:], 0) if last else order[::-1])]
    return square, (own, swapped(step, ROW)), [sends[0], *came]


def gathered(n, x, held=None):
    pieces = {0: x}
    for k in reversed(range(8, n, 4)):
        pieces[k] = swapped(x, k)
    pieces[ROW] = swapped(x, ROW)
    pieces[COLUMN] = swapped(x, COLUMN)
    if held is not None:
        pieces[n - 4], pieces[0] = lax.optimization_barrier((pieces[n - 4], held))
    for k in reversed(range(8, n, 4)):
        pieces[k + ROW] = swapped(pieces[k], ROW)
    pieces[COLUMN + ROW] = swapped(pieces[ROW], COLUMN)
    for k in range(0, n, 2):
        pieces[k + CORE] = swapped(pieces[k], CORE)
    return [pieces[k] for k in range(n)]


def shards(wavefn, left_ops, right_ops, precond, fetch_map, store_map, pair_list, live_count):
    n = lax.axis_size("term")
    me = lax.axis_index("term").astype(jnp.int32).reshape(1)
    width = wavefn.shape[1]
    cells = wavefn.size * n
    *tables, held = prep(n, me, fetch_map, store_map, pair_list[0].T.reshape(-1), live_count, wavefn, left_ops, right_ops)
    block = jax.ShapeDtypeStruct(wavefn.shape, jnp.float32)
    tile = jax.ShapeDtypeStruct((8, width), jnp.float32)
    vector = wavefn
    for iteration in range(ITERS):
        pieces = gathered(n, vector, held if iteration == 0 else None)
        vector = pieces[0]
        square, sums, parts = scattered(n, tables, pieces, iteration == ITERS - 1)
        arrays = (*sums, square, vector, precond, *parts)
        if iteration < ITERS - 1:
            vector = local(step_kernel, "step", block, (), arrays)
    residual, corrected, partial = local(
        functools.partial(last_kernel, cells), "last", (block, block, tile), (), arrays)
    tiles = lax.all_to_all(jnp.broadcast_to(partial[None], (n, 8, width)), "term",
                           split_axis=0, concat_axis=0, tiled=True)
    return local(functools.partial(norm_kernel, cells), "norm", block, (), (corrected, tiles)), residual


def solution(mesh):
    field = P(("group", "term"), None, None)
    return jax.shard_map(
        shards,
        mesh=mesh,
        in_specs=(field, field, field, field, P(), P(), P("term", None, None), P("term")),
        out_specs=(field, field),
        check_vma=False,
    )
```

```python
import functools

import jax
import jax.numpy as jnp
from jax import lax
from jax.experimental import pallas as pl
from jax.experimental.pallas import tpu as pltpu
from jax.sharding import PartitionSpec as P

ITERS = 2
CORE, ROW, COLUMN = 1, 2, 4
SENDERS = 6
SMEM = pl.BlockSpec(memory_space=pltpu.SMEM)
VMEM = pl.BlockSpec(memory_space=pltpu.VMEM)


def params(mebibytes):
    return pltpu.CompilerParams(vmem_limit_bytes=mebibytes * 2**20)


def halves(x):
    high = x.astype(jnp.bfloat16)
    return high, (x - high.astype(jnp.float32)).astype(jnp.bfloat16)


def tile_sum(x):
    return jnp.sum(x.reshape(-1, 8, x.shape[-1]), axis=0)


class Part:
    def __init__(self, ref, start):
        self.ref, self.start = ref, start

    def __getitem__(self, i):
        return self.ref[self.start + i]

    def __setitem__(self, i, value):
        self.ref[self.start + i] = value


def lengths(n, terms, npairs):
    return n, n, SENDERS * n // 2, terms * n, terms * n, npairs, npairs, npairs, 1


def parts(ref, n, terms, npairs):
    sizes = lengths(n, terms, npairs)
    return [Part(ref, sum(sizes[:i])) for i in range(len(sizes))]


def prep_kernel(n, spare, me_ref, fetch_in, store_in, pairs_in, live_in, vector_in, left_in, right_in, l4_ref, rr_ref,
                table_ref, vector_ref,
                seen_ref, fetch_ref, store_ref, pairs_ref, live_ref, left_ref, right_ref, sems):
    copies = [pltpu.make_async_copy(source, target, sems.at[i]) for i, (source, target) in enumerate((
        (fetch_in, fetch_ref), (store_in, store_ref), (pairs_in, pairs_ref), (live_in, live_ref),
        (left_in, left_ref), (right_in, right_ref), (vector_in, vector_ref)))]
    for copy in copies:
        copy.start()
    me = me_ref[0]
    terms = left_ref.shape[0]
    width = left_ref.shape[1]
    zero = terms * n
    npairs = pairs_ref.shape[0] // 3
    pick_ref, mine_ref, place_ref, first_ref, second_ref, dst_ref, one_ref, two_ref, count_ref = parts(
        table_ref, n, terms, npairs)

    def clear(cell, carry):
        first_ref[cell] = zero
        second_ref[cell] = zero
        seen_ref[cell] = 0
        return carry

    lax.fori_loop(0, terms * n, clear, 0, unroll=8)
    for copy in copies[:4]:
        copy.wait()

    def relative(r, carry):
        device = lax.bitwise_xor(me, r)
        pick_ref[r] = fetch_ref[device, me]
        mine_ref[r] = store_ref[me, device]
        return carry

    lax.fori_loop(0, n, relative, 0)

    def chip(g, carry):
        for q in range(SENDERS):
            place_ref[q * (n // 2) + g] = store_ref[lax.bitwise_xor(me, q), lax.bitwise_xor(me, 2 * g)]
        return carry

    lax.fori_loop(0, n // 2, chip, 0)

    def pair(p, carry):
        extra, ops = carry
        a = lax.bitwise_xor(pairs_ref[p], me)
        j = pairs_ref[npairs + p]
        o = lax.bitwise_xor(pairs_ref[2 * npairs + p], me)
        cell = j * n + o
        source = a * terms + j
        seen = seen_ref[cell]
        seen_ref[cell] = seen + 1
        before = second_ref[cell]
        place = jnp.where(seen == 2, spare + extra, before)
        first_ref[cell] = jnp.where(seen == 0, source, first_ref[cell])
        second_ref[cell] = jnp.where(seen == 0, before, jnp.where(seen == 1, source, place))
        dst_ref[ops] = place
        one_ref[ops] = before
        two_ref[ops] = source
        return extra + (seen == 2).astype(jnp.int32), ops + (seen >= 2).astype(jnp.int32)

    _, ops = lax.fori_loop(0, live_ref[0], pair, (jnp.int32(0), jnp.int32(0)))
    count_ref[0] = ops
    for copy in copies[4:]:
        copy.wait()

    for j in range(terms):
        high, low = halves(left_ref[j])
        for k, part in enumerate((high, low, high, low)):
            l4_ref[j, :, k * width:(k + 1) * width] = part
        high, low = halves(right_ref[j])
        for k in range(2):
            row = (k * terms + j) * width
            rr_ref[row:row + width, :width] = high
            rr_ref[row:row + width, width:] = low


def at_home(x):
    return pltpu.with_memory_space_constraint(x, pltpu.HBM)


def prep(n, me, fetch, store, pairs, live, vector, left_ops, right_ops):
    terms, width = left_ops.shape[:2]
    npairs = pairs.shape[0] // 3
    return pl.pallas_call(
        functools.partial(prep_kernel, n, terms * n + 1),
        out_shape=(
            jax.ShapeDtypeStruct((terms, width, 4 * width), jnp.bfloat16),
            jax.ShapeDtypeStruct((2 * terms * width, 2 * width), jnp.bfloat16),
            jax.ShapeDtypeStruct((sum(lengths(n, terms, npairs)),), jnp.int32),
            jax.ShapeDtypeStruct(vector.shape, jnp.float32),
        ),
        in_specs=[SMEM] + [pl.BlockSpec(memory_space=pltpu.HBM)] * 7,
        out_specs=[VMEM] * 2 + [SMEM, VMEM],
        scratch_shapes=[
            pltpu.SMEM((terms * n,), jnp.int32),
            pltpu.SMEM(fetch.shape, jnp.int32),
            pltpu.SMEM(store.shape, jnp.int32),
            pltpu.SMEM(pairs.shape, jnp.int32),
            pltpu.SMEM((1,), jnp.int32),
            pltpu.VMEM(left_ops.shape, jnp.float32),
            pltpu.VMEM(left_ops.shape, jnp.float32),
            pltpu.SemaphoreType.DMA((7,)),
        ],
        compiler_params=params(16),
        name="prep",
    )(me, at_home(fetch), at_home(store), at_home(pairs), live, at_home(vector), at_home(left_ops), at_home(right_ops))


def apply_kernel(n, npairs, over_rows, rows, start, table_ref, l4_ref, rr_ref, *refs):
    pieces, (near_ref, far_ref, row_ref, row_far_ref, column_ref, column_far_ref, square_ref, block, total) = refs[:n], refs[n:]
    terms, width = l4_ref.shape[:2]
    pick_ref, mine_ref, _, first_ref, second_ref, dst_ref, one_ref, two_ref, count_ref = parts(table_ref, n, terms, npairs)
    square = jnp.zeros((8, width), jnp.float32)
    product = jnp.zeros((8, width), jnp.float32)
    block[terms * n] = jnp.zeros((rows, width), jnp.float32)
    left = l4_ref[:, start:start + rows, :].reshape(terms * rows, 4 * width)
    for c in range(n // 2):
        columns = []
        for r in (2 * c, 2 * c + 1):
            high, low = halves(pieces[r][pick_ref[r]])
            columns.append(jnp.concatenate([high, high, low, low], axis=0))
            held = pieces[r][:, start:start + rows, :]
            square = square + tile_sum(held * held)
        both = jnp.dot(left, jnp.concatenate(columns, axis=1), preferred_element_type=jnp.float32)
        for k in range(2):
            at = (2 * c + k) * terms
            block[at:at + terms] = both[:, k * width:(k + 1) * width].reshape(terms, rows, width)
    square_ref[...] = square

    def add(i, carry):
        block[dst_ref[i]] = block[one_ref[i]] + block[two_ref[i]]
        return carry

    lax.fori_loop(0, count_ref[0], add, 0)
    late = 0
    for low_end in range(0, n, 4):
        for r in range(low_end, low_end + 4):
            for j in range(terms):
                at = j * n + r
                high, low = halves(block[first_ref[at]] + block[second_ref[at]])
                total[r, :, j * width:(j + 1) * width] = high
                total[r, :, (terms + j) * width:(terms + j + 1) * width] = low
        both = jnp.dot(total[low_end:low_end + 4].reshape(4 * rows, 2 * terms * width), rr_ref[...],
                       preferred_element_type=jnp.float32)
        slots = both[:, :width] + both[:, width:]
        for r in range(low_end, low_end + 4):
            slot = slots[(r - low_end) * rows:(r - low_end + 1) * rows]
            product = product + tile_sum(pieces[r][mine_ref[r], start:start + rows, :] * slot)
            g, core = divmod(r, 2)
            if g == 3:
                (column_far_ref if core else column_ref)[...] = slot
            elif g in over_rows:
                at = over_rows.index(g) * rows
                (row_far_ref if core else row_ref)[at:at + rows, :] = slot
            else:
                (far_ref if core else near_ref)[late * rows:(late + 1) * rows, :] = slot
                late += core
    for ref in (far_ref, row_ref, row_far_ref):
        ref[ref.shape[0] - 8:, :] = product


def apply(n, over_rows, rows, start, tables, pieces):
    terms, width = tables[0].shape[:2]
    npairs = (tables[2].shape[0] - sum(lengths(n, terms, 0))) // 3
    spare = npairs // 3
    late = n // 2 - 1 - len(over_rows)
    shape = lambda *dims: jax.ShapeDtypeStruct(dims, jnp.float32)
    return pl.pallas_call(
        functools.partial(apply_kernel, n, npairs, over_rows, rows, start),
        out_shape=(shape(late * rows, width), shape(late * rows + 8, width)) + (shape(len(over_rows) * rows + 8, width),) * 2
        + (shape(rows, width),) * 2 + (shape(8, width),),
        in_specs=[SMEM] + [VMEM] * (2 + n),
        out_specs=[VMEM] * 7,
        scratch_shapes=[
            pltpu.VMEM((terms * n + 1 + spare, rows, width), jnp.float32),
            pltpu.VMEM((n, rows, 2 * terms * width), jnp.bfloat16),
        ],
        compiler_params=params(32 if n <= 16 else 56),
        name="apply",
    )(tables[2], *tables[:2], *pieces)


def joined(parts, count):
    if len(parts) == 1:
        return parts[0]
    height, width = parts[0].shape
    end = height // (8 * count) * 8 * count
    whole = jnp.concatenate([x[:end].reshape(count, -1, width) for x in parts], axis=1).reshape(-1, width)
    return whole if end == height else jnp.concatenate([whole, sum(x[end:] for x in parts)])


def swapped(x, k):
    n = lax.axis_size("term")
    return lax.ppermute(x, "term", [(i, i ^ k) for i in range(n)])


def local(kernel, name, out_shape, scalars, arrays):
    many = isinstance(out_shape, tuple)
    return pl.pallas_call(
        kernel,
        out_shape=out_shape,
        in_specs=[SMEM] * len(scalars) + [VMEM] * len(arrays),
        out_specs=[VMEM] * len(out_shape) if many else VMEM,
        compiler_params=params(16),
        name=name,
    )(*scalars, *arrays)


def fold_kernel(n, late, over_rows, table_ref, near_ref, far_in, far_ref, row_ref, row_far_ref, column_ref, column_far_ref,
                own_ref, step_ref, *send_refs):
    width = near_ref.shape[1]
    chips = n // 2
    place_ref = Part(table_ref, 2 * n)
    end = len(late) * width
    over = len(over_rows) * width
    tile = far_in[end:] + far_ref[end:] + row_ref[over:] + row_far_ref[over:]
    for i, g in enumerate(late):
        come = [(0, near_ref, i), (1, far_ref, i)]
        if g == 1:
            come += [(4, column_ref, 0), (5, column_far_ref, 0)]
        if g + 1 in over_rows:
            come += [(2, row_ref, over_rows.index(g + 1)), (3, row_far_ref, over_rows.index(g + 1))]
        for b in range(2):
            block = sum(ref[at * width:(at + 1) * width] * (place_ref[q * chips + g] == b).astype(jnp.float32)
                        for q, ref, at in come)
            if g == 0:
                own_ref[b] = block
            elif g == 1:
                step_ref[b] = block
            else:
                send_refs[g // 2 - 1][b * width:(b + 1) * width] = block
    for send_ref in send_refs:
        send_ref[2 * width:] = tile


def landed(own_ref, step_ref, refs):
    width = own_ref.shape[2]
    sent, came = refs[0], refs[1:]
    tile = sent[2 * width:]
    for ref in came:
        tile = tile + ref[2 * width:]
    sums = []
    for b in range(2):
        total = own_ref[b] + step_ref[b]
        for ref in came:
            total = total + ref[b * width:(b + 1) * width]
        sums.append(total)
    return sums, jnp.sum(tile)


def step_kernel(own_ref, step_ref, square_ref, vector_ref, precond_ref, *refs):
    out_ref = refs[-1]
    sigma, product = landed(own_ref, step_ref, refs[:-1])
    theta = product / jnp.sum(square_ref[...])
    for b in range(2):
        v = vector_ref[b]
        out_ref[b] = v - precond_ref[b] * (sigma[b] - theta * v)


def last_kernel(cells, own_ref, step_ref, square_ref, vector_ref, precond_ref, *refs):
    residual_ref, out_ref, tile_ref = refs[-3:]
    sigma, product = landed(own_ref, step_ref, refs[:-3])
    square = jnp.sum(square_ref[...])
    theta = product / square
    scale = 1.0 / jnp.sqrt(square / cells + 1e-06)
    tile = jnp.zeros(tile_ref.shape, jnp.float32)
    for b in range(2):
        v = vector_ref[b]
        residual = (sigma[b] - theta * v) * scale
        residual_ref[b] = residual
        corrected = v * scale - precond_ref[b] * residual
        out_ref[b] = corrected
        tile = tile + tile_sum(corrected * corrected)
    tile_ref[...] = tile


def norm_kernel(cells, corrected_ref, tiles_ref, out_ref):
    scale = 1.0 / jnp.sqrt(jnp.sum(jnp.sum(tiles_ref[...], axis=0)) / cells + 1e-06)
    out_ref[...] = corrected_ref[...] * scale


def scattered(n, tables, pieces, last):
    width = pieces[0].shape[1]
    chips = n // 2
    rows = width if n <= 16 else width // 4
    over_rows = list(range(chips - 1, 3, -2))
    late = [g for g in range(chips) if g != 3 and g not in over_rows]
    shape = lambda *dims: jax.ShapeDtypeStruct(dims, jnp.float32)
    runs = [apply(n, over_rows, rows, start, tables, pieces) for start in range(0, width, rows)]
    counts = (len(late), len(late), len(over_rows), len(over_rows), 1, 1)
    near, far, row, row_far, column, column_far = (joined([x[i] for x in runs], k) for i, k in enumerate(counts))
    square = functools.reduce(jnp.add, [x[6] for x in runs])
    own, step, *sends = local(
        functools.partial(fold_kernel, n, late, over_rows), "fold",
        (shape(2, width, width),) * 2 + (shape(2 * width + 8, width),) * (chips // 2 - 1), tables[2:3],
        (near, far, swapped(far, CORE), swapped(row, ROW), swapped(row_far, ROW + CORE), swapped(column, COLUMN),
         swapped(column_far, COLUMN + CORE)))
    order = range(len(sends))
    came = [swapped(sends[i], 2 * ROW * (i + 1)) for i in ((*order[1:], 0) if last else order[::-1])]
    return square, (own, swapped(step, ROW)), [sends[0], *came]


def gathered(n, x, held=None):
    pieces = {0: x}
    for k in reversed(range(8, n, 4)):
        pieces[k] = swapped(x, k)
    pieces[ROW] = swapped(x, ROW)
    pieces[COLUMN] = swapped(x, COLUMN)
    for k in reversed(range(8, n, 4)):
        pieces[k + ROW] = swapped(pieces[k], ROW)
    pieces[COLUMN + ROW] = swapped(pieces[ROW], COLUMN)
    if held is not None:
        pieces[n - 4], held = lax.optimization_barrier((pieces[n - 4], held))
    for k in range(0, n, 2):
        pieces[k + CORE] = swapped(pieces[k], CORE)
    if held is not None:
        pieces[0] = held
    return [pieces[k] for k in range(n)]


def shards(wavefn, left_ops, right_ops, precond, fetch_map, store_map, pair_list, live_count):
    n = lax.axis_size("term")
    me = lax.axis_index("term").astype(jnp.int32).reshape(1)
    width = wavefn.shape[1]
    cells = wavefn.size * n
    *tables, held = prep(n, me, fetch_map, store_map, pair_list[0].T.reshape(-1), live_count, wavefn, left_ops, right_ops)
    block = jax.ShapeDtypeStruct(wavefn.shape, jnp.float32)
    tile = jax.ShapeDtypeStruct((8, width), jnp.float32)
    vector = wavefn
    for iteration in range(ITERS):
        pieces = gathered(n, vector, held if iteration == 0 else None)
        vector = pieces[0]
        square, sums, parts = scattered(n, tables, pieces, iteration == ITERS - 1)
        arrays = (*sums, square, vector, precond, *parts)
        if iteration < ITERS - 1:
            vector = local(step_kernel, "step", block, (), arrays)
    residual, corrected, partial = local(
        functools.partial(last_kernel, cells), "last", (block, block, tile), (), arrays)
    tiles = lax.all_to_all(jnp.broadcast_to(partial[None], (n, 8, width)), "term",
                           split_axis=0, concat_axis=0, tiled=True)
    return local(functools.partial(norm_kernel, cells), "norm", block, (), (corrected, tiles)), residual


def solution(mesh):
    field = P(("group", "term"), None, None)
    return jax.shard_map(
        shards,
        mesh=mesh,
        in_specs=(field, field, field, field, P(), P(), P("term", None, None), P("term")),
        out_specs=(field, field),
        check_vma=False,
    )
```

```python
import functools

import jax
import jax.numpy as jnp
from jax import lax
from jax.experimental import pallas as pl
from jax.experimental.pallas import tpu as pltpu
from jax.sharding import PartitionSpec as P

ITERS = 2
CORE, ROW, COLUMN = 1, 2, 4
SENDERS = 6
SMEM = pl.BlockSpec(memory_space=pltpu.SMEM)
VMEM = pl.BlockSpec(memory_space=pltpu.VMEM)


def params(mebibytes):
    return pltpu.CompilerParams(vmem_limit_bytes=mebibytes * 2**20)


def halves(x):
    high = x.astype(jnp.bfloat16)
    return high, (x - high.astype(jnp.float32)).astype(jnp.bfloat16)


def tile_sum(x):
    return jnp.sum(x.reshape(-1, 8, x.shape[-1]), axis=0)


class Part:
    def __init__(self, ref, start):
        self.ref, self.start = ref, start

    def __getitem__(self, i):
        return self.ref[self.start + i]

    def __setitem__(self, i, value):
        self.ref[self.start + i] = value


def lengths(n, terms, npairs):
    return n, n, SENDERS * n // 2, terms * n, terms * n, npairs, npairs, npairs, 1


def parts(ref, n, terms, npairs):
    sizes = lengths(n, terms, npairs)
    return [Part(ref, sum(sizes[:i])) for i in range(len(sizes))]


def prep_kernel(n, spare, me_ref, fetch_in, store_in, pairs_in, live_in, vector_in, left_in, right_in, l4_ref, rr_ref,
                table_ref, vector_ref,
                seen_ref, fetch_ref, store_ref, pairs_ref, live_ref, left_ref, right_ref, sems):
    copies = [pltpu.make_async_copy(source, target, sems.at[i]) for i, (source, target) in enumerate((
        (fetch_in, fetch_ref), (store_in, store_ref), (pairs_in, pairs_ref), (live_in, live_ref),
        (left_in, left_ref), (right_in, right_ref), (vector_in, vector_ref)))]
    for copy in copies:
        copy.start()
    me = me_ref[0]
    terms = left_ref.shape[0]
    width = left_ref.shape[1]
    zero = terms * n
    npairs = pairs_ref.shape[0] // 3
    pick_ref, mine_ref, place_ref, first_ref, second_ref, dst_ref, one_ref, two_ref, count_ref = parts(
        table_ref, n, terms, npairs)

    def clear(cell, carry):
        first_ref[cell] = zero
        second_ref[cell] = zero
        seen_ref[cell] = 0
        return carry

    lax.fori_loop(0, terms * n, clear, 0, unroll=8)
    for copy in copies[:4]:
        copy.wait()

    def relative(r, carry):
        device = lax.bitwise_xor(me, r)
        pick_ref[r] = fetch_ref[device, me]
        mine_ref[r] = store_ref[me, device]
        return carry

    lax.fori_loop(0, n, relative, 0)

    def chip(g, carry):
        for q in range(SENDERS):
            place_ref[q * (n // 2) + g] = store_ref[lax.bitwise_xor(me, q), lax.bitwise_xor(me, 2 * g)]
        return carry

    lax.fori_loop(0, n // 2, chip, 0)

    def pair(p, carry):
        extra, ops = carry
        a = lax.bitwise_xor(pairs_ref[p], me)
        j = pairs_ref[npairs + p]
        o = lax.bitwise_xor(pairs_ref[2 * npairs + p], me)
        cell = j * n + o
        source = a * terms + j
        seen = seen_ref[cell]
        seen_ref[cell] = seen + 1
        before = second_ref[cell]
        place = jnp.where(seen == 2, spare + extra, before)
        first_ref[cell] = jnp.where(seen == 0, source, first_ref[cell])
        second_ref[cell] = jnp.where(seen == 0, before, jnp.where(seen == 1, source, place))
        dst_ref[ops] = place
        one_ref[ops] = before
        two_ref[ops] = source
        return extra + (seen == 2).astype(jnp.int32), ops + (seen >= 2).astype(jnp.int32)

    _, ops = lax.fori_loop(0, live_ref[0], pair, (jnp.int32(0), jnp.int32(0)))
    count_ref[0] = ops
    for copy in copies[4:]:
        copy.wait()

    for j in range(terms):
        high, low = halves(left_ref[j])
        for k, part in enumerate((high, low, high, low)):
            l4_ref[j, :, k * width:(k + 1) * width] = part
        high, low = halves(right_ref[j])
        for k in range(2):
            row = (k * terms + j) * width
            rr_ref[row:row + width, :width] = high
            rr_ref[row:row + width, width:] = low


def at_home(x):
    return pltpu.with_memory_space_constraint(x, pltpu.HBM)


def prep(n, me, fetch, store, pairs, live, vector, left_ops, right_ops):
    terms, width = left_ops.shape[:2]
    npairs = pairs.shape[0] // 3
    return pl.pallas_call(
        functools.partial(prep_kernel, n, terms * n + 1),
        out_shape=(
            jax.ShapeDtypeStruct((terms, width, 4 * width), jnp.bfloat16),
            jax.ShapeDtypeStruct((2 * terms * width, 2 * width), jnp.bfloat16),
            jax.ShapeDtypeStruct((sum(lengths(n, terms, npairs)),), jnp.int32),
            jax.ShapeDtypeStruct(vector.shape, jnp.float32),
        ),
        in_specs=[SMEM] + [pl.BlockSpec(memory_space=pltpu.HBM)] * 7,
        out_specs=[VMEM] * 2 + [SMEM, VMEM],
        scratch_shapes=[
            pltpu.SMEM((terms * n,), jnp.int32),
            pltpu.SMEM(fetch.shape, jnp.int32),
            pltpu.SMEM(store.shape, jnp.int32),
            pltpu.SMEM(pairs.shape, jnp.int32),
            pltpu.SMEM((1,), jnp.int32),
            pltpu.VMEM(left_ops.shape, jnp.float32),
            pltpu.VMEM(left_ops.shape, jnp.float32),
            pltpu.SemaphoreType.DMA((7,)),
        ],
        compiler_params=params(16),
        name="prep",
    )(me, at_home(fetch), at_home(store), at_home(pairs), live, at_home(vector), at_home(left_ops), at_home(right_ops))


def apply_kernel(n, npairs, over_rows, rows, start, table_ref, l4_ref, rr_ref, *refs):
    pieces, (near_ref, far_ref, row_ref, row_far_ref, column_ref, column_far_ref, square_ref, block, total) = refs[:n], refs[n:]
    terms, width = l4_ref.shape[:2]
    pick_ref, mine_ref, _, first_ref, second_ref, dst_ref, one_ref, two_ref, count_ref = parts(table_ref, n, terms, npairs)
    square = jnp.zeros((8, width), jnp.float32)
    product = jnp.zeros((8, width), jnp.float32)
    block[terms * n] = jnp.zeros((rows, width), jnp.float32)
    left = l4_ref[:, start:start + rows, :].reshape(terms * rows, 4 * width)
    for c in range(n // 2):
        columns = []
        for r in (2 * c, 2 * c + 1):
            high, low = halves(pieces[r][pick_ref[r]])
            columns.append(jnp.concatenate([high, high, low, low], axis=0))
            held = pieces[r][:, start:start + rows, :]
            square = square + tile_sum(held * held)
        both = jnp.dot(left, jnp.concatenate(columns, axis=1), preferred_element_type=jnp.float32)
        for k in range(2):
            at = (2 * c + k) * terms
            block[at:at + terms] = both[:, k * width:(k + 1) * width].reshape(terms, rows, width)
    square_ref[...] = square

    def add(i, carry):
        block[dst_ref[i]] = block[one_ref[i]] + block[two_ref[i]]
        return carry

    lax.fori_loop(0, count_ref[0], add, 0)
    late = 0
    for low_end in range(0, n, 2):
        for r in range(low_end, low_end + 2):
            for j in range(terms):
                at = j * n + r
                high, low = halves(block[first_ref[at]] + block[second_ref[at]])
                total[r, :, j * width:(j + 1) * width] = high
                total[r, :, (terms + j) * width:(terms + j + 1) * width] = low
        both = jnp.dot(total[low_end:low_end + 2].reshape(2 * rows, 2 * terms * width), rr_ref[...],
                       preferred_element_type=jnp.float32)
        slots = both[:, :width] + both[:, width:]
        for r in range(low_end, low_end + 2):
            slot = slots[(r - low_end) * rows:(r - low_end + 1) * rows]
            product = product + tile_sum(pieces[r][mine_ref[r], start:start + rows, :] * slot)
            g, core = divmod(r, 2)
            if g == 3:
                (column_far_ref if core else column_ref)[...] = slot
            elif g in over_rows:
                at = over_rows.index(g) * rows
                (row_far_ref if core else row_ref)[at:at + rows, :] = slot
            else:
                (far_ref if core else near_ref)[late * rows:(late + 1) * rows, :] = slot
                late += core
    for ref in (far_ref, row_ref, row_far_ref):
        ref[ref.shape[0] - 8:, :] = product


def apply(n, over_rows, rows, start, tables, pieces):
    terms, width = tables[0].shape[:2]
    npairs = (tables[2].shape[0] - sum(lengths(n, terms, 0))) // 3
    spare = npairs // 3
    late = n // 2 - 1 - len(over_rows)
    shape = lambda *dims: jax.ShapeDtypeStruct(dims, jnp.float32)
    return pl.pallas_call(
        functools.partial(apply_kernel, n, npairs, over_rows, rows, start),
        out_shape=(shape(late * rows, width), shape(late * rows + 8, width)) + (shape(len(over_rows) * rows + 8, width),) * 2
        + (shape(rows, width),) * 2 + (shape(8, width),),
        in_specs=[SMEM] + [VMEM] * (2 + n),
        out_specs=[VMEM] * 7,
        scratch_shapes=[
            pltpu.VMEM((terms * n + 1 + spare, rows, width), jnp.float32),
            pltpu.VMEM((n, rows, 2 * terms * width), jnp.bfloat16),
        ],
        compiler_params=params(32 if n <= 16 else 56),
        name="apply",
    )(tables[2], *tables[:2], *pieces)


def joined(parts, count):
    if len(parts) == 1:
        return parts[0]
    height, width = parts[0].shape
    end = height // (8 * count) * 8 * count
    whole = jnp.concatenate([x[:end].reshape(count, -1, width) for x in parts], axis=1).reshape(-1, width)
    return whole if end == height else jnp.concatenate([whole, sum(x[end:] for x in parts)])


def swapped(x, k):
    n = lax.axis_size("term")
    return lax.ppermute(x, "term", [(i, i ^ k) for i in range(n)])


def local(kernel, name, out_shape, scalars, arrays):
    many = isinstance(out_shape, tuple)
    return pl.pallas_call(
        kernel,
        out_shape=out_shape,
        in_specs=[SMEM] * len(scalars) + [VMEM] * len(arrays),
        out_specs=[VMEM] * len(out_shape) if many else VMEM,
        compiler_params=params(16),
        name=name,
    )(*scalars, *arrays)


def fold_kernel(n, late, over_rows, table_ref, near_ref, far_in, far_ref, row_ref, row_far_ref, column_ref, column_far_ref,
                own_ref, step_ref, *send_refs):
    width = near_ref.shape[1]
    chips = n // 2
    place_ref = Part(table_ref, 2 * n)
    end = len(late) * width
    over = len(over_rows) * width
    tile = far_in[end:] + far_ref[end:] + row_ref[over:] + row_far_ref[over:]
    for i, g in enumerate(late):
        come = [(0, near_ref, i), (1, far_ref, i)]
        if g == 1:
            come += [(4, column_ref, 0), (5, column_far_ref, 0)]
        if g + 1 in over_rows:
            come += [(2, row_ref, over_rows.index(g + 1)), (3, row_far_ref, over_rows.index(g + 1))]
        for b in range(2):
            block = sum(ref[at * width:(at + 1) * width] * (place_ref[q * chips + g] == b).astype(jnp.float32)
                        for q, ref, at in come)
            if g == 0:
                own_ref[b] = block
            elif g == 1:
                step_ref[b] = block
            else:
                send_refs[g // 2 - 1][b * width:(b + 1) * width] = block
    for send_ref in send_refs:
        send_ref[2 * width:] = tile


def landed(own_ref, step_ref, refs):
    width = own_ref.shape[2]
    sent, came = refs[0], refs[1:]
    tile = sent[2 * width:]
    for ref in came:
        tile = tile + ref[2 * width:]
    sums = []
    for b in range(2):
        total = own_ref[b] + step_ref[b]
        for ref in came:
            total = total + ref[b * width:(b + 1) * width]
        sums.append(total)
    return sums, jnp.sum(tile)


def step_kernel(own_ref, step_ref, square_ref, vector_ref, precond_ref, *refs):
    out_ref = refs[-1]
    sigma, product = landed(own_ref, step_ref, refs[:-1])
    theta = product / jnp.sum(square_ref[...])
    for b in range(2):
        v = vector_ref[b]
        out_ref[b] = v - precond_ref[b] * (sigma[b] - theta * v)


def last_kernel(cells, own_ref, step_ref, square_ref, vector_ref, precond_ref, *refs):
    residual_ref, out_ref, tile_ref = refs[-3:]
    sigma, product = landed(own_ref, step_ref, refs[:-3])
    square = jnp.sum(square_ref[...])
    theta = product / square
    scale = 1.0 / jnp.sqrt(square / cells + 1e-06)
    tile = jnp.zeros(tile_ref.shape, jnp.float32)
    for b in range(2):
        v = vector_ref[b]
        residual = (sigma[b] - theta * v) * scale
        residual_ref[b] = residual
        corrected = v * scale - precond_ref[b] * residual
        out_ref[b] = corrected
        tile = tile + tile_sum(corrected * corrected)
    tile_ref[...] = tile


def norm_kernel(cells, corrected_ref, tiles_ref, out_ref):
    scale = 1.0 / jnp.sqrt(jnp.sum(jnp.sum(tiles_ref[...], axis=0)) / cells + 1e-06)
    out_ref[...] = corrected_ref[...] * scale


def scattered(n, tables, pieces, last):
    width = pieces[0].shape[1]
    chips = n // 2
    rows = width if n <= 16 else width // 4
    over_rows = list(range(chips - 1, 3, -2))
    late = [g for g in range(chips) if g != 3 and g not in over_rows]
    shape = lambda *dims: jax.ShapeDtypeStruct(dims, jnp.float32)
    runs = [apply(n, over_rows, rows, start, tables, pieces) for start in range(0, width, rows)]
    counts = (len(late), len(late), len(over_rows), len(over_rows), 1, 1)
    near, far, row, row_far, column, column_far = (joined([x[i] for x in runs], k) for i, k in enumerate(counts))
    square = functools.reduce(jnp.add, [x[6] for x in runs])
    own, step, *sends = local(
        functools.partial(fold_kernel, n, late, over_rows), "fold",
        (shape(2, width, width),) * 2 + (shape(2 * width + 8, width),) * (chips // 2 - 1), tables[2:3],
        (near, far, swapped(far, CORE), swapped(row, ROW), swapped(row_far, ROW + CORE), swapped(column, COLUMN),
         swapped(column_far, COLUMN + CORE)))
    order = range(len(sends))
    came = [swapped(sends[i], 2 * ROW * (i + 1)) for i in ((*order[1:], 0) if last else order[::-1])]
    return square, (own, swapped(step, ROW)), [sends[0], *came]


def gathered(n, x, held=None):
    pieces = {0: x}
    for k in reversed(range(8, n, 4)):
        pieces[k] = swapped(x, k)
    pieces[ROW] = swapped(x, ROW)
    pieces[COLUMN] = swapped(x, COLUMN)
    if held is not None:
        pieces[n - 4], pieces[0] = lax.optimization_barrier((pieces[n - 4], held))
    for k in reversed(range(8, n, 4)):
        pieces[k + ROW] = swapped(pieces[k], ROW)
    pieces[COLUMN + ROW] = swapped(pieces[ROW], COLUMN)
    for k in range(0, n, 2):
        pieces[k + CORE] = swapped(pieces[k], CORE)
    return [pieces[k] for k in range(n)]


def shards(wavefn, left_ops, right_ops, precond, fetch_map, store_map, pair_list, live_count):
    n = lax.axis_size("term")
    me = lax.axis_index("term").astype(jnp.int32).reshape(1)
    width = wavefn.shape[1]
    cells = wavefn.size * n
    *tables, held = prep(n, me, fetch_map, store_map, pair_list[0].T.reshape(-1), live_count, wavefn, left_ops, right_ops)
    block = jax.ShapeDtypeStruct(wavefn.shape, jnp.float32)
    tile = jax.ShapeDtypeStruct((8, width), jnp.float32)
    vector = wavefn
    for iteration in range(ITERS):
        pieces = gathered(n, vector, held if iteration == 0 else None)
        vector = pieces[0]
        square, sums, parts = scattered(n, tables, pieces, iteration == ITERS - 1)
        arrays = (*sums, square, vector, precond, *parts)
        if iteration < ITERS - 1:
            vector = local(step_kernel, "step", block, (), arrays)
    residual, corrected, partial = local(
        functools.partial(last_kernel, cells), "last", (block, block, tile), (), arrays)
    tiles = lax.all_to_all(jnp.broadcast_to(partial[None], (n, 8, width)), "term",
                           split_axis=0, concat_axis=0, tiled=True)
    return local(functools.partial(norm_kernel, cells), "norm", block, (), (corrected, tiles)), residual


def solution(mesh):
    field = P(("group", "term"), None, None)
    return jax.shard_map(
        shards,
        mesh=mesh,
        in_specs=(field, field, field, field, P(), P(), P("term", None, None), P("term")),
        out_specs=(field, field),
        check_vma=False,
    )
```
